32 devices in a mesh: dp: 2 (over x), ctx: 4 (over z), exp: 4 (over y, core).
Axes of the slice: x: 2, y: 2, z: 4, core: 2. Of those that a mesh axis runs over, the one named last changes fastest.
Arguments:
- tokens: bfloat16 [8, 1024, 1536], P(('dp', 'exp'), 'ctx'), may hold values from -6 to 6
- gain_attn: float32 [1536], replicated, may hold values from 0.5 to 1.5
- w_query: bfloat16 [1536, 1536], P(('dp', 'ctx', 'exp')), may hold values from -1.25 to 1.25
- w_key: bfloat16 [1536, 512], P(('dp', 'ctx', 'exp')), may hold values from -0.15625 to 0.15625
- w_value: bfloat16 [1536, 512], P(('dp', 'ctx', 'exp')), may hold values from -0.15625 to 0.15625
- w_out: bfloat16 [1536, 1536], P(('dp', 'ctx', 'exp')), may hold values from -6 to 6
- gain_moe: float32 [1536], replicated, may hold values from 0.5 to 1.5
- w_in: bfloat16 [16, 1536, 1024], P('exp', ('dp', 'ctx')), may hold values from -0.15625 to 0.15625
- w_down: bfloat16 [16, 512, 1536], P('exp', ('dp', 'ctx')), may hold values from -1.5 to 1.5
- routes: int32 [8, 1024, 8], P(('dp', 'exp'), 'ctx'), may hold values from 0 to 15, all different within a row; in each aligned block of 256 rows (0 to 255, 256 to 511, ..., all dimensions but the last counted through in order) at most 192 rows name the same one
- gates: bfloat16 [8, 1024, 8], P(('dp', 'exp'), 'ctx'), may hold values from 0.19921875 to 0.59765625
- lengths: int32 [8, 3], P(('dp', 'exp')), may hold values from 1 to 896, 1024 in all within a row
- cotangent: float32 [8, 1024, 1536], P(('dp', 'exp'), 'ctx'), may hold values from -6 to 6
Outputs:
- mixed: bfloat16 [8, 1024, 1536], P(('dp', 'exp'), 'ctx')
- grad_tokens: float32 [8, 1024, 1536], P(('dp', 'exp'), 'ctx')
- grad_gain_attn: float32 [1536], P(('dp', 'ctx', 'exp'))
- grad_query: float32 [1536, 1536], P(('dp', 'ctx', 'exp'))
- grad_key: float32 [1536, 512], P(('dp', 'ctx', 'exp'))
- grad_value: float32 [1536, 512], P(('dp', 'ctx', 'exp'))
- grad_out: float32 [1536, 1536], P(('dp', 'ctx', 'exp'))
- grad_gain_moe: float32 [1536], P(('dp', 'ctx', 'exp'))
- grad_in: float32 [16, 1536, 1024], P('exp', ('dp', 'ctx'))
- grad_down: float32 [16, 512, 1536], P('exp', ('dp', 'ctx'))
The draws below stay inside these ranges and needn't reach their ends.
Inputs may be any that keep to these rules, and one draw needn't show every extreme that they name: `routes`: each row names 8 different experts. In each aligned block of 256 rows (the rows of one device) no expert is named by more than 192 rows. Each group's 3 lengths sum to 1024, and its longest is exactly 896.
All inputs are finite; a program needn't handle non-finite values.
Results may differ from the reference program's by a relative error of at most 0.017.
Values may be sent and summed in bfloat16 or wider, within the bound.
No kernel may reach another device: no remote copies, remote signals or barrier semaphores. Data moves between devices by JAX's collectives and lax.ppermute only.
A program may use at most 256 MiB of HBM per device.

```python
import math
from functools import partial
import jax
import jax.numpy as jnp
import numpy as np
from jax import lax

D = 1536
HEADS = 24
KV_HEADS = 8
HEAD_DIM = 64
FF = 512
TOP = 8
NSEQ = 3
TOK_DEV = 256
EXPERTS = 16
SEQ_TOK = 1024
GROUPS = 8
CAP = 192


def levels(own_key, shape, shards, smallest, top_value):
    def one(dim, parts):
        heights = jax.random.uniform(jax.random.fold_in(jax.random.fold_in(own_key, 6), dim), (parts,), jnp.float32, smallest / len(shards), top_value / len(shards))
        return jnp.repeat(jnp.exp(heights), shape[dim] // parts).reshape((-1,) + (1,) * (len(shape) - dim - 1))

    level = one(*shards[0])
    for cut in shards[1:]:
        level = level * one(*cut)
    return level


def split_up(count, total, bound, slope):
    portions = [(1 << 20) // math.isqrt(rank ** slope) + 1 for rank in range(2, count + 1)]
    rest, counts = total - bound - (count - 1), [1] * (count - 1)
    while rest > 0:
        candidates = [i for i in range(count - 1) if counts[i] < bound]
        mass, remaining = sum([portions[i] for i in candidates]), rest
        for i in candidates:
            addition = min(bound - counts[i], max(1, remaining * portions[i] // mass), rest)
            counts[i] = counts[i] + addition
            rest = rest - addition
    return np.array([bound] + counts)


def ragged_sizes(rng, count, total, limit, slope):
    if count == 2:
        one = jax.random.randint(rng, (), max(1, total - limit), min(limit, total - 1) + 1)
        return jnp.stack([one, total - one])
    tallies = jnp.asarray(split_up(count, total, limit, slope), jnp.int32)
    couples = (count - 1) // 2
    source_of, receiver = tallies[1:1 + 2 * couples:2], tallies[2:2 + 2 * couples:2]
    margin = jnp.minimum(source_of - 1, limit - receiver)
    passed = jax.random.randint(jax.random.fold_in(rng, 1), (couples,), 0, 1 << 20) % (margin + 1)
    tallies = tallies.at[1:1 + 2 * couples:2].set(source_of - passed).at[2:2 + 2 * couples:2].set(receiver + passed)
    return tallies[jax.random.permutation(jax.random.fold_in(rng, 2), count)]


def deal_out(own_key, own, number, rows, count, top, bound, slope):
    ranking = jax.random.permutation(own_key, count)
    crowded, common = portions_of(count, rows * top, bound, slope, True), portions_of(count, rows * top, bound, slope, False)
    places = jnp.arange(count)

    def named(sizes, offset_by):
        used = int((sizes > 0).sum())
        fixed = max(1, used // 4)
        moved = fixed + (places - fixed + offset_by * (used - fixed)) % max(1, count - fixed)
        return jnp.zeros((count,), jnp.int32).at[ranking[jnp.where(places < fixed, places, moved)]].set(jnp.asarray(sizes, jnp.int32))

    sizes = jnp.where(number % 4 == 0, named(crowded, number // 4), named(common, number - number // 4 - 1))
    mixed = jax.random.permutation(jax.random.fold_in(own, 3), count)
    donor, taker = mixed[0:count // 2 * 2:2], mixed[1:count // 2 * 2:2]
    room = jnp.minimum(sizes[donor] - 1, bound - sizes[taker]) // 2
    room = jnp.where((donor == ranking[0]) | (taker == ranking[0]) | (sizes[taker] == 0), 0, jnp.maximum(room, 0))
    moved = jax.random.randint(jax.random.fold_in(own, 4), (count // 2,), 0, 1 << 20) % (room + 1)
    sizes = sizes.at[donor].add(-moved).at[taker].add(moved)
    members = jnp.searchsorted(jnp.cumsum(sizes), jnp.arange(rows * top), side="right").astype(jnp.int32)
    table = members.reshape(top, rows).T
    table = table[jax.random.permutation(jax.random.fold_in(own, 1), rows)]
    offset_by = jax.random.randint(jax.random.fold_in(own, 2), (rows, 1), 0, top)
    return jnp.take_along_axis(table, (jnp.arange(top)[None, :] + offset_by) % top, axis=1)


def portions_of(amount, total, bound, skew, full):
    portions = [(1 << 20) // math.isqrt(grade ** skew) + 1 for grade in range(1, amount + 1)]
    largest = bound if full else min(bound, max(-(-total // amount), total * portions[0] // sum(portions)))
    least = 1 if total - largest >= amount - 1 else 0
    counts, rest = [largest] + [least] * (amount - 1), total - largest - least * (amount - 1)
    while rest > 0:
        candidates = [i for i in range(1, amount) if counts[i] < largest] or [i for i in range(1, amount) if counts[i] < bound]
        pool, remaining = sum([portions[i] for i in candidates]), rest
        for i in candidates:
            addition = min(bound - counts[i], max(1, remaining * portions[i] // pool), rest)
            counts[i] = counts[i] + addition
            rest = rest - addition
    return np.array(counts)


def normal_values(own_key, extent, scale, reach, shards=(), kind=jnp.bfloat16):
    level = levels(own_key, extent, shards, -0.22, 0.18) if shards else 1.0
    array = jax.random.normal(own_key, extent, jnp.float32) * scale * level
    return jnp.minimum(jnp.maximum(array, -reach), reach).astype(kind)


def setup_inputs(seed: int = 0) -> dict:
    seeds = jax.random.split(jax.random.key(seed), 14)
    tokens = normal_values(seeds[0], (GROUPS, SEQ_TOK, D), 1.0, 6.0, ((0, 8), (1, 4)))
    gain_attn = jnp.clip(1.0 + 0.1 * jax.random.normal(seeds[1], (D,), jnp.float32), 0.5, 1.5)
    w_query = normal_values(seeds[2], (D, D), (D // 64) ** -0.5, 1.25, ((0, 32),))
    w_key = normal_values(seeds[3], (D, KV_HEADS * HEAD_DIM), D ** -0.5, 0.15625, ((0, 32),))
    w_value = normal_values(seeds[4], (D, KV_HEADS * HEAD_DIM), D ** -0.5, 0.15625, ((0, 32),))
    w_out = normal_values(seeds[5], (D, D), 1 ** -0.5, 6.0, ((0, 32),))
    gain_moe = jnp.clip(1.0 + 0.1 * jax.random.normal(seeds[6], (D,), jnp.float32), 0.5, 1.5)
    w_in = normal_values(seeds[7], (EXPERTS, D, 2 * FF), D ** -0.5, 0.15625, ((0, 4), (1, 8)))
    w_down = normal_values(seeds[8], (EXPERTS, FF, D), (FF // 32) ** -0.5, 1.5, ((0, 4), (1, 8)))
    routes_keys = jax.random.split(jax.random.fold_in(seeds[9], 1), GROUPS * SEQ_TOK // TOK_DEV)
    routes_turns = jax.random.permutation(jax.random.fold_in(seeds[9], 3), GROUPS * SEQ_TOK // TOK_DEV)
    routes = jax.vmap(lambda own, number: deal_out(jax.random.fold_in(seeds[9], 2), own, number, TOK_DEV, EXPERTS, TOP, CAP, 1))(routes_keys, routes_turns).reshape((GROUPS, SEQ_TOK, TOP))
    gates = jnp.clip(0.19921875 + 0.3984375 * jax.random.uniform(seeds[10], (GROUPS, SEQ_TOK, TOP), jnp.float32) ** levels(seeds[10], (GROUPS, SEQ_TOK, TOP), ((0, 8), (1, 4)), -0.2, 0.2), 0.19921875, 0.59765625).astype(jnp.bfloat16)
    lengths = jax.vmap(lambda own: ragged_sizes(own, NSEQ, SEQ_TOK, SEQ_TOK - TOK_DEV // 2, 1))(jax.random.split(seeds[11], GROUPS)).reshape((GROUPS, NSEQ)).astype(jnp.int32)
    cotangent = normal_values(seeds[12], (GROUPS, SEQ_TOK, D), 1.0, 6.0, ((0, 8), (1, 4)), jnp.float32)
    return {"tokens": tokens, "gain_attn": gain_attn, "w_query": w_query, "w_key": w_key, "w_value": w_value, "w_out": w_out, "gain_moe": gain_moe, "w_in": w_in, "w_down": w_down, "routes": routes, "gates": gates, "lengths": lengths, "cotangent": cotangent}


@jax.custom_vjp
def low(v):
    return lax.optimization_barrier(v.astype(jnp.bfloat16)).astype(jnp.float32)

@jax.custom_vjp
def low_back(v):
    return v

def low_keep(v):
    return (low(v), None)

def low_pass(kept, grad):
    return (grad,)

def back_keep(v):
    return (v, None)

def back_low(kept, grad):
    return (low(grad),)
low.defvjp(low_keep, low_pass)
low_back.defvjp(back_keep, back_low)
eps_norm = 1e-06
score_scale = 0.015625
residual_scale = 0.22
rope_base = 10000.0
precise = lax.Precision.HIGHEST

def rms_norm(vectors, gain_vec):
    return vectors * lax.rsqrt(lax.optimization_barrier(jnp.mean(vectors * vectors, axis=-1, keepdims=True)) + eps_norm) * gain_vec

def rotate(vectors, position, direction):
    half_dim = vectors.shape[-1] // 2
    frequency = rope_base ** (-2.0 * jnp.arange(half_dim, dtype=jnp.float32) / vectors.shape[-1])
    angles = position.astype(jnp.float32)[:, None] * frequency[None, :]
    cosine = jnp.cos(angles)[:, None, :]
    sines = direction * jnp.sin(angles)[:, None, :]
    front_half = vectors[..., :half_dim]
    second = vectors[..., half_dim:]
    return jnp.concatenate([front_half * cosine - second * sines, second * cosine + front_half * sines], axis=-1)

def documents(lengths, length_all):
    doc_ends = jnp.cumsum(lengths).astype(jnp.int32)
    doc_starts = (doc_ends - lengths).astype(jnp.int32)
    places = jnp.arange(length_all, dtype=jnp.int32)
    doc_ids = lax.optimization_barrier(jnp.sum((places[:, None] >= doc_ends[None, :]).astype(jnp.int32), axis=1)).astype(jnp.int32)
    chosen = doc_ids[:, None] == jnp.arange(lengths.shape[0], dtype=jnp.int32)[None, :]
    offsets = lax.optimization_barrier(jnp.sum(jnp.where(chosen, doc_starts[None, :], 0), axis=1)).astype(jnp.int32)
    return (doc_ids, (places - offsets).astype(jnp.int32))

def group_attention(normed, query_w, key_w, value_w, doc_ids, position):
    length_all = normed.shape[0]
    group_size = HEADS // KV_HEADS
    queries = low(rotate(low_back(jnp.dot(normed, query_w, precision=precise)).reshape(length_all, HEADS, HEAD_DIM), position, 1.0))
    key_rows = low(rotate(low_back(jnp.dot(normed, key_w, precision=precise)).reshape(length_all, KV_HEADS, HEAD_DIM), position, 1.0))
    value_rows = low(low_back(jnp.dot(normed, value_w, precision=precise))).reshape(length_all, KV_HEADS, HEAD_DIM)
    places = jnp.arange(length_all, dtype=jnp.int32)
    allowed = (doc_ids[:, None] == doc_ids[None, :]) & (places[None, :] <= places[:, None])
    query_heads = jnp.transpose(queries.reshape(length_all, KV_HEADS, group_size, HEAD_DIM), (1, 0, 2, 3))
    key_heads = jnp.transpose(key_rows, (1, 0, 2))
    value_heads = jnp.transpose(value_rows, (1, 0, 2))

    def one_head(operands):
        query_head, key_head, value_head = operands
        scores = low_back(jnp.einsum('sgd,td->gst', query_head, key_head, precision=precise)) * score_scale
        scores = jnp.where(allowed[None], scores, -1e+30)
        chances = jax.nn.softmax(scores, axis=-1)
        return jnp.einsum('gst,td->sgd', low(chances), value_head, precision=precise)
    mixture = lax.map(jax.checkpoint(one_head), (query_heads, key_heads, value_heads))
    return jnp.transpose(mixture, (1, 0, 2, 3)).reshape(length_all, HEADS * HEAD_DIM)

def reference(tokens, gain_attn, w_query, w_key, w_value, w_out, gain_moe, w_in, w_down, routes, gates, lengths, cotangent):
    groups = tokens.shape[0]
    length_all = tokens.shape[1]
    model_width = tokens.shape[2]
    doc_ids, positions = jax.vmap(partial(documents, length_all=length_all))(lengths)
    flat_routes = routes.reshape(groups * length_all, TOP)
    chosen = (flat_routes[:, :, None] == jnp.arange(EXPERTS, dtype=jnp.int32)[None, None, :]).astype(jnp.float32)
    dense_gates = lax.optimization_barrier(jnp.sum(chosen * gates.reshape(groups * length_all, TOP, 1).astype(jnp.float32), axis=1))

    def forward(inputs, gain_a, query_w, key_w, value_w, out_w, gain_m, in_w, down_w):
        normed = low(rms_norm(inputs, gain_a))

        def per_group(operands):
            return group_attention(operands[0], query_w, key_w, value_w, operands[1], operands[2])
        mixture = lax.map(jax.checkpoint(per_group), (normed, doc_ids, positions))
        mixed_rows = low_back(low(mixture)).reshape(groups * length_all, model_width)
        attention = low_back(jnp.dot(mixed_rows, out_w, precision=precise))
        middle = inputs.reshape(groups * length_all, model_width) + residual_scale * attention
        hidden = low(rms_norm(middle, gain_m))

        def per_expert(running, operands):
            expert_in, expert_down, weight = operands
            gate_up = low_back(jnp.dot(hidden, expert_in, precision=precise))
            active = low_back(low(jax.nn.silu(gate_up[:, :FF]) * gate_up[:, FF:]))
            result = low_back(low(jnp.dot(active, expert_down, precision=precise)))
            return (running + weight[:, None] * result, None)
        expert_sum, unused = lax.scan(jax.checkpoint(per_expert), jnp.zeros_like(middle), (in_w, down_w, dense_gates.T))
        return (middle + residual_scale * expert_sum).reshape(groups, length_all, model_width)
    final_sum, pullback = jax.vjp(forward, tokens.astype(jnp.float32), gain_attn, w_query.astype(jnp.float32), w_key.astype(jnp.float32), w_value.astype(jnp.float32), w_out.astype(jnp.float32), gain_moe, w_in.astype(jnp.float32), w_down.astype(jnp.float32))
    gradients = pullback(cotangent)
    return (final_sum.astype(jnp.bfloat16), gradients[0], gradients[1], gradients[2], gradients[3], gradients[4], gradients[5], gradients[6], gradients[7], gradients[8])
```

```python
import functools

import jax
import jax.numpy as jnp
from jax import lax
from jax.experimental import pallas as pl
from jax.experimental.pallas import tpu as pltpu
from jax.sharding import PartitionSpec as P

HEADS = 24
KV_HEADS = 8
HEAD_DIM = 64
FF = 512
TOP = 8

eps_norm = 1e-06
score_scale = 0.015625
residual_scale = 0.22
rope_base = 10000.0

BF = jnp.bfloat16
F32 = jnp.float32
SCALE = 3
VMEM_LIMIT = 60 * 1024 * 1024
ANY = pl.BlockSpec(memory_space=pl.ANY)
VM = pl.BlockSpec(memory_space=pltpu.VMEM)
SM = pl.BlockSpec(memory_space=pltpu.SMEM)
NN = (((1,), (0,)), ((), ()))
NT = (((1,), (1,)), ((), ()))
TN = (((0,), (0,)), ((), ()))


def mm(a, b, dims=NN):
    return lax.dot_general(a, b, dims, preferred_element_type=F32)


def params(**kw):
    return pltpu.CompilerParams(vmem_limit_bytes=VMEM_LIMIT, **kw)


def cost(flops, nbytes, trans=0):
    return pl.CostEstimate(
        flops=int(flops / SCALE), bytes_accessed=int(nbytes / SCALE), transcendentals=0
    )


def shift(x, axis, by):
    n = lax.axis_size(axis)
    return lax.ppermute(x, axis, [(i, (i + by) % n) for i in range(n)])


def flip(x, axis, mask):
    n = lax.axis_size(axis)
    return lax.ppermute(x, axis, [(i, i ^ mask) for i in range(n)])


class Stages:
    def __init__(self, token):
        self.token = token

    def hold(self, x):
        leaves, tree = jax.tree.flatten(x)
        leaves = [lax.optimization_barrier((leaf, self.token))[0] for leaf in leaves]
        return jax.tree.unflatten(tree, leaves)

    def end(self, *outs):
        self.token = lax.optimization_barrier((self.token, *jax.tree.leaves(outs)))[0]


def ring(x, axis):
    out = [x]
    for _ in range(lax.axis_size(axis) - 1):
        out.append(shift(out[-1], axis, 1))
    return out


def hop(x, pairs):
    return lax.ppermute(x, "ctx", pairs)


UP, DOWN = [(0, 1), (1, 2), (2, 3)], [(1, 0), (2, 1), (3, 2)]
ACROSS = [(0, 2), (1, 3), (2, 0), (3, 1)]
INNER, OUTER = [(0, 1), (3, 2)], [(1, 0), (2, 3)]


def line_places(z):
    return [z, jnp.bitwise_xor(z, 2), jnp.where(z == 0, 3, z - 1), jnp.where(z == 3, 0, z + 1)]


def line_gather(across, below, above, end, x):
    z = lax.axis_index("ctx")
    return [x, across, jnp.where(z == 0, end, below), jnp.where(z == 3, end, above)]


def pick(x, index, dim=0):
    return lax.dynamic_index_in_dim(x, index, dim, False)


def dp_reduce(parts):
    n = lax.axis_size("dp")
    total = parts[n - 1]
    for k in range(1, n):
        total = (shift(total, "dp", 1).astype(F32) + parts[n - 1 - k].astype(F32)).astype(BF)
    return total


def assemble(found, places):
    found = [t.reshape(-1, *t.shape[-2:]) for t in found]
    each, rows, width = found[0].shape
    count = each * len(found)
    total = count * rows
    if rows % 16:
        blocks = jnp.concatenate(found)
        return jnp.zeros_like(blocks).at[places].set(blocks).reshape(total, width)

    def body(places_ref, *refs):
        refs, out_ref, sems = refs[:-2], refs[-2], refs[-1]
        copies = []
        for i in range(count):
            at = pl.multiple_of(places_ref[i] * rows, rows)
            copies.append(
                pltpu.make_async_copy(refs[i // each].at[i % each], out_ref.at[pl.ds(at, rows), :], sems.at[i])
            )
        for copy in copies:
            copy.start()
        for copy in copies:
            copy.wait()

    return pl.pallas_call(
        body,
        out_shape=jax.ShapeDtypeStruct((total, width), found[0].dtype),
        in_specs=[SM] + [ANY] * len(found),
        out_specs=VM,
        scratch_shapes=[pltpu.SemaphoreType.DMA((count,))],
        compiler_params=params(),
        cost_estimate=cost(0, 4 * total * width),
        name="assemble",
    )(places, *found)


def rms(v):
    return lax.rsqrt(jnp.mean(v * v, axis=-1, keepdims=True) + eps_norm)


def turn(block, cos, sin):
    lane = lax.broadcasted_iota(jnp.int32, block.shape, 1)
    partner = jnp.where(
        (lane & 63) < 32, pltpu.roll(block, 96, 1), pltpu.roll(block, 32, 1)
    )
    return block * cos + partner * sin


def project(tok, gain, w, cos, sin, block_at):
    rows, d = tok.shape
    n = w.shape[1]
    blocks = (n - 128) // 128

    def body(at_ref, tok_ref, gain_ref, w_ref, cos_ref, sin_ref, out_ref):
        t = tok_ref[...].astype(F32)
        normed = (t * rms(t) * gain_ref[...]).astype(BF)
        u = mm(normed, w_ref[...])
        for b in range(blocks):
            out_ref[:, b * 128 : (b + 1) * 128] = turn(
                u[:, b * 128 : (b + 1) * 128], cos_ref[...], sin_ref[...]
            ).astype(BF)
        out_ref[:, blocks * 128 :] = u[:, blocks * 128 :].astype(BF)

    return pl.pallas_call(
        body,
        grid_spec=pltpu.PrefetchScalarGridSpec(
            num_scalar_prefetch=1,
            grid=(1,),
            in_specs=[
                pl.BlockSpec((rows, d), lambda i, at: (0, 0)),
                pl.BlockSpec((1, d), lambda i, at: (0, 0)),
                pl.BlockSpec((d, n), lambda i, at: (0, 0)),
                pl.BlockSpec((rows, 128), lambda i, at: (at[0], 0)),
                pl.BlockSpec((rows, 128), lambda i, at: (at[0], 0)),
            ],
            out_specs=pl.BlockSpec((rows, n), lambda i, at: (0, 0)),
        ),
        out_shape=jax.ShapeDtypeStruct((rows, n), BF),
        compiler_params=params(),
        cost_estimate=cost(2 * rows * d * n, 2 * d * n + 4 * rows * d),
        name="project",
    )(block_at, tok, gain, w, cos, sin)


def swapped(e):
    return (e & 1) * 2 + (e >> 1)


def lower_half(shape):
    return lax.broadcasted_iota(jnp.int32, shape, 1) < 64


def stage_heads(block, dst, rows_at, heads, factor):
    rows = block.shape[0]
    low = lower_half((rows, 128))
    for h in range(heads):
        part = block[:, (h // 2) * 128 : (h // 2 + 1) * 128].astype(F32) * factor
        keep = low if h % 2 == 0 else jnp.logical_not(low)
        dst[h, rows_at, :] = jnp.where(keep, part, 0.0).astype(BF)


def doubled(block):
    block = block.astype(F32)
    low = lower_half(block.shape)
    other = pltpu.roll(block, 64, 1)
    return jnp.where(low, block, other), jnp.where(low, other, block)


def allowed_mask(s_ref, keys, rows, first):
    q = lax.broadcasted_iota(jnp.int32, (1, rows), 1) + first
    begin = jnp.zeros_like(q)
    for i in range(5, s_ref.shape[0] - 1):
        begin = jnp.where(q >= s_ref[i], jnp.maximum(begin, s_ref[i]), begin)
    k = lax.broadcasted_iota(jnp.int32, (keys, rows), 0)
    return (k >= begin) & (k <= q)


def attend(scalars, pieces, heads, kvs):
    blocks = len(pieces)
    rows, width = pieces[0].shape
    span = blocks * rows
    qw = heads * HEAD_DIM
    share = heads // kvs

    def body(s_ref, *refs):
        ins, (out_ref, lse_ref, qs, kd, vd, vt, ob) = refs[:blocks], refs[blocks:]
        me = s_ref[4]
        for k in range(blocks):
            at = pl.ds(pl.multiple_of(s_ref[k] * rows, rows), rows)
            block = ins[k][...]
            stage_heads(block, qs, at, heads, score_scale)
            for i, x in enumerate(doubled(block[:, qw : qw + 128])):
                kd[i, at, :] = x.astype(BF)
            for i, x in enumerate(doubled(block[:, qw + 128 : qw + 256])):
                vd[i, at, :] = x
        for i in range(kvs):
            vt[i] = vd[i].T.astype(BF)

        def one(h, _):
            kv = h // share
            for p in range(blocks):
                keys = (p + 1) * rows
                q = qs[h, p * rows : (p + 1) * rows, :]
                s = mm(kd[kv, :keys, :], q, NT)
                s = jnp.where(allowed_mask(s_ref, keys, rows, p * rows), s, -1e30)
                peak = jnp.max(s, axis=0, keepdims=True)
                e = jnp.exp(s - peak)
                total = jnp.sum(e, axis=0, keepdims=True)
                o = mm(vt[kv, :, :keys], e.astype(BF)) / total
                ob[h, p * rows : (p + 1) * rows, :] = o.T
                lse_ref[pl.ds(h, 1), p * rows : (p + 1) * rows] = peak + jnp.log(total)
            return 0

        lax.fori_loop(0, heads, one, 0)
        low = lower_half((rows, 128))
        for p in range(blocks):
            to = lax.rem(p - me + blocks, blocks)
            for b in range(heads // 2):
                at = slice(p * rows, (p + 1) * rows)
                out_ref[to, :, b * 128 : (b + 1) * 128] = jnp.where(
                    low, ob[2 * b, at, :], ob[2 * b + 1, at, :]
                ).astype(BF)

    pairs = heads * rows * rows * blocks * (blocks + 1) // 2
    return pl.pallas_call(
        body,
        out_shape=(
            jax.ShapeDtypeStruct((blocks, rows, qw), BF),
            jax.ShapeDtypeStruct((8, span), F32),
        ),
        in_specs=[SM] + [VM] * blocks,
        out_specs=(VM, VM),
        scratch_shapes=[
            pltpu.VMEM((heads, span, 128), BF),
            pltpu.VMEM((kvs, span, 128), BF),
            pltpu.VMEM((kvs, span, 128), F32),
            pltpu.VMEM((kvs, 128, span), BF),
            pltpu.VMEM((heads, span, 128), F32),
        ],
        compiler_params=params(),
        cost_estimate=cost(pairs * 1024, 4 * span * width, pairs),
        name="attend",
    )(scalars, *pieces)


def attend_back(scalars, pieces, grads, lse, cos, sin, heads, kvs):
    blocks = len(pieces)
    rows, width = pieces[0].shape
    span = blocks * rows
    qw = heads * HEAD_DIM
    share = heads // kvs

    def body(s_ref, *refs):
        ins, gins = refs[:blocks], refs[blocks : 2 * blocks]
        lse_ref, cos_ref, sin_ref, out_ref, qs, gs, kd, kf, kt, vd, dk, dv, dq = refs[2 * blocks :]
        me = s_ref[4]
        for k in range(blocks):
            at = pl.ds(pl.multiple_of(s_ref[k] * rows, rows), rows)
            block = ins[k][...]
            stage_heads(block, qs, at, heads, score_scale)
            for i, x in enumerate(doubled(block[:, qw : qw + 128])):
                kd[i, at, :] = x.astype(BF)
                kf[i, at, :] = x
            for i, x in enumerate(doubled(block[:, qw + 128 : qw + 256])):
                vd[i, at, :] = x.astype(BF)
            at = pl.ds(pl.multiple_of(lax.rem(me + k, blocks) * rows, rows), rows)
            stage_heads(gins[k][...], gs, at, heads, 1.0)
        for i in range(kvs):
            kt[i] = kf[i].T.astype(BF)
        dk[...] = jnp.zeros_like(dk)
        dv[...] = jnp.zeros_like(dv)

        def one(h, _):
            kv = h // share
            for p in range(blocks):
                keys = (p + 1) * rows
                at = slice(p * rows, (p + 1) * rows)
                q = qs[h, at, :]
                g = gs[h, at, :]
                s = mm(kd[kv, :keys, :], q, NT)
                log_total = lse_ref[pl.ds(h, 1), at]
                chances = jnp.where(
                    allowed_mask(s_ref, keys, rows, p * rows), jnp.exp(s - log_total), 0.0
                )
                gp = mm(vd[kv, :keys, :], g, NT)
                row_dot = jnp.sum(chances * gp, axis=0, keepdims=True)
                ds = (chances * (gp - row_dot)).astype(BF)
                dq[h, at, :] = mm(kt[kv, :, :keys], ds).T
                dk[kv, :keys, :] += mm(ds, q)
                dv[kv, :keys, :] += mm(chances.astype(BF), g)
            return 0

        lax.fori_loop(0, heads, one, 0)
        low = lower_half((rows, 128))
        for p in range(blocks):
            at = slice(p * rows, (p + 1) * rows)
            cosine, sine = cos_ref[at, :], -sin_ref[at, :]
            for b in range(heads // 2):
                x = jnp.where(low, dq[2 * b, at, :], dq[2 * b + 1, at, :]) * score_scale
                out_ref[at, b * 128 : (b + 1) * 128] = turn(x, cosine, sine).astype(BF)
            k0, k1, v0, v1 = dk[0, at, :], dk[1, at, :], dv[0, at, :], dv[1, at, :]
            k0, k1 = k0 + pltpu.roll(k0, 64, 1), k1 + pltpu.roll(k1, 64, 1)
            v0, v1 = v0 + pltpu.roll(v0, 64, 1), v1 + pltpu.roll(v1, 64, 1)
            out_ref[at, qw : qw + 128] = turn(jnp.where(low, k0, k1), cosine, sine).astype(BF)
            out_ref[at, qw + 128 : qw + 256] = jnp.where(low, v0, v1).astype(BF)

    pairs = heads * rows * rows * blocks * (blocks + 1) // 2
    return pl.pallas_call(
        body,
        out_shape=jax.ShapeDtypeStruct((span, width), BF),
        in_specs=[SM] + [VM] * (2 * blocks + 3),
        out_specs=VM,
        scratch_shapes=[
            pltpu.VMEM((heads, span, 128), BF),
            pltpu.VMEM((heads, span, 128), BF),
            pltpu.VMEM((kvs, span, 128), BF),
            pltpu.VMEM((kvs, span, 128), F32),
            pltpu.VMEM((kvs, 128, span), BF),
            pltpu.VMEM((kvs, span, 128), BF),
            pltpu.VMEM((kvs, span, 128), F32),
            pltpu.VMEM((kvs, span, 128), F32),
            pltpu.VMEM((heads, span, 128), F32),
        ],
        compiler_params=params(),
        cost_estimate=cost(pairs * 2560, 8 * span * width, pairs),
        name="attend_back",
    )(scalars, *pieces, *grads, lse, cos, sin)


def join(scalars, mixes, w_out, tok, gain):
    blocks = len(mixes)
    rows, part = mixes[0].shape
    d = tok.shape[1]

    def body(s_ref, *refs):
        ins, (w_ref, tok_ref, gain_ref, mid_ref, hid_ref) = refs[:blocks], refs[blocks:]
        me = s_ref[4]
        branch = jnp.zeros((rows, d), F32)
        for k in range(blocks):
            at = pl.ds(pl.multiple_of(lax.rem(me - k + blocks, blocks) * part, part), part)
            branch = branch + mm(ins[k][...], w_ref[at, :])
        middle = tok_ref[...].astype(F32) + residual_scale * branch
        mid_ref[...] = middle
        hid_ref[...] = (middle * rms(middle) * gain_ref[...]).astype(BF)

    return pl.pallas_call(
        body,
        out_shape=(jax.ShapeDtypeStruct((rows, d), F32), jax.ShapeDtypeStruct((rows, d), BF)),
        in_specs=[SM] + [VM] * (blocks + 3),
        out_specs=(VM, VM),
        compiler_params=params(),
        cost_estimate=cost(2 * rows * d * d, 2 * d * d + 10 * rows * d),
        name="join",
    )(scalars, *mixes, w_out, tok, gain)


def join_back(scalars, addends, middle, cot, gain, w_out, mixes, here, nd, ne):
    blocks = len(mixes)
    rows, part = mixes[0].shape
    d = middle.shape[1]

    w_rows = d // (nd * blocks * ne)

    def body(s_ref, here_ref, a_ref, b_ref, c_ref, mid_ref, cot_ref, gain_ref, w_ref, *refs):
        ins, (gmid_ref, gmix_ref, gw_ref, gg_ref) = refs[:blocks], refs[blocks:]
        me = s_ref[4]
        grad_hidden = a_ref[...].astype(F32) + b_ref[...].astype(F32) + c_ref[...].astype(F32)
        middle = mid_ref[...]
        inv = rms(middle)
        normal = middle * inv
        gg_ref[...] = jnp.sum(grad_hidden * normal, axis=0, keepdims=True)
        u = grad_hidden * gain_ref[...]
        grad_middle = cot_ref[...] + inv * (u - normal * jnp.mean(u * normal, axis=-1, keepdims=True))
        gmid_ref[...] = grad_middle
        branch = (residual_scale * grad_middle).astype(BF)
        for k in range(blocks):
            at = pl.ds(pl.multiple_of(lax.rem(me - k + blocks, blocks) * part, part), part)
            gmix_ref[k] = mm(branch, w_ref[at, :], NT).astype(BF)
            gw = mm(ins[k][...], branch, TN)
            for i in range(part // w_rows):
                q = lax.rem(me - k + blocks, blocks) * (part // w_rows) + i
                e = swapped(jnp.bitwise_xor(lax.rem(q, ne), here_ref[3]))
                b = lax.div(q, ne)
                m = lax.rem(lax.div(b, blocks) - here_ref[0] + nd, nd)
                gw_ref[e, m, lax.rem(b, blocks)] = gw[i * w_rows : (i + 1) * w_rows, :].astype(BF)

    return pl.pallas_call(
        body,
        out_shape=(
            jax.ShapeDtypeStruct((rows, d), F32),
            jax.ShapeDtypeStruct((blocks, rows, part), BF),
            jax.ShapeDtypeStruct((ne, nd, blocks, w_rows, d), BF),
            jax.ShapeDtypeStruct((1, d), F32),
        ),
        in_specs=[SM, SM] + [VM] * (7 + blocks),
        out_specs=(VM, VM, VM, VM),
        compiler_params=params(),
        cost_estimate=cost(4 * rows * d * d, 4 * d * d + 18 * rows * d),
        name="join_back",
    )(scalars, here, *addends, middle, cot, gain, w_out, *mixes)


def halves(w, odd, devices):
    n, r, width = w.shape
    unit = FF // devices
    if 2 * unit != 128:
        parts = w.reshape(n, r, 2, devices // 4, 2, 2, unit)
        parts = jnp.transpose(parts, (5, 0, 1, 2, 3, 4, 6)).reshape(2, n, r, FF)
        return pick(parts, odd), pick(parts, 1 - odd)

    def body(odd_ref, w_ref, mine_ref, their_ref):
        low = lower_half((r, 128))
        even = odd_ref[0] == 0
        for m in range(width // 256):
            a = w_ref[0, :, 2 * m * 128 : (2 * m + 1) * 128].astype(F32)
            b = w_ref[0, :, (2 * m + 1) * 128 : (2 * m + 2) * 128].astype(F32)
            evens = jnp.where(low, a, pltpu.roll(b, 64, 1))
            odds = jnp.where(low, pltpu.roll(a, 64, 1), b)
            at = slice(m * 128, (m + 1) * 128)
            mine_ref[0, :, at] = jnp.where(even, evens, odds).astype(BF)
            their_ref[0, :, at] = jnp.where(even, odds, evens).astype(BF)

    spec = pl.BlockSpec((1, r, FF), lambda e: (e, 0, 0))
    return pl.pallas_call(
        body,
        grid=(n,),
        out_shape=(jax.ShapeDtypeStruct((n, r, FF), BF),) * 2,
        in_specs=[SM, pl.BlockSpec((1, r, width), lambda e: (e, 0, 0))],
        out_specs=(spec, spec),
        compiler_params=params(),
        cost_estimate=cost(0, 4 * n * r * width),
        name="halves",
    )(odd[None].astype(jnp.int32), w)


def whole(own, other, theirs, odd, devices):
    _, r, width = own.shape
    r3 = r // 3
    unit = FF // devices
    if 2 * unit != 128:
        total = own.astype(F32) + other.astype(F32)
        theirs = theirs.astype(F32)
        parts = jnp.stack([jnp.where(odd == 0, total[0], theirs), jnp.where(odd == 0, theirs, total[0])])
        parts = parts.reshape(2, r, 2, devices // 4, 2, unit)
        down = [total[2, b * r3 : (b + 1) * r3] for b in range(3)]
        return jnp.transpose(parts, (1, 2, 3, 4, 0, 5)).reshape(r, 2 * width), jnp.concatenate(down, axis=1)

    def body(odd_ref, own_ref, other_ref, their_ref, in_ref, down_ref):
        low = lower_half((r, 128))
        even = odd_ref[0] == 0
        for m in range(width // 128):
            at = slice(m * 128, (m + 1) * 128)
            mine = own_ref[0, :, at].astype(F32) + other_ref[0, :, at].astype(F32)
            their = their_ref[:, at].astype(F32)
            evens, odds = jnp.where(even, mine, their), jnp.where(even, their, mine)
            in_ref[:, 2 * m * 128 : (2 * m + 1) * 128] = jnp.where(low, evens, pltpu.roll(odds, 64, 1))
            in_ref[:, (2 * m + 1) * 128 : (2 * m + 2) * 128] = jnp.where(low, pltpu.roll(evens, 64, 1), odds)
        for b in range(3):
            at = slice(b * r3, (b + 1) * r3)
            down_ref[:, b * width : (b + 1) * width] = own_ref[2, at, :].astype(F32) + other_ref[2, at, :].astype(F32)

    return pl.pallas_call(
        body,
        out_shape=(
            jax.ShapeDtypeStruct((r, 2 * width), F32),
            jax.ShapeDtypeStruct((r3, 3 * width), F32),
        ),
        in_specs=[SM, VM, VM, VM],
        out_specs=(VM, VM),
        compiler_params=params(),
        cost_estimate=cost(0, 20 * r * width),
        name="whole",
    )(odd[None].astype(jnp.int32), own, other, theirs)


def experts_rows(places, which, rows_in, cots, shards, sums, last):
    piece, d = rows_in[0].shape
    group = 2
    rows = piece * group
    tiles = len(rows_in) // group
    total = rows * tiles
    count = len(shards)
    n, _, r, width = shards[0].shape
    half = width // 2
    r3 = r // 3
    first = sums is None

    def body(places_ref, *refs):
        n_in = tiles * group
        h_refs, c_refs, refs = refs[:n_in], refs[n_in : 2 * n_in], refs[2 * n_in :]
        w_refs, refs = refs[:count], refs[count:]
        if not first:
            in_h, in_o, refs = refs[0], refs[1], refs[2:]
        if last:
            out_h, rest_h, out_o, rest_o, gb_ref, gat_ref, *refs = refs
        else:
            out_h, out_o, gb_ref, gat_ref, *refs = refs
        if first:
            ht_ref, *refs = refs
        wiv, wdv, ga_ref, hv, cv, sems, row_sems = refs
        t = pl.program_id(0)
        moves = []
        for i in range(n_in):
            at = pl.ds(i % group * piece, piece)
            moves.append(
                (
                    pltpu.make_async_copy(h_refs[i], hv.at[i // group, at, :], row_sems.at[0, i]),
                    pltpu.make_async_copy(c_refs[i], cv.at[i // group, at, :], row_sems.at[1, i]),
                )
            )

        @pl.when(t == 0)
        def _():
            copies = []
            for i in range(count):
                for e in range(n):
                    parts = []
                    for b in range(2):
                        at = pl.multiple_of(places_ref[3 * i + b] * r, r)
                        parts.append((w_refs[i].at[e, b], wiv.at[pl.ds(at, r), e * width : (e + 1) * width]))
                    at = pl.multiple_of(places_ref[3 * i + 2] * r3 + e * half, r3)
                    for b in range(3):
                        parts.append(
                            (
                                w_refs[i].at[e, 2, b * r3 : (b + 1) * r3, :],
                                wdv.at[pl.ds(at, r3), b * width : (b + 1) * width],
                            )
                        )
                    for k, (a, b) in enumerate(parts):
                        copies.append(pltpu.make_async_copy(a, b, sems.at[i, e, k]))
            for copy in copies:
                copy.start()
            for a, b in moves:
                a.start()
                b.start()
            for copy in copies:
                copy.wait()

        for i in range(tiles):

            @pl.when(t == i)
            def _():
                for a, b in moves[i * group : (i + 1) * group]:
                    a.wait()
                    b.wait()

        h = hv[t]
        c = cv[t, :, :d]
        gates = cv[t, :, d:].astype(F32)
        lane = lax.broadcasted_iota(jnp.int32, gates.shape, 1) - places_ref[3 * count]
        for e in range(n):
            g = jnp.sum(jnp.where(lane == which + e, gates, 0.0), axis=1, keepdims=True)
            gu = mm(h, wiv[:, e * width : (e + 1) * width])
            gate, up = gu[:, :half], gu[:, half:]
            sg = jax.nn.sigmoid(gate)
            silu = gate * sg
            ga = mm(c, wdv[e * half : (e + 1) * half, :], NT) * g
            ga_ref[:, e * half : (e + 1) * half] = (silu * up * g).astype(BF)
            gb_ref[:, e * width : e * width + half] = (ga * up * (sg + silu * (1.0 - sg))).astype(BF)
            gb_ref[:, e * width + half : (e + 1) * width] = (ga * silu).astype(BF)
        o = mm(ga_ref[...], wdv[...])
        gh = mm(gb_ref[...], wiv[...], NT)
        gat_ref[...] = ga_ref[...].T
        if first:
            ht_ref[...] = h.T
        if not first:
            o = o + in_o[...]
            gh = gh + in_h[...]
        if last:

            @pl.when(t < tiles // 2)
            def _():
                out_o[...] = o.astype(BF)
                out_h[...] = gh.astype(BF)

            @pl.when(t >= tiles // 2)
            def _():
                rest_o[...] = o.astype(BF)
                rest_h[...] = gh.astype(BF)

        else:
            out_o[...] = o
            out_h[...] = gh

    tile = lambda c: pl.BlockSpec((rows, c), lambda t: (t, 0))
    flat = lambda c: pl.BlockSpec((c, rows), lambda t: (0, t))
    if last:
        sum_shapes = (jax.ShapeDtypeStruct((total // 2, d), BF),) * 4
        front = pl.BlockSpec((rows, d), lambda t: (jnp.minimum(t, tiles // 2 - 1), 0))
        back = pl.BlockSpec((rows, d), lambda t: (jnp.maximum(t - tiles // 2, 0), 0))
        sum_specs = (front, back, front, back)
    else:
        sum_shapes = (jax.ShapeDtypeStruct((total, d), F32),) * 2
        sum_specs = (tile(d), tile(d))
    return pl.pallas_call(
        body,
        grid=(tiles,),
        out_shape=sum_shapes
        + (
            jax.ShapeDtypeStruct((total, n * width), BF),
            jax.ShapeDtypeStruct((n * half, total), BF),
        )
        + ((jax.ShapeDtypeStruct((d, total), BF),) if first else ()),
        in_specs=[SM]
        + [ANY] * (2 * len(rows_in) + count)
        + ([] if first else [tile(d), tile(d)]),
        out_specs=sum_specs + (tile(n * width), flat(n * half)) + ((flat(d),) if first else ()),
        scratch_shapes=[
            pltpu.VMEM((d, n * width), BF),
            pltpu.VMEM((n * half, d), BF),
            pltpu.VMEM((rows, n * half), BF),
            pltpu.VMEM((tiles, rows, d), BF),
            pltpu.VMEM((tiles, rows, cots[0].shape[1]), BF),
            pltpu.SemaphoreType.DMA((count, n, 5)),
            pltpu.SemaphoreType.DMA((2, len(rows_in))),
        ],
        compiler_params=params(),
        cost_estimate=cost(6 * n * total * d * width, 50e6, n * total * half),
        name="experts_rows",
    )(places, *rows_in, *cots, *shards, *(() if first else sums))


def experts_weights(scalars, rows_t, cots, gb, ga_t, n, devices):
    d, total = rows_t.shape
    width, half = gb.shape[1] // n, ga_t.shape[0] // n
    r = d // devices
    r3 = r // 3
    nd = devices // 4
    tiles = len(cots)
    rows = total // tiles

    def body(s_ref, h_any, gb_any, ga_any, *refs):
        c_refs, refs = refs[:tiles], refs[tiles:]
        outs, (down, h_ref, gb_ref, ga_ref, c_ref, stage, sems, c_sems, out_sems) = refs[: n * nd], refs[n * nd :]
        ahead = [lax.rem(s_ref[0] + k, nd) for k in range(nd)]
        spans = [pl.ds(pl.multiple_of(x * 4 * r, 4 * r), 4 * r) for x in ahead]
        first = [pltpu.make_async_copy(gb_any, gb_ref, sems.at[0])]
        first += [
            pltpu.make_async_copy(h_any.at[spans[k], :], h_ref.at[k], sems.at[1 + k]) for k in range(nd)
        ]
        second = [pltpu.make_async_copy(ga_any, ga_ref, c_sems.at[tiles])]
        second += [
            pltpu.make_async_copy(c_refs[i].at[:, :d], c_ref.at[pl.ds(i * rows, rows), :], c_sems.at[i])
            for i in range(tiles)
        ]
        for copy in first + second:
            copy.start()
        first[0].wait()
        for k in range(nd):
            first[1 + k].wait()
            part = mm(h_ref[k], gb_ref[...]).astype(BF)
            for z in range(4):
                where = jnp.bitwise_xor(s_ref[2], z // 2)
                slot = jnp.bitwise_xor(s_ref[1], z % 2)
                for e in range(n):
                    stage[e * nd + k, where, slot] = part[z * r : (z + 1) * r, e * width : (e + 1) * width]
        for copy in second:
            copy.wait()
        leaving = []
        for e in range(n):
            down[...] = mm(ga_ref[e * half : (e + 1) * half, :], c_ref[...]).astype(BF)
            for k in range(nd):
                for z in range(2):
                    where = jnp.bitwise_xor(s_ref[2], z)
                    at = pl.ds(pl.multiple_of((2 * ahead[k] + z) * r3, r3), r3)
                    for b in range(3):
                        stage[e * nd + k, where, 2, b * r3 : (b + 1) * r3, :] = down[
                            at, b * width : (b + 1) * width
                        ]
                leaving.append(
                    pltpu.make_async_copy(stage.at[e * nd + k], outs[e * nd + k], out_sems.at[e * nd + k])
                )
                leaving[-1].start()
        for copy in leaving:
            copy.wait()

    outs = pl.pallas_call(
        body,
        out_shape=[jax.ShapeDtypeStruct((2, 3, r, width), BF)] * (n * nd),
        in_specs=[SM] + [ANY] * (3 + tiles),
        out_specs=[ANY] * (n * nd),
        scratch_shapes=[
            pltpu.VMEM((half, d), BF),
            pltpu.VMEM((nd, 4 * r, total), BF),
            pltpu.VMEM((total, n * width), BF),
            pltpu.VMEM((n * half, total), BF),
            pltpu.VMEM((total, d), BF),
            pltpu.VMEM((n * nd, 2, 3, r, width), BF),
            pltpu.SemaphoreType.DMA((1 + nd,)),
            pltpu.SemaphoreType.DMA((tiles + 1,)),
            pltpu.SemaphoreType.DMA((n * nd,)),
        ],
        compiler_params=params(),
        cost_estimate=cost(3 * n * total * d * width, 20e6),
        name="experts_weights",
    )(scalars, rows_t, gb, ga_t, *cots)
    return [outs[e * nd : (e + 1) * nd] for e in range(n)]


def finish(scalars, dqkv, w, toks, gain, gain_grad, here, nd, ne):
    blocks = len(toks)
    rows, d = toks[0].shape
    width = dqkv.shape[1]

    w_rows = d // (nd * blocks * ne)

    def body(s_ref, here_ref, dq_ref, w_ref, gain_ref, gg_ref, *refs):
        ins, (gn_ref, gw_ref, acc) = refs[:blocks], refs[blocks:]
        gg = jnp.zeros((1, d), F32)
        for k in range(blocks):
            to = s_ref[k]
            at = pl.ds(pl.multiple_of(to * rows, rows), rows)
            dqkv_block = dq_ref[at, :]
            t = ins[k][...].astype(F32)
            normal = t * rms(t)
            normed = (normal * gain_ref[...]).astype(BF)
            gn = mm(dqkv_block, w_ref[...], NT)
            gg = gg + jnp.sum(gn * normal, axis=0, keepdims=True)
            gn_ref[to] = gn.astype(BF)
            part = mm(normed, dqkv_block, TN)
            acc[...] = part if k == 0 else acc[...] + part
        row = lax.broadcasted_iota(jnp.int32, (128, d), 0)
        both = jnp.where(row == 0, gg, jnp.where(row == 1, gg_ref[...], 0.0)).T
        for q in range(d // w_rows):
            e = swapped(jnp.bitwise_xor(q % ne, here_ref[3]))
            m = lax.rem(q // ne // blocks - here_ref[0] + nd, nd)
            at = slice(q * w_rows, (q + 1) * w_rows)
            gw_ref[e, m, q // ne % blocks, :, :width] = acc[at, :].astype(BF)
            gw_ref[e, m, q // ne % blocks, :, width:] = both[at, :].astype(BF)

    return pl.pallas_call(
        body,
        out_shape=(
            jax.ShapeDtypeStruct((blocks, rows, d), BF),
            jax.ShapeDtypeStruct((ne, nd, blocks, w_rows, width + 128), BF),
        ),
        in_specs=[SM, SM] + [VM] * (4 + blocks),
        out_specs=(VM, VM),
        scratch_shapes=[pltpu.VMEM((d, width), F32)],
        compiler_params=params(),
        cost_estimate=cost(4 * blocks * rows * d * width, 8 * blocks * rows * d),
        name="finish",
    )(scalars, here, dqkv, w, gain, gain_grad, *toks)


def per_device(
    tokens,
    gain_attn,
    w_query,
    w_key,
    w_value,
    w_out,
    gain_moe,
    w_in,
    w_down,
    routes,
    gates,
    lengths,
    cotangent,
):
    nd, nz, ne = lax.axis_size("dp"), lax.axis_size("ctx"), lax.axis_size("exp")
    x, z, j = lax.axis_index("dp"), lax.axis_index("ctx"), lax.axis_index("exp")
    rows, d = tokens.shape[1:]
    span = rows * nz
    w_rows = w_query.shape[0]
    heads, kvs = HEADS // nz, KV_HEADS // nz
    qw, kw = heads * HEAD_DIM, kvs * HEAD_DIM
    local_experts = w_in.shape[0]
    experts = local_experts * ne
    i32 = jnp.int32
    mod = lambda v, n: lax.rem(v + 8 * n, n)

    ends = jnp.cumsum(lengths[0]).astype(i32)
    places = [mod(z - k, nz) for k in range(nz)]
    scalars = jnp.concatenate([jnp.stack(places + [z]).astype(i32), ends])
    place = jnp.arange(span, dtype=i32)
    place = place - jnp.max(jnp.where(place[:, None] >= ends[None, :-1], ends[None, :-1], 0), axis=1)
    lane = jnp.arange(128, dtype=i32)
    half = HEAD_DIM // 2
    frequency = rope_base ** (-2.0 * jnp.arange(half, dtype=F32) / HEAD_DIM)
    angles = place.astype(F32)[:, None] * frequency[None, :]
    cos = jnp.tile(jnp.cos(angles), (1, 128 // half))
    sin = jnp.tile(jnp.sin(angles), (1, 128 // half)) * jnp.where((lane & 63) < 32, -1.0, 1.0)[None, :]

    run = Stages(gain_attn)
    gain_a, gain_m = gain_attn[None, :], gain_moe[None, :]
    devices = nd * nz
    odd, zh = jnp.bitwise_and(z, 1), z // 2
    batch = local_experts // 2
    tok, cot = tokens[0], cotangent[0]
    cot_b = (residual_scale * cot).astype(BF)
    flip_e = lambda v, e: flip(v, "exp", e)

    def row_blocks(found, owners):
        at = [
            (mod(x - m, nd) * nz + p) * ne + jnp.bitwise_xor(j, e + 2 * b)
            for e in (0, 1) for m in range(nd) for b in (0, 1) for p in owners
        ]
        return assemble(found, jnp.stack(at).astype(i32))

    here = jnp.stack([x, odd, zh, j]).astype(i32)

    parts = [
        jnp.concatenate(
            [
                w_query[:, p * qw : (p + 1) * qw],
                w_key[:, p * kw : (p + 1) * kw],
                w_value[:, p * kw : (p + 1) * kw],
            ],
            axis=1,
        )
        for p in range(nz)
    ]
    w_parts = jnp.stack(parts)
    toks = [tok, shift(tok, "ctx", 1)]
    w_mine = [pick(w_parts, z)] + [shift(pick(w_parts, mod(z + k, nz)), "ctx", k) for k in range(1, nz)]
    hits = routes[0][:, :, None] == jnp.arange(128, dtype=i32)[None, None, :]
    dense = jnp.sum(jnp.where(hits, gates[0].astype(F32)[:, :, None], 0.0), axis=1).astype(BF)
    cot_b = jnp.concatenate([cot_b, dense], axis=1)
    mine_in, their_in = halves(w_in, odd, devices)
    down = jnp.concatenate([w_down[:, :, b * FF : (b + 1) * FF] for b in range(d // FF)], axis=1)
    run.end(toks, w_mine)

    cut = rows // 2
    half_2 = [shift(run.hold(toks[1][:cut]), "ctx", 1)]
    w_mine = jnp.stack(w_mine)
    w_mine = jnp.stack([w_mine, flip_e(run.hold(w_mine), 2)])
    line = [hop(run.hold(w_out), pairs) for pairs in (ACROSS, UP, DOWN)]
    run.end(half_2, w_mine, line, mine_in)

    half_2.append(shift(run.hold(toks[1][cut:]), "ctx", 1))
    w_found = ring(run.hold(w_mine), "dp")
    line_end = hop(run.hold(line[0]), OUTER)
    run.end(half_2, w_found, line_end)

    toks.append(jnp.concatenate(half_2))
    toks.append(shift(run.hold(toks[2]), "ctx", 1))
    got_1 = flip(run.hold(their_in[:batch]), "ctx", 1)
    w_found = w_found + [flip_e(t, 1) for t in run.hold(w_found)]
    w_line = ring(run.hold(jnp.stack(line_gather(*line, line_end, w_out))), "dp")
    cot_2 = flip_e(run.hold(cot_b), 2)
    w_qkv = row_blocks(w_found, places)
    at = [p[None].astype(i32) for p in places]
    pieces = [project(toks[k], gain_a, w_qkv, cos, sin, at[k]) for k in range(nz - 1)]
    run.end(toks, pieces, got_1, w_line, cot_2)

    near_1 = jnp.stack([mine_in[:batch], got_1, down[:batch]], axis=1)
    far = [flip(run.hold(near_1[:1]), "ctx", 2)]
    own_1 = ring(run.hold(near_1), "dp")
    w_line = jnp.stack(w_line)
    w_line = jnp.stack([w_line, flip_e(run.hold(w_line), 2)], axis=1)
    cot_n = flip(run.hold(cot_b), "ctx", 1)
    pieces.append(project(run.hold(toks[3]), gain_a, w_qkv, cos, sin, at[3]))
    mix_out, lse = attend(scalars, pieces, heads, kvs)
    run.end(far, own_1, w_line, cot_n, mix_out)

    mixes = run.hold([mix_out[k] for k in range(nz)])
    mixes = [mixes[0]] + [shift(mixes[k], "ctx", k) for k in range(1, nz)]
    w_line = [w_line, flip_e(run.hold(w_line), 1)]
    cot_n2 = flip_e(run.hold(cot_n), 2)
    w_out_all = row_blocks(w_line, line_places(z))
    run.end(mixes, w_out_all, cot_n2)

    cot_1, cot_3 = flip_e(run.hold(cot_b), 1), flip_e(run.hold(cot_2), 1)
    got_2 = flip(run.hold(their_in[batch:]), "ctx", 1)
    middle, hidden = join(scalars, run.hold(mixes), w_out_all, tok, gain_m)
    run.end(hidden, got_2, cot_1, cot_3)

    hidden_2, hidden_n = flip_e(run.hold(hidden), 2), flip(run.hold(hidden), "ctx", 1)
    near_2 = jnp.stack([mine_in[batch:], got_2, down[batch:]], axis=1)
    far.append(flip(run.hold(near_1[1:]), "ctx", 2))
    own_2 = ring(run.hold(near_2), "dp")
    hidden_1 = flip_e(run.hold(hidden), 1)
    run.end(hidden_1, hidden_2, hidden_n, far, own_2)

    hidden_n2 = flip_e(run.hold(hidden_n), 2)
    hidden_n1, hidden_3 = flip_e(run.hold(hidden_n), 1), flip_e(run.hold(hidden_2), 1)
    over_1 = ring(run.hold(jnp.concatenate(far)), "dp")
    far_2 = [flip(run.hold(near_2[:1]), "ctx", 2)]
    run.end(hidden_n2, hidden_n1, hidden_3, over_1, far_2)

    hidden_n3 = flip_e(run.hold(hidden_n2), 1)
    cot_n1, cot_n3 = flip_e(run.hold(cot_n), 1), flip_e(run.hold(cot_n2), 1)
    rows_in = [hidden, hidden_n, hidden_2, hidden_n2, hidden_1, hidden_n1, hidden_3, hidden_n3]
    cots = [cot_b, cot_n, cot_2, cot_n2, cot_1, cot_n1, cot_3, cot_n3]
    w_at = []
    for zc in (z, jnp.bitwise_xor(z, 2)):
        for m in range(nd):
            xc = mod(x - m, nd)
            w_at += [xc * nz + zc, xc * nz + jnp.bitwise_xor(zc, 1), xc * 2 + zc // 2]
    w_at = jnp.stack(w_at + [j * local_experts]).astype(i32)
    far_2.append(flip(run.hold(near_2[1:]), "ctx", 2))
    over_2 = [ring(run.hold(far_2[0]), "dp")]
    sum_h, sum_o, gb, ga_t, rows_t = experts_rows(
        w_at, 0, run.hold(rows_in), cots, own_1 + over_1, None, False
    )
    run.end(far_2, over_2, sum_h)

    over_2.append(ring(run.hold(far_2[1]), "dp"))
    gw_1 = experts_weights(here, rows_t, cots, run.hold(gb), ga_t, batch, devices)
    run.end(over_2, gw_1)

    x_0 = dp_reduce(run.hold(gw_1[0]))
    over_2 = [jnp.concatenate(t) for t in zip(*over_2)]
    sum_h, rest_h, sum_o, rest_o, gb, ga_t = experts_rows(
        w_at, batch, run.hold(rows_in), cots, own_2 + over_2, (sum_h, sum_o), True
    )
    run.end(x_0, sum_h)

    def swap(own, other):
        return flip((own[0, 1].astype(F32) + other[1].astype(F32)).astype(BF), "ctx", 1)

    rest_h = flip_e(run.hold(rest_h), 1)
    run.end(rest_h)

    part = rows // 2
    sum_h = [
        (sum_h[a * part : b * part].astype(F32) + rest_h[a * part : b * part].astype(F32)).astype(BF)
        for a, b in ((0, 2), (2, 3), (3, 4), (4, 5), (5, 6), (6, 7), (7, 8))
    ]
    by_y, by_z = flip_e(run.hold(sum_h[5]), 2), flip(run.hold(sum_h[6]), "ctx", 1)
    z_0 = flip(run.hold(x_0)[1], "ctx", 2)
    x_1 = dp_reduce(run.hold(gw_1[1]))
    gw_2 = experts_weights(here, rows_t, cots, run.hold(gb), ga_t, batch, devices)
    run.end(by_y, by_z, z_0, x_1, gw_2)

    add = lambda a, b: (a.astype(F32) + b.astype(F32)).astype(BF)
    near_h = flip_e(run.hold(jnp.concatenate([sum_h[3], add(sum_h[4], by_z)])), 2)
    other_h = flip(run.hold(jnp.concatenate([add(sum_h[1], by_y), sum_h[2]])), "ctx", 1)
    z_1 = flip(run.hold(x_1)[1], "ctx", 2)
    x_2 = dp_reduce(run.hold(gw_2[0]))
    rest_o = flip_e(run.hold(rest_o), 1)
    run.end(near_h, other_h, z_1, x_2, rest_o)

    def fold(g):
        return g[0].astype(F32), (g[1].astype(F32) + g[3].astype(F32)).astype(BF)

    swap_0 = swap(*run.hold([x_0, z_0]))
    grad_middle, grad_mix, grad_w_out, grad_gain_m = join_back(
        scalars, [sum_h[0], *run.hold([near_h, other_h])], middle, cot, gain_m, w_out_all, mixes, here, nd, ne
    )
    grad_mixes = [grad_mix[0]] + [shift(grad_mix[k], "ctx", -k) for k in range(1, nz)]
    wo_core = flip_e(grad_w_out[2:], 1)
    run.end(grad_mixes, wo_core, swap_0)

    x_3 = dp_reduce(run.hold(gw_2[1]))
    z_2 = flip(run.hold(x_2)[1], "ctx", 2)
    swap_1 = swap(*run.hold([x_1, z_1]))
    wo_core = run.hold(wo_core)
    wo = add(grad_w_out[0], wo_core[0])
    wo_far = flip_e(add(grad_w_out[1], wo_core[1]), 2)
    dqkv = attend_back(scalars, pieces, run.hold(grad_mixes), lse, cos, sin, heads, kvs)
    sum_o = add(sum_o, run.hold(rest_o))
    run.end(x_3, z_2, swap_1, wo_far, dqkv, sum_o)

    wo = dp_reduce(list(run.hold(add(wo, wo_far))))
    grad_normed, grad_w = finish(
        scalars, run.hold(dqkv), w_qkv, toks, gain_a, grad_gain_m, here, nd, ne
    )
    run.end(grad_normed, grad_w, wo)

    tail = run.hold(grad_normed)
    feed = hop(pick(tail, 3 - z), INNER)
    z_3 = flip(run.hold(x_3)[1], "ctx", 2)
    far_o = flip_e(run.hold(sum_o[2 * rows :]), 2)
    gw_core = flip_e(run.hold(grad_w[2:]), 1)
    run.end(feed, z_3, far_o, gw_core)

    across = hop(run.hold(add(pick(tail, jnp.bitwise_xor(z, 2)), feed)), ACROSS)
    below = hop(run.hold(pick(tail, jnp.minimum(z + 1, 3))), UP)
    above = hop(run.hold(pick(tail, jnp.maximum(z - 1, 0))), DOWN)
    mine = add(grad_w[0], gw_core[0])
    mine = add(mine, flip_e(run.hold(add(grad_w[1], gw_core[1])), 2))
    mine = dp_reduce(list(mine))
    other_o = flip(run.hold(add(sum_o[rows : 2 * rows], far_o[rows:])), "ctx", 1)
    run.end(across, below, above, mine, other_o)

    swap_2, swap_3 = swap(*run.hold([x_2, z_2])), swap(*run.hold([x_3, z_3]))
    mine, wo = run.hold(mine), run.hold(wo)
    parts = [pick(mine, z)] + [shift(pick(mine, mod(z + k, nz)), "ctx", k) for k in range(1, nz)]
    outs = [pick(wo, z)] + [shift(pick(wo, mod(z + k, nz)), "ctx", k) for k in range(1, nz)]
    grad_out = sum(t.astype(F32) for t in outs)

    gn = pick(tail, z).astype(F32) + below.astype(F32) + above.astype(F32) + across.astype(F32)
    expert_sum = sum_o[:rows].astype(F32) + far_o[:rows].astype(F32) + other_o.astype(F32)
    mixed_out = (middle + residual_scale * expert_sum).astype(BF)
    gains = sum(p[:, qw + 2 * kw : qw + 2 * kw + 2].astype(F32) for p in parts)
    order = jnp.stack(parts)
    order = [pick(order, mod(z - p, nz)).astype(F32) for p in range(nz)]
    grad_query = jnp.concatenate([g[:, :qw] for g in order], axis=1)
    grad_key = jnp.concatenate([g[:, qw : qw + kw] for g in order], axis=1)
    grad_value = jnp.concatenate([g[:, qw + kw : qw + 2 * kw] for g in order], axis=1)

    grads = [
        whole(own[0], other, theirs, odd, devices)
        for own, other, theirs in (
            (x_0, z_0, swap_0), (x_1, z_1, swap_1), (x_2, z_2, swap_2), (x_3, z_3, swap_3)
        )
    ]
    grads_in = jnp.stack([g[0] for g in grads])
    grads_down = jnp.stack([g[1] for g in grads])

    t = tok.astype(F32)
    inv = rms(t)
    normal = t * inv
    u = gn * gain_a
    grad_tokens = grad_middle + inv * (u - normal * jnp.mean(u * normal, axis=-1, keepdims=True))
    return (
        mixed_out[None],
        grad_tokens[None],
        gains[:, 0],
        grad_query,
        grad_key,
        grad_value,
        grad_out.astype(F32),
        gains[:, 1],
        grads_in,
        grads_down,
    )


def solution(mesh):
    every = ("dp", "ctx", "exp")
    return jax.shard_map(
        per_device,
        mesh=mesh,
        in_specs=(
            P(("dp", "exp"), "ctx", None),
            P(),
            P(every, None),
            P(every, None),
            P(every, None),
            P(every, None),
            P(),
            P("exp", ("dp", "ctx"), None),
            P("exp", ("dp", "ctx"), None),
            P(("dp", "exp"), "ctx", None),
            P(("dp", "exp"), "ctx", None),
            P(("dp", "exp"), None),
            P(("dp", "exp"), "ctx", None),
        ),
        out_specs=(
            P(("dp", "exp"), "ctx", None),
            P(("dp", "exp"), "ctx", None),
            P(every),
            P(every, None),
            P(every, None),
            P(every, None),
            P(every, None),
            P(every),
            P("exp", ("dp", "ctx"), None),
            P("exp", ("dp", "ctx"), None),
        ),
        check_vma=False,
    )
```

```python
import functools

import jax
import jax.numpy as jnp
from jax import lax
from jax.experimental import pallas as pl
from jax.experimental.pallas import tpu as pltpu
from jax.sharding import PartitionSpec as P

HEADS = 24
KV_HEADS = 8
HEAD_DIM = 64
FF = 512
TOP = 8

eps_norm = 1e-06
score_scale = 0.015625
residual_scale = 0.22
rope_base = 10000.0

BF = jnp.bfloat16
F32 = jnp.float32
SCALE = 3
VMEM_LIMIT = 60 * 1024 * 1024
ANY = pl.BlockSpec(memory_space=pl.ANY)
VM = pl.BlockSpec(memory_space=pltpu.VMEM)
SM = pl.BlockSpec(memory_space=pltpu.SMEM)
NN = (((1,), (0,)), ((), ()))
NT = (((1,), (1,)), ((), ()))
TN = (((0,), (0,)), ((), ()))


def mm(a, b, dims=NN):
    return lax.dot_general(a, b, dims, preferred_element_type=F32)


def params(**kw):
    return pltpu.CompilerParams(vmem_limit_bytes=VMEM_LIMIT, **kw)


def cost(flops, nbytes, trans=0):
    return pl.CostEstimate(
        flops=int(flops / SCALE), bytes_accessed=int(nbytes / SCALE), transcendentals=0
    )


def shift(x, axis, by):
    n = lax.axis_size(axis)
    return lax.ppermute(x, axis, [(i, (i + by) % n) for i in range(n)])


def flip(x, axis, mask):
    n = lax.axis_size(axis)
    return lax.ppermute(x, axis, [(i, i ^ mask) for i in range(n)])


class Stages:
    def __init__(self, token):
        self.token = token

    def hold(self, x):
        leaves, tree = jax.tree.flatten(x)
        leaves = [lax.optimization_barrier((leaf, self.token))[0] for leaf in leaves]
        return jax.tree.unflatten(tree, leaves)

    def end(self, *outs):
        self.token = lax.optimization_barrier((self.token, *jax.tree.leaves(outs)))[0]


def ring(x, axis):
    out = [x]
    for _ in range(lax.axis_size(axis) - 1):
        out.append(shift(out[-1], axis, 1))
    return out


def hop(x, pairs):
    return lax.ppermute(x, "ctx", pairs)


UP, DOWN = [(0, 1), (1, 2), (2, 3)], [(1, 0), (2, 1), (3, 2)]
ACROSS = [(0, 2), (1, 3), (2, 0), (3, 1)]
INNER, OUTER = [(0, 1), (3, 2)], [(1, 0), (2, 3)]


def line_places(z):
    return [z, jnp.bitwise_xor(z, 2), jnp.where(z == 0, 3, z - 1), jnp.where(z == 3, 0, z + 1)]


def line_gather(across, below, above, end, x):
    z = lax.axis_index("ctx")
    return [x, across, jnp.where(z == 0, end, below), jnp.where(z == 3, end, above)]


def add(a, b):
    return (a.astype(F32) + b.astype(F32)).astype(BF)


def pick(x, index, dim=0):
    return lax.dynamic_index_in_dim(x, index, dim, False)


def dp_reduce(parts):
    n = lax.axis_size("dp")
    total = parts[n - 1]
    for k in range(1, n):
        total = add(shift(total, "dp", 1), parts[n - 1 - k])
    return total


def dp_reduce_pair(parts):
    n = lax.axis_size("dp")
    total = parts[n - 1]
    for k in range(1, n - 1):
        total = add(shift(total, "dp", 1), parts[n - 1 - k])
    if n == 1:
        return [total[0], total[1]]
    total = shift(total, "dp", 1)
    return [add(total[0], parts[0][0]), add(total[1], parts[0][1])]


def assemble(found, places):
    found = [t.reshape(-1, *t.shape[-2:]) for t in found]
    each, rows, width = found[0].shape
    count = each * len(found)
    total = count * rows
    if rows % 16:
        blocks = jnp.concatenate(found)
        return jnp.zeros_like(blocks).at[places].set(blocks).reshape(total, width)

    def body(places_ref, *refs):
        refs, out_ref, sems = refs[:-2], refs[-2], refs[-1]
        copies = []
        for i in range(count):
            at = pl.multiple_of(places_ref[i] * rows, rows)
            copies.append(
                pltpu.make_async_copy(refs[i // each].at[i % each], out_ref.at[pl.ds(at, rows), :], sems.at[i])
            )
        for copy in copies:
            copy.start()
        for copy in copies:
            copy.wait()

    return pl.pallas_call(
        body,
        out_shape=jax.ShapeDtypeStruct((total, width), found[0].dtype),
        in_specs=[SM] + [ANY] * len(found),
        out_specs=VM,
        scratch_shapes=[pltpu.SemaphoreType.DMA((count,))],
        compiler_params=params(),
        cost_estimate=cost(0, 4 * total * width),
        name="assemble",
    )(places, *found)


def rms(v):
    return lax.rsqrt(jnp.mean(v * v, axis=-1, keepdims=True) + eps_norm)


def turn(block, cos, sin):
    lane = lax.broadcasted_iota(jnp.int32, block.shape, 1)
    partner = jnp.where(
        (lane & 63) < 32, pltpu.roll(block, 96, 1), pltpu.roll(block, 32, 1)
    )
    return block * cos + partner * sin


def project(toks, gain, w, cos, sin, places):
    rows, d = toks[0].shape
    n = w.shape[1]
    turned = n - 128
    count = len(toks)

    def body(at_ref, gain_ref, w_ref, cos_ref, sin_ref, *refs):
        for i in range(count):
            tok_ref, out_ref = refs[i], refs[count + i]
            at = pl.ds(pl.multiple_of(at_ref[i] * rows, rows), rows)
            cosine, sine = cos_ref[at, :], sin_ref[at, :]
            t = tok_ref[...].astype(F32)
            normed = (t * rms(t) * gain_ref[...]).astype(BF)
            u = mm(normed, w_ref[...])
            for b in range(0, turned, 128):
                out_ref[:, b : b + 128] = turn(u[:, b : b + 128], cosine, sine).astype(BF)
            out_ref[:, turned:] = u[:, turned:].astype(BF)

    return pl.pallas_call(
        body,
        out_shape=[jax.ShapeDtypeStruct((rows, n), BF)] * count,
        in_specs=[SM] + [VM] * (4 + count),
        out_specs=[VM] * count,
        compiler_params=params(),
        cost_estimate=cost(2 * count * rows * d * n, 2 * d * n + 4 * count * rows * d),
        name="project",
    )(places, gain, w, cos, sin, *toks)


def swapped(e):
    return (e & 1) * 2 + (e >> 1)


def split_store(a_ref, b_ref, e, at, value):
    @pl.when(e < 2)
    def _():
        a_ref[(e, *at)] = value

    @pl.when(e >= 2)
    def _():
        b_ref[(e - 2, *at)] = value


def lower_half(shape):
    return lax.broadcasted_iota(jnp.int32, shape, 1) < 64


def stage_heads(block, dst, rows_at, heads, factor):
    rows = block.shape[0]
    low = lower_half((rows, 128))
    for h in range(heads):
        part = block[:, (h // 2) * 128 : (h // 2 + 1) * 128].astype(F32) * factor
        keep = low if h % 2 == 0 else jnp.logical_not(low)
        dst[h, rows_at, :] = jnp.where(keep, part, 0.0).astype(BF)


def doubled(block):
    block = block.astype(F32)
    low = lower_half(block.shape)
    other = pltpu.roll(block, 64, 1)
    return jnp.where(low, block, other), jnp.where(low, other, block)


def allowed_mask(s_ref, keys, rows, first):
    q = lax.broadcasted_iota(jnp.int32, (1, rows), 1) + first
    begin = jnp.zeros_like(q)
    for i in range(5, s_ref.shape[0] - 1):
        begin = jnp.where(q >= s_ref[i], jnp.maximum(begin, s_ref[i]), begin)
    k = lax.broadcasted_iota(jnp.int32, (keys, rows), 0)
    return (k >= begin) & (k <= q)


def attend(scalars, pieces, heads, kvs):
    blocks = len(pieces)
    rows, width = pieces[0].shape
    span = blocks * rows
    qw = heads * HEAD_DIM
    share = heads // kvs

    def body(s_ref, *refs):
        ins, (out_ref, lse_ref, qs, kd, vd, vt, ob) = refs[:blocks], refs[blocks:]
        me = s_ref[4]
        for k in range(blocks):
            at = pl.ds(pl.multiple_of(s_ref[k] * rows, rows), rows)
            block = ins[k][...]
            stage_heads(block, qs, at, heads, score_scale)
            for i, x in enumerate(doubled(block[:, qw : qw + 128])):
                kd[i, at, :] = x.astype(BF)
            for i, x in enumerate(doubled(block[:, qw + 128 : qw + 256])):
                vd[i, at, :] = x
        for i in range(kvs):
            vt[i] = vd[i].T.astype(BF)

        def one(h, _):
            kv = h // share
            for p in range(blocks):
                keys = (p + 1) * rows
                q = qs[h, p * rows : (p + 1) * rows, :]
                s = mm(kd[kv, :keys, :], q, NT)
                s = jnp.where(allowed_mask(s_ref, keys, rows, p * rows), s, -1e30)
                peak = jnp.max(s, axis=0, keepdims=True)
                e = jnp.exp(s - peak)
                total = jnp.sum(e, axis=0, keepdims=True)
                o = mm(vt[kv, :, :keys], e.astype(BF)) / total
                ob[h, p * rows : (p + 1) * rows, :] = o.T
                lse_ref[pl.ds(h, 1), p * rows : (p + 1) * rows] = peak + jnp.log(total)
            return 0

        lax.fori_loop(0, heads, one, 0)
        low = lower_half((rows, 128))
        for p in range(blocks):
            to = lax.rem(p - me + blocks, blocks)
            for b in range(heads // 2):
                at = slice(p * rows, (p + 1) * rows)
                out_ref[to, :, b * 128 : (b + 1) * 128] = jnp.where(
                    low, ob[2 * b, at, :], ob[2 * b + 1, at, :]
                ).astype(BF)

    pairs = heads * rows * rows * blocks * (blocks + 1) // 2
    return pl.pallas_call(
        body,
        out_shape=(
            jax.ShapeDtypeStruct((blocks, rows, qw), BF),
            jax.ShapeDtypeStruct((8, span), F32),
        ),
        in_specs=[SM] + [VM] * blocks,
        out_specs=(VM, VM),
        scratch_shapes=[
            pltpu.VMEM((heads, span, 128), BF),
            pltpu.VMEM((kvs, span, 128), BF),
            pltpu.VMEM((kvs, span, 128), F32),
            pltpu.VMEM((kvs, 128, span), BF),
            pltpu.VMEM((heads, span, 128), F32),
        ],
        compiler_params=params(),
        cost_estimate=cost(pairs * 1024, 4 * span * width, pairs),
        name="attend",
    )(scalars, *pieces)


def attend_back(scalars, pieces, grads, lse, cos, sin, heads, kvs):
    blocks = len(pieces)
    rows, width = pieces[0].shape
    span = blocks * rows
    qw = heads * HEAD_DIM
    share = heads // kvs

    def body(s_ref, *refs):
        ins, gins = refs[:blocks], refs[blocks : 2 * blocks]
        lse_ref, cos_ref, sin_ref, out_ref, qs, gs, kd, kf, kt, vd, dk, dv, dq = refs[2 * blocks :]
        me = s_ref[4]
        for k in range(blocks):
            at = pl.ds(pl.multiple_of(s_ref[k] * rows, rows), rows)
            block = ins[k][...]
            stage_heads(block, qs, at, heads, score_scale)
            for i, x in enumerate(doubled(block[:, qw : qw + 128])):
                kd[i, at, :] = x.astype(BF)
                kf[i, at, :] = x
            for i, x in enumerate(doubled(block[:, qw + 128 : qw + 256])):
                vd[i, at, :] = x.astype(BF)
            at = pl.ds(pl.multiple_of(lax.rem(me + k, blocks) * rows, rows), rows)
            stage_heads(gins[k][...], gs, at, heads, 1.0)
        for i in range(kvs):
            kt[i] = kf[i].T.astype(BF)
        dk[...] = jnp.zeros_like(dk)
        dv[...] = jnp.zeros_like(dv)

        def one(h, _):
            kv = h // share
            for p in range(blocks):
                keys = (p + 1) * rows
                at = slice(p * rows, (p + 1) * rows)
                q = qs[h, at, :]
                g = gs[h, at, :]
                s = mm(kd[kv, :keys, :], q, NT)
                log_total = lse_ref[pl.ds(h, 1), at]
                chances = jnp.where(
                    allowed_mask(s_ref, keys, rows, p * rows), jnp.exp(s - log_total), 0.0
                )
                gp = mm(vd[kv, :keys, :], g, NT)
                row_dot = jnp.sum(chances * gp, axis=0, keepdims=True)
                ds = (chances * (gp - row_dot)).astype(BF)
                dq[h, at, :] = mm(kt[kv, :, :keys], ds).T
                dk[kv, :keys, :] += mm(ds, q)
                dv[kv, :keys, :] += mm(chances.astype(BF), g)
            return 0

        lax.fori_loop(0, heads, one, 0)
        low = lower_half((rows, 128))
        for p in range(blocks):
            at = slice(p * rows, (p + 1) * rows)
            cosine, sine = cos_ref[at, :], -sin_ref[at, :]
            for b in range(heads // 2):
                x = jnp.where(low, dq[2 * b, at, :], dq[2 * b + 1, at, :]) * score_scale
                out_ref[at, b * 128 : (b + 1) * 128] = turn(x, cosine, sine).astype(BF)
            k0, k1, v0, v1 = dk[0, at, :], dk[1, at, :], dv[0, at, :], dv[1, at, :]
            k0, k1 = k0 + pltpu.roll(k0, 64, 1), k1 + pltpu.roll(k1, 64, 1)
            v0, v1 = v0 + pltpu.roll(v0, 64, 1), v1 + pltpu.roll(v1, 64, 1)
            out_ref[at, qw : qw + 128] = turn(jnp.where(low, k0, k1), cosine, sine).astype(BF)
            out_ref[at, qw + 128 : qw + 256] = jnp.where(low, v0, v1).astype(BF)

    pairs = heads * rows * rows * blocks * (blocks + 1) // 2
    return pl.pallas_call(
        body,
        out_shape=jax.ShapeDtypeStruct((span, width), BF),
        in_specs=[SM] + [VM] * (2 * blocks + 3),
        out_specs=VM,
        scratch_shapes=[
            pltpu.VMEM((heads, span, 128), BF),
            pltpu.VMEM((heads, span, 128), BF),
            pltpu.VMEM((kvs, span, 128), BF),
            pltpu.VMEM((kvs, span, 128), F32),
            pltpu.VMEM((kvs, 128, span), BF),
            pltpu.VMEM((kvs, span, 128), BF),
            pltpu.VMEM((kvs, span, 128), F32),
            pltpu.VMEM((kvs, span, 128), F32),
            pltpu.VMEM((heads, span, 128), F32),
        ],
        compiler_params=params(),
        cost_estimate=cost(pairs * 2560, 8 * span * width, pairs),
        name="attend_back",
    )(scalars, *pieces, *grads, lse, cos, sin)


def join(scalars, mixes, w_out, tok, gain):
    blocks = len(mixes)
    rows, part = mixes[0].shape
    d = tok.shape[1]

    def body(s_ref, *refs):
        ins, (w_ref, tok_ref, gain_ref, mid_ref, hid_ref) = refs[:blocks], refs[blocks:]
        me = s_ref[4]
        branch = jnp.zeros((rows, d), F32)
        for k in range(blocks):
            at = pl.ds(pl.multiple_of(lax.rem(me - k + blocks, blocks) * part, part), part)
            branch = branch + mm(ins[k][...], w_ref[at, :])
        middle = tok_ref[...].astype(F32) + residual_scale * branch
        mid_ref[...] = middle
        hid_ref[...] = (middle * rms(middle) * gain_ref[...]).astype(BF)

    return pl.pallas_call(
        body,
        out_shape=(jax.ShapeDtypeStruct((rows, d), F32), jax.ShapeDtypeStruct((rows, d), BF)),
        in_specs=[SM] + [VM] * (blocks + 3),
        out_specs=(VM, VM),
        compiler_params=params(),
        cost_estimate=cost(2 * rows * d * d, 2 * d * d + 10 * rows * d),
        name="join",
    )(scalars, *mixes, w_out, tok, gain)


def join_back(scalars, addends, middle, cot, gain, w_out):
    blocks = 4
    rows, d = middle.shape
    part = d // blocks

    def body(s_ref, a_ref, b_ref, c_ref, mid_ref, cot_ref, gain_ref, w_ref, gmid_ref, gmix_ref, br_ref, gg_ref):
        me = s_ref[4]
        grad_hidden = a_ref[...].astype(F32) + b_ref[...].astype(F32) + c_ref[...].astype(F32)
        middle = mid_ref[...]
        inv = rms(middle)
        normal = middle * inv
        gg_ref[...] = jnp.sum(grad_hidden * normal, axis=0, keepdims=True)
        u = grad_hidden * gain_ref[...]
        grad_middle = cot_ref[...] + inv * (u - normal * jnp.mean(u * normal, axis=-1, keepdims=True))
        gmid_ref[...] = grad_middle
        br_ref[...] = (residual_scale * grad_middle).astype(BF)
        for k in range(blocks):
            at = pl.ds(pl.multiple_of(lax.rem(me - k + blocks, blocks) * part, part), part)
            gmix_ref[k] = mm(br_ref[...], w_ref[at, :], NT).astype(BF)

    return pl.pallas_call(
        body,
        out_shape=(
            jax.ShapeDtypeStruct((rows, d), F32),
            jax.ShapeDtypeStruct((blocks, rows, part), BF),
            jax.ShapeDtypeStruct((rows, d), BF),
            jax.ShapeDtypeStruct((1, d), F32),
        ),
        in_specs=[SM] + [VM] * 7,
        out_specs=(VM, VM, VM, VM),
        compiler_params=params(),
        cost_estimate=cost(2 * rows * d * d, 2 * d * d + 18 * rows * d),
        name="join_back",
    )(scalars, *addends, middle, cot, gain, w_out)


def join_weights(scalars, here, branch, mixes, nd, ne):
    blocks = len(mixes)
    rows, part = mixes[0].shape
    d = branch.shape[1]
    w_rows = d // (nd * blocks * ne)

    def body(s_ref, here_ref, br_ref, *refs):
        ins, (gwa_ref, gwb_ref) = refs[:blocks], refs[blocks:]
        me = s_ref[4]
        for k in range(blocks):
            gw = mm(ins[k][...], br_ref[...], TN)
            for i in range(part // w_rows):
                q = lax.rem(me - k + blocks, blocks) * (part // w_rows) + i
                e = swapped(jnp.bitwise_xor(lax.rem(q, ne), here_ref[3]))
                b = lax.div(q, ne)
                m = lax.rem(lax.div(b, blocks) - here_ref[0] + nd, nd)
                put = gw[i * w_rows : (i + 1) * w_rows, :].astype(BF)
                split_store(gwa_ref, gwb_ref, e, (m, lax.rem(b, blocks)), put)

    return pl.pallas_call(
        body,
        out_shape=(jax.ShapeDtypeStruct((2, nd, blocks, w_rows, d), BF),) * 2,
        in_specs=[SM, SM] + [VM] * (1 + blocks),
        out_specs=(VM, VM),
        compiler_params=params(),
        cost_estimate=cost(2 * rows * d * d, 2 * d * d + 4 * rows * d),
        name="join_weights",
    )(scalars, here, branch, *mixes)


def halves(w, odd, devices):
    n, r, width = w.shape
    unit = FF // devices
    if 2 * unit != 128:
        parts = w.reshape(n, r, 2, devices // 4, 2, 2, unit)
        parts = jnp.transpose(parts, (5, 0, 1, 2, 3, 4, 6)).reshape(2, n, r, FF)
        return pick(parts, odd), pick(parts, 1 - odd)

    def body(odd_ref, w_ref, mine_ref, their_ref):
        low = lower_half((r, 128))
        even = odd_ref[0] == 0
        for m in range(width // 256):
            a = w_ref[0, :, 2 * m * 128 : (2 * m + 1) * 128].astype(F32)
            b = w_ref[0, :, (2 * m + 1) * 128 : (2 * m + 2) * 128].astype(F32)
            evens = jnp.where(low, a, pltpu.roll(b, 64, 1))
            odds = jnp.where(low, pltpu.roll(a, 64, 1), b)
            at = slice(m * 128, (m + 1) * 128)
            mine_ref[0, :, at] = jnp.where(even, evens, odds).astype(BF)
            their_ref[0, :, at] = jnp.where(even, odds, evens).astype(BF)

    spec = pl.BlockSpec((1, r, FF), lambda e: (e, 0, 0))
    return pl.pallas_call(
        body,
        grid=(n,),
        out_shape=(jax.ShapeDtypeStruct((n, r, FF), BF),) * 2,
        in_specs=[SM, pl.BlockSpec((1, r, width), lambda e: (e, 0, 0))],
        out_specs=(spec, spec),
        compiler_params=params(),
        cost_estimate=cost(0, 4 * n * r * width),
        name="halves",
    )(odd[None].astype(jnp.int32), w)


def whole(parts, odd, devices):
    count = len(parts)
    _, r, width = parts[0][0].shape
    r3 = r // 3
    unit = FF // devices

    def plain(own, other, theirs):
        total = own.astype(F32) + other.astype(F32)
        theirs = theirs.astype(F32)
        pair = jnp.stack([jnp.where(odd == 0, total[0], theirs), jnp.where(odd == 0, theirs, total[0])])
        pair = pair.reshape(2, r, 2, devices // 4, 2, unit)
        down = [total[2, b * r3 : (b + 1) * r3] for b in range(3)]
        return jnp.transpose(pair, (1, 2, 3, 4, 0, 5)).reshape(r, 2 * width), jnp.concatenate(down, axis=1)

    if 2 * unit != 128:
        done = [plain(*p) for p in parts]
        return jnp.stack([p[0] for p in done]), jnp.stack([p[1] for p in done])

    def body(odd_ref, own_ref, other_ref, their_ref, *refs):
        in_ref, down_ref = refs[-2], refs[-1]
        low = lower_half((r, 128))
        even = odd_ref[0] == 0
        for m in range(width // 128):
            at = slice(m * 128, (m + 1) * 128)
            mine = own_ref[0, :, at].astype(F32) + other_ref[0, :, at].astype(F32)
            their = their_ref[:, at].astype(F32)
            evens, odds = jnp.where(even, mine, their), jnp.where(even, their, mine)
            in_ref[0, :, 2 * m * 128 : (2 * m + 1) * 128] = jnp.where(low, evens, pltpu.roll(odds, 64, 1))
            in_ref[0, :, (2 * m + 1) * 128 : (2 * m + 2) * 128] = jnp.where(
                low, pltpu.roll(evens, 64, 1), odds
            )
        for b in range(3):
            at = slice(b * r3, (b + 1) * r3)
            down_ref[0, :, b * width : (b + 1) * width] = (
                own_ref[2, at, :].astype(F32) + other_ref[2, at, :].astype(F32)
            )

    done = ()
    for e, (own, other, theirs) in enumerate(parts):
        fixed = lambda *shape: pl.BlockSpec(shape, lambda i: (0,) * len(shape))
        done = pl.pallas_call(
            body,
            grid=(1,),
            out_shape=(
                jax.ShapeDtypeStruct((count, r, 2 * width), F32),
                jax.ShapeDtypeStruct((count, r3, 3 * width), F32),
            ),
            in_specs=[SM, fixed(3, r, width), fixed(3, r, width), fixed(r, width)] + [ANY] * len(done),
            out_specs=(
                pl.BlockSpec((1, r, 2 * width), lambda i, e=e: (e, 0, 0)),
                pl.BlockSpec((1, r3, 3 * width), lambda i, e=e: (e, 0, 0)),
            ),
            input_output_aliases={4: 0, 5: 1} if done else {},
            compiler_params=params(),
            cost_estimate=cost(0, 20 * r * width),
            name="whole",
        )(odd[None].astype(jnp.int32), own, other, theirs, *done)
    return done


def experts_rows(places, which, rows_in, cots, shards, sums, last):
    piece, d = rows_in[0].shape
    group = 2
    rows = piece * group
    tiles = len(rows_in) // group
    total = rows * tiles
    count, n = len(shards), len(shards[0])
    r, width = shards[0][0][0].shape[-2:]
    arrays = {id(t): t for shard in shards for t, _ in shard}
    slot = {key: k for k, key in enumerate(arrays)}
    arrays = list(arrays.values())
    half = width // 2
    r3 = r // 3
    first = sums is None

    def body(places_ref, *refs):
        n_in = tiles * group
        h_refs, c_refs, refs = refs[:n_in], refs[n_in : 2 * n_in], refs[2 * n_in :]
        w_refs, refs = refs[: len(arrays)], refs[len(arrays) :]
        if not first:
            in_h, in_o, refs = refs[0], refs[1], refs[2:]
        if last:
            out_h, rest_h, out_o, rest_o, gb_ref, gat_ref, *refs = refs
        else:
            out_h, out_o, gb_ref, gat_ref, *refs = refs
        if first:
            ht_ref, *refs = refs
        wiv, wdv, ga_ref, hv, cv, sems, row_sems = refs
        t = pl.program_id(0)
        moves = []
        for i in range(n_in):
            at = pl.ds(i % group * piece, piece)
            moves.append(
                (
                    pltpu.make_async_copy(h_refs[i], hv.at[i // group, at, :], row_sems.at[0, i]),
                    pltpu.make_async_copy(c_refs[i], cv.at[i // group, at, :], row_sems.at[1, i]),
                )
            )

        @pl.when(t == 0)
        def _():
            copies = []
            for i in range(count):
                for e in range(n):
                    array, which_of = shards[i][e]
                    source = w_refs[slot[id(array)]]
                    source = source if which_of is None else source.at[which_of]
                    parts = []
                    for b in range(2):
                        at = pl.multiple_of(places_ref[3 * i + b] * r, r)
                        parts.append((source.at[b], wiv.at[pl.ds(at, r), e * width : (e + 1) * width]))
                    at = pl.multiple_of(places_ref[3 * i + 2] * r3 + e * half, r3)
                    for b in range(3):
                        parts.append(
                            (
                                source.at[2, b * r3 : (b + 1) * r3, :],
                                wdv.at[pl.ds(at, r3), b * width : (b + 1) * width],
                            )
                        )
                    for k, (a, b) in enumerate(parts):
                        copies.append(pltpu.make_async_copy(a, b, sems.at[i, e, k]))
            for copy in copies:
                copy.start()
            for a, b in moves[:group]:
                a.start()
                b.start()
            for copy in copies:
                copy.wait()
            for a, b in moves[group:]:
                a.start()
                b.start()

        for i in range(tiles):

            @pl.when(t == i)
            def _():
                for a, b in moves[i * group : (i + 1) * group]:
                    a.wait()
                    b.wait()

        h = hv[t]
        c = cv[t, :, :d]
        gates = cv[t, :, d:].astype(F32)
        lane = lax.broadcasted_iota(jnp.int32, gates.shape, 1) - places_ref[3 * count]
        for e in range(n):
            g = jnp.sum(jnp.where(lane == which + e, gates, 0.0), axis=1, keepdims=True)
            gu = mm(h, wiv[:, e * width : (e + 1) * width])
            gate, up = gu[:, :half], gu[:, half:]
            sg = jax.nn.sigmoid(gate)
            silu = gate * sg
            ga = mm(c, wdv[e * half : (e + 1) * half, :], NT) * g
            ga_ref[:, e * half : (e + 1) * half] = (silu * up * g).astype(BF)
            gb_ref[:, e * width : e * width + half] = (ga * up * (sg + silu * (1.0 - sg))).astype(BF)
            gb_ref[:, e * width + half : (e + 1) * width] = (ga * silu).astype(BF)
        o = mm(ga_ref[...], wdv[...])
        gh = mm(gb_ref[...], wiv[...], NT)
        gat_ref[...] = ga_ref[...].T
        if first:
            ht_ref[...] = h.T
        if not first:
            o = o + in_o[...].astype(F32)
            gh = gh + in_h[...].astype(F32)
        if last:

            @pl.when(t < tiles // 2)
            def _():
                out_o[...] = o.astype(BF)
                out_h[...] = gh.astype(BF)

            @pl.when(t >= tiles // 2)
            def _():
                rest_o[...] = o.astype(BF)
                rest_h[...] = gh.astype(BF)

        else:
            out_o[...] = o.astype(BF)
            out_h[...] = gh.astype(BF)

    tile = lambda c: pl.BlockSpec((rows, c), lambda t: (t, 0))
    flat = lambda c: pl.BlockSpec((c, rows), lambda t: (0, t))
    if last:
        sum_shapes = (jax.ShapeDtypeStruct((total // 2, d), BF),) * 4
        front = pl.BlockSpec((rows, d), lambda t: (jnp.minimum(t, tiles // 2 - 1), 0))
        back = pl.BlockSpec((rows, d), lambda t: (jnp.maximum(t - tiles // 2, 0), 0))
        sum_specs = (front, back, front, back)
    else:
        sum_shapes = (jax.ShapeDtypeStruct((total, d), BF),) * 2
        sum_specs = (tile(d), tile(d))
    return pl.pallas_call(
        body,
        grid=(tiles,),
        out_shape=sum_shapes
        + (
            jax.ShapeDtypeStruct((total, n * width), BF),
            jax.ShapeDtypeStruct((n * half, total), BF),
        )
        + ((jax.ShapeDtypeStruct((d, total), BF),) if first else ()),
        in_specs=[SM]
        + [ANY] * (2 * len(rows_in) + len(arrays))
        + ([] if first else [tile(d), tile(d)]),
        out_specs=sum_specs + (tile(n * width), flat(n * half)) + ((flat(d),) if first else ()),
        scratch_shapes=[
            pltpu.VMEM((d, n * width), BF),
            pltpu.VMEM((n * half, d), BF),
            pltpu.VMEM((rows, n * half), BF),
            pltpu.VMEM((tiles, rows, d), BF),
            pltpu.VMEM((tiles, rows, cots[0].shape[1]), BF),
            pltpu.SemaphoreType.DMA((count, n, 5)),
            pltpu.SemaphoreType.DMA((2, len(rows_in))),
        ],
        compiler_params=params(),
        cost_estimate=cost(6 * n * total * d * width, 50e6, n * total * half),
        name="experts_rows",
    )(places, *rows_in, *cots, *arrays, *(() if first else sums))


def experts_weights(scalars, rows_t, cots, gb, ga_t, n, devices):
    d, total = rows_t.shape
    width, half = gb.shape[1] // n, ga_t.shape[0] // n
    r = d // devices
    r3 = r // 3
    nd = devices // 4
    tiles = len(cots)
    rows = total // tiles

    def body(s_ref, h_any, gb_any, ga_any, *refs):
        c_refs, refs = refs[:tiles], refs[tiles:]
        outs, (down, h_ref, gb_ref, ga_ref, c_ref, stage, sems, c_sems, out_sems) = refs[: n * nd], refs[n * nd :]
        ahead = [lax.rem(s_ref[0] + k, nd) for k in range(nd)]
        spans = [pl.ds(pl.multiple_of(x * 4 * r, 4 * r), 4 * r) for x in ahead]
        first = [pltpu.make_async_copy(gb_any, gb_ref, sems.at[0])]
        first += [
            pltpu.make_async_copy(h_any.at[spans[k], :], h_ref.at[k], sems.at[1 + k]) for k in range(nd)
        ]
        second = [pltpu.make_async_copy(ga_any, ga_ref, c_sems.at[tiles])]
        second += [
            pltpu.make_async_copy(c_refs[i].at[:, :d], c_ref.at[pl.ds(i * rows, rows), :], c_sems.at[i])
            for i in range(tiles)
        ]
        for copy in first[:2]:
            copy.start()
        first[0].wait()
        for k in range(nd):
            first[1 + k].wait()
            for copy in first[2:] + second if k == 0 else []:
                copy.start()
            part = mm(h_ref[k], gb_ref[...]).astype(BF)
            for z in range(4):
                where = jnp.bitwise_xor(s_ref[2], z // 2)
                slot = jnp.bitwise_xor(s_ref[1], z % 2)
                for e in range(n):
                    stage[e * nd + k, where, slot] = part[z * r : (z + 1) * r, e * width : (e + 1) * width]
        for copy in second:
            copy.wait()
        leaving = []
        for e in range(n):
            down[...] = mm(ga_ref[e * half : (e + 1) * half, :], c_ref[...]).astype(BF)
            for k in range(nd):
                for z in range(2):
                    where = jnp.bitwise_xor(s_ref[2], z)
                    at = pl.ds(pl.multiple_of((2 * ahead[k] + z) * r3, r3), r3)
                    for b in range(3):
                        stage[e * nd + k, where, 2, b * r3 : (b + 1) * r3, :] = down[
                            at, b * width : (b + 1) * width
                        ]
                leaving.append(
                    pltpu.make_async_copy(stage.at[e * nd + k], outs[e * nd + k], out_sems.at[e * nd + k])
                )
                leaving[-1].start()
        for copy in leaving:
            copy.wait()

    outs = pl.pallas_call(
        body,
        out_shape=[jax.ShapeDtypeStruct((2, 3, r, width), BF)] * (n * nd),
        in_specs=[SM] + [ANY] * (3 + tiles),
        out_specs=[ANY] * (n * nd),
        scratch_shapes=[
            pltpu.VMEM((half, d), BF),
            pltpu.VMEM((nd, 4 * r, total), BF),
            pltpu.VMEM((total, n * width), BF),
            pltpu.VMEM((n * half, total), BF),
            pltpu.VMEM((total, d), BF),
            pltpu.VMEM((n * nd, 2, 3, r, width), BF),
            pltpu.SemaphoreType.DMA((1 + nd,)),
            pltpu.SemaphoreType.DMA((tiles + 1,)),
            pltpu.SemaphoreType.DMA((n * nd,)),
        ],
        compiler_params=params(),
        cost_estimate=cost(3 * n * total * d * width, 20e6),
        name="experts_weights",
    )(scalars, rows_t, gb, ga_t, *cots)
    return [outs[e * nd : (e + 1) * nd] for e in range(n)]


def finish(dqkv, w, blocks):
    total, width = dqkv.shape
    d = w.shape[0]
    rows = total // blocks

    def body(dq_ref, w_ref, gn_ref):
        gn_ref[0] = mm(dq_ref[...], w_ref[...], NT).astype(BF)

    return pl.pallas_call(
        body,
        grid=(blocks,),
        out_shape=jax.ShapeDtypeStruct((blocks, rows, d), BF),
        in_specs=[pl.BlockSpec((rows, width), lambda t: (t, 0)), pl.BlockSpec((d, width), lambda t: (0, 0))],
        out_specs=pl.BlockSpec((1, rows, d), lambda t: (t, 0, 0)),
        compiler_params=params(),
        cost_estimate=cost(2 * total * d * width, 4 * total * d),
        name="finish",
    )(dqkv, w)


def finish_weights(scalars, here, dqkv, gn, toks, gain, gain_grad, nd, ne):
    blocks = len(toks)
    rows, d = toks[0].shape
    width = dqkv.shape[1]
    w_rows = d // (nd * blocks * ne)

    def body(s_ref, here_ref, dq_ref, gn_ref, gain_ref, gg_ref, *refs):
        ins, (gwa_ref, gwb_ref, acc) = refs[:blocks], refs[blocks:]
        gg = jnp.zeros((1, d), F32)
        for k in range(blocks):
            to = s_ref[k]
            at = pl.ds(pl.multiple_of(to * rows, rows), rows)
            t = ins[k][...].astype(F32)
            normal = t * rms(t)
            normed = (normal * gain_ref[...]).astype(BF)
            gg = gg + jnp.sum(gn_ref[to].astype(F32) * normal, axis=0, keepdims=True)
            part = mm(normed, dq_ref[at, :], TN)
            acc[...] = part if k == 0 else acc[...] + part
        row = lax.broadcasted_iota(jnp.int32, (128, d), 0)
        both = jnp.where(row == 0, gg, jnp.where(row == 1, gg_ref[...], 0.0)).T
        for q in range(d // w_rows):
            e = swapped(jnp.bitwise_xor(q % ne, here_ref[3]))
            m = lax.rem(q // ne // blocks - here_ref[0] + nd, nd)
            at = slice(q * w_rows, (q + 1) * w_rows)
            put = jnp.concatenate([acc[at, :], both[at, :]], axis=1).astype(BF)
            split_store(gwa_ref, gwb_ref, e, (m, q // ne % blocks), put)

    return pl.pallas_call(
        body,
        out_shape=(jax.ShapeDtypeStruct((2, nd, blocks, w_rows, width + 128), BF),) * 2,
        in_specs=[SM, SM] + [VM] * (4 + blocks),
        out_specs=(VM, VM),
        scratch_shapes=[pltpu.VMEM((d, width), F32)],
        compiler_params=params(),
        cost_estimate=cost(2 * blocks * rows * d * width, 6 * blocks * rows * d),
        name="finish_weights",
    )(scalars, here, dqkv, gn, gain, gain_grad, *toks)


def per_device(
    tokens,
    gain_attn,
    w_query,
    w_key,
    w_value,
    w_out,
    gain_moe,
    w_in,
    w_down,
    routes,
    gates,
    lengths,
    cotangent,
):
    nd, nz, ne = lax.axis_size("dp"), lax.axis_size("ctx"), lax.axis_size("exp")
    x, z, j = lax.axis_index("dp"), lax.axis_index("ctx"), lax.axis_index("exp")
    rows, d = tokens.shape[1:]
    span = rows * nz
    w_rows = w_query.shape[0]
    heads, kvs = HEADS // nz, KV_HEADS // nz
    qw, kw = heads * HEAD_DIM, kvs * HEAD_DIM
    local_experts = w_in.shape[0]
    experts = local_experts * ne
    i32 = jnp.int32
    mod = lambda v, n: lax.rem(v + 8 * n, n)

    ends = jnp.cumsum(lengths[0]).astype(i32)
    places = [mod(z - k, nz) for k in range(nz)]
    scalars = jnp.concatenate([jnp.stack(places + [z]).astype(i32), ends])
    place = jnp.arange(span, dtype=i32)
    place = place - jnp.max(jnp.where(place[:, None] >= ends[None, :-1], ends[None, :-1], 0), axis=1)
    lane = jnp.arange(128, dtype=i32)
    half = HEAD_DIM // 2
    frequency = rope_base ** (-2.0 * jnp.arange(half, dtype=F32) / HEAD_DIM)
    angles = place.astype(F32)[:, None] * frequency[None, :]
    cos = jnp.tile(jnp.cos(angles), (1, 128 // half))
    sin = jnp.tile(jnp.sin(angles), (1, 128 // half)) * jnp.where((lane & 63) < 32, -1.0, 1.0)[None, :]

    run = Stages(gain_attn)
    gain_a, gain_m = gain_attn[None, :], gain_moe[None, :]
    devices = nd * nz
    odd, zh = jnp.bitwise_and(z, 1), z // 2
    batch = local_experts // 2
    tok, cot = tokens[0], cotangent[0]
    flip_e = lambda v, e: flip(v, "exp", e)

    def row_blocks(found, owners, order):
        at = [
            (mod(x - m, nd) * nz + p) * ne + jnp.bitwise_xor(j, e + 2 * b)
            for e in (0, 1) for b, m in order for p in owners
        ]
        return assemble(found, jnp.stack(at).astype(i32))

    by_m = [(b, m) for m in range(nd) for b in (0, 1)]
    by_b = [(b, m) for b in (0, 1) for m in range(nd)]

    here = jnp.stack([x, odd, zh, j]).astype(i32)

    parts = [
        jnp.concatenate(
            [
                w_query[:, p * qw : (p + 1) * qw],
                w_key[:, p * kw : (p + 1) * kw],
                w_value[:, p * kw : (p + 1) * kw],
            ],
            axis=1,
        )
        for p in range(nz)
    ]
    cut = rows // 2
    toks = [tok, shift(tok, "ctx", 1)]
    w_parts = jnp.stack(parts)
    w_mine = [pick(w_parts, z)] + [shift(pick(w_parts, mod(z + k, nz)), "ctx", k) for k in range(1, nz)]
    run.end(toks, w_mine)

    half_2 = [shift(run.hold(toks[1])[:cut], "ctx", 1)]
    mine_in, their_in = halves(run.hold(w_in), odd, devices)
    down = run.hold(w_down)
    down = jnp.concatenate([down[:, :, b * FF : (b + 1) * FF] for b in range(d // FF)], axis=1)
    w_mine = jnp.stack(w_mine)
    w_mine = jnp.stack([w_mine, flip_e(run.hold(w_mine), 2)])
    line = [hop(run.hold(w_out), pairs) for pairs in (ACROSS, UP, DOWN)]
    run.end(half_2, w_mine, line, mine_in)

    half_2.append(shift(run.hold(toks[1])[cut:], "ctx", 1))
    hits = run.hold(routes)[0][:, :, None] == jnp.arange(128, dtype=i32)[None, None, :]
    dense = jnp.sum(jnp.where(hits, gates[0].astype(F32)[:, :, None], 0.0), axis=1).astype(BF)
    cot_b = jnp.concatenate([(residual_scale * run.hold(cot)).astype(BF), dense], axis=1)
    w_found = ring(run.hold(w_mine), "dp")
    line_end = hop(run.hold(line[0]), OUTER)
    run.end(half_2, w_found, line_end, cot_b)

    toks.append(jnp.concatenate(half_2))
    toks.append(shift(run.hold(toks[2]), "ctx", 1))
    got_1 = flip(run.hold(their_in[:batch]), "ctx", 1)
    w_found = w_found + [flip_e(t, 1) for t in run.hold(w_found)]
    w_line = ring(run.hold(jnp.stack(line_gather(*line, line_end, w_out))), "dp")
    cot_2 = flip_e(run.hold(cot_b), 2)
    w_qkv = row_blocks(w_found, places, by_m)
    at = jnp.stack(places).astype(i32)
    pieces = project(toks[: nz - 1], gain_a, w_qkv, cos, sin, at[: nz - 1])
    run.end(toks, pieces, got_1, w_line, cot_2)

    packet = lambda e, got: jnp.stack([mine_in[e], got[e % batch], down[e]])
    near = [packet(e, got_1) for e in range(batch)]
    far = [flip(run.hold(near[0]), "ctx", 2)]
    own = [ring(run.hold(jnp.stack(near)), "dp")]
    w_line = jnp.stack(w_line)
    w_line = jnp.stack([w_line, flip_e(run.hold(w_line), 2)])
    cot_n = flip(run.hold(cot_b), "ctx", 1)
    pieces = pieces + project([run.hold(toks[3])], gain_a, w_qkv, cos, sin, at[nz - 1 :])
    mix_out, lse = attend(scalars, pieces, heads, kvs)
    run.end(far, own, w_line, cot_n, mix_out)

    mixes = run.hold([mix_out[k] for k in range(nz)])
    mixes = [mixes[0]] + [shift(mixes[k], "ctx", k) for k in range(1, nz)]
    w_line = [w_line, flip_e(run.hold(w_line), 1)]
    cot_n2 = flip_e(run.hold(cot_n), 2)
    w_out_all = row_blocks(w_line, line_places(z), by_b)
    run.end(mixes, w_out_all, cot_n2)

    cot_1, cot_3 = flip_e(run.hold(cot_b), 1), flip_e(run.hold(cot_2), 1)
    cot_n1, cot_n3 = flip_e(run.hold(cot_n), 1), flip_e(run.hold(cot_n2), 1)
    got_2 = flip(run.hold(their_in[batch:]), "ctx", 1)
    middle, hidden = join(scalars, run.hold(mixes), w_out_all, tok, gain_m)
    run.end(hidden, got_2, cot_1, cot_3, cot_n1, cot_n3)

    hidden_2, hidden_n = flip_e(run.hold(hidden), 2), flip(run.hold(hidden), "ctx", 1)
    far += [flip(run.hold(near[e]), "ctx", 2) for e in range(1, batch)]
    near += [packet(e, got_2) for e in range(batch, local_experts)]
    own.append(ring(run.hold(jnp.stack(near[batch:])), "dp"))
    hidden_1 = flip_e(run.hold(hidden), 1)
    run.end(hidden_1, hidden_2, hidden_n, far, own)

    hidden_n2 = flip_e(run.hold(hidden_n), 2)
    hidden_n1, hidden_3 = flip_e(run.hold(hidden_n), 1), flip_e(run.hold(hidden_2), 1)
    over = [ring(run.hold(jnp.stack(far)), "dp")]
    far.append(flip(run.hold(near[batch]), "ctx", 2))
    run.end(hidden_n1, hidden_3, hidden_n2, over, far)

    rows_in = [hidden, hidden_n, hidden_2, hidden_n2, hidden_1, hidden_n1, hidden_3, None]
    cots = [cot_b, cot_n, cot_2, cot_n2, cot_1, cot_n1, cot_3, cot_n3]
    w_at = []
    for zc in (z, jnp.bitwise_xor(z, 2)):
        for m in range(nd):
            xc = mod(x - m, nd)
            w_at += [xc * nz + zc, xc * nz + jnp.bitwise_xor(zc, 1), xc * 2 + zc // 2]
    w_at = jnp.stack(w_at + [j * local_experts]).astype(i32)
    rows_in = run.hold(rows_in[:-1]) + [flip_e(run.hold(hidden_n2), 1)]
    far += [flip(run.hold(near[e]), "ctx", 2) for e in range(batch + 1, local_experts)]
    over.append(ring(run.hold(far[batch]), "dp"))
    shards = [[(t, e) for e in range(batch)] for t in own[0] + over[0]]
    sum_h, sum_o, gb, ga_t, rows_t = experts_rows(w_at, 0, rows_in, cots, shards, None, False)
    run.end(far, over, sum_h)

    over += [ring(run.hold(far[e]), "dp") for e in range(batch + 1, local_experts)]
    gw_1 = experts_weights(here, rows_t, cots, run.hold(gb), ga_t, batch, devices)
    run.end(over, gw_1)

    x_0 = dp_reduce_pair(run.hold(gw_1[0]))
    shards = [[(t, e) for e in range(batch)] for t in own[1]]
    shards += [[(t, None) for t in pair] for pair in zip(*over[1:])]
    sum_h, rest_h, sum_o, rest_o, gb, ga_t = experts_rows(
        w_at, batch, run.hold(rows_in), cots, shards, (sum_h, sum_o), True
    )
    run.end(x_0, sum_h)

    rest_h = flip_e(run.hold(rest_h), 1)
    run.end(rest_h)

    part = rows // 2
    sum_h = [
        add(sum_h[a * part : b * part], rest_h[a * part : b * part])
        for a, b in ((0, 2), (2, 3), (3, 4), (4, 5), (5, 6), (6, 7), (7, 8))
    ]
    by_y, by_z = flip_e(run.hold(sum_h[5]), 2), flip(run.hold(sum_h[6]), "ctx", 1)
    z_0 = flip(run.hold(x_0[1]), "ctx", 2)
    x_1 = dp_reduce_pair(run.hold(gw_1[1]))
    rest_o = flip_e(run.hold(rest_o), 1)
    gw_2 = experts_weights(here, rows_t, cots, run.hold(gb), ga_t, batch, devices)
    run.end(by_y, by_z, z_0, x_1, rest_o, gw_2)

    near_h = flip_e(jnp.concatenate([sum_h[3], add(run.hold(sum_h[4]), by_z)]), 2)
    other_h = flip(jnp.concatenate([add(run.hold(sum_h[1]), by_y), sum_h[2]]), "ctx", 1)
    z_1 = flip(run.hold(x_1[1]), "ctx", 2)
    x_2 = dp_reduce_pair(run.hold(gw_2[0]))
    sum_o = [add(sum_o[a * rows : (a + 1) * rows], rest_o[a * rows : (a + 1) * rows]) for a in range(4)]
    run.end(near_h, other_h, z_1, x_2, sum_o)

    grad_middle, grad_mix, branch, grad_gain_m = join_back(
        scalars, [sum_h[0], *run.hold([near_h, other_h])], middle, cot, gain_m, w_out_all
    )
    grad_mixes = [grad_mix[0]] + [shift(grad_mix[k], "ctx", -k) for k in range(1, nz)]
    x_3 = dp_reduce_pair(run.hold(gw_2[1]))
    far_o1 = flip_e(run.hold(sum_o[3]), 2)
    wo_a, wo_b = join_weights(scalars, here, branch, mixes, nd, ne)
    run.end(grad_mixes, x_3, far_o1, wo_b)

    z_2 = flip(run.hold(x_2[1]), "ctx", 2)
    far_o = flip_e(run.hold(sum_o[2]), 2)
    other_o = flip(add(sum_o[1], run.hold(far_o1)), "ctx", 1)
    wo_b = flip_e(run.hold(wo_b), 1)
    dqkv = attend_back(scalars, pieces, run.hold(grad_mixes), lse, cos, sin, heads, kvs)
    grad_normed = finish(dqkv, w_qkv, nz)
    run.end(z_2, far_o, other_o, wo_b, grad_normed)

    z_3 = flip(run.hold(x_3[1]), "ctx", 2)
    gw_a, gw_b = finish_weights(scalars, here, dqkv, run.hold(grad_normed), toks, gain_a, grad_gain_m, nd, ne)
    x_held = run.hold([x_0[0], x_1[0], x_2[0]])
    swap = flip(jnp.stack([add(t[1], u[1]) for t, u in zip(x_held, (z_0, z_1, z_2))]), "ctx", 1)
    wo = add(wo_a, lax.optimization_barrier((wo_b, gw_b))[0])
    run.end(gw_b, swap, wo, z_3)

    tail = run.hold(grad_normed)
    total = shift(pick(tail, mod(z - 1, nz)), "ctx", 1)
    gw_b = flip_e(run.hold(gw_b), 1)
    wo_far = flip_e(run.hold(wo[1]), 2)
    swap_3 = flip(add(run.hold(x_3[0])[1], z_3[1]), "ctx", 1)
    gw = add(gw_a, gw_b)
    run.end(total, gw, wo_far, swap_3)

    total = shift(add(total, pick(run.hold(tail), mod(z - 2, nz))), "ctx", 1)
    gw_far = flip_e(run.hold(gw[1]), 2)
    wo = dp_reduce(list(run.hold(add(wo[0], wo_far))))
    run.end(total, gw_far, wo)

    total = shift(add(total, pick(run.hold(tail), mod(z - 3, nz))), "ctx", 1)
    gw = dp_reduce(list(run.hold(add(gw[0], gw_far))))
    run.end(total, gw)

    mine = jnp.concatenate(run.hold([gw, wo]), axis=2)
    parts = [pick(mine, z)] + [shift(pick(mine, mod(z + k, nz)), "ctx", k) for k in range(1, nz)]

    gn = pick(tail, z).astype(F32) + total.astype(F32)
    expert_sum = sum_o[0].astype(F32) + far_o.astype(F32) + other_o.astype(F32)
    mixed_out = (middle + residual_scale * expert_sum).astype(BF)
    q_end, k_end, v_end = qw, qw + kw, qw + 2 * kw
    gains = sum(p[:, v_end : v_end + 2].astype(F32) for p in parts)
    grad_out = sum(p[:, v_end + 128 :].astype(F32) for p in parts)
    order = jnp.stack([p[:, :v_end] for p in parts])
    order = [pick(order, mod(z - p, nz)).astype(F32) for p in range(nz)]
    grad_query = jnp.concatenate([g[:, :q_end] for g in order], axis=1)
    grad_key = jnp.concatenate([g[:, q_end:k_end] for g in order], axis=1)
    grad_value = jnp.concatenate([g[:, k_end:] for g in order], axis=1)

    grads_in, grads_down = whole(
        [
            (x_0[0], z_0, swap[0]), (x_1[0], z_1, swap[1]), (x_2[0], z_2, swap[2]), (x_3[0], z_3, swap_3)
        ],
        odd,
        devices,
    )

    t = tok.astype(F32)
    inv = rms(t)
    normal = t * inv
    u = gn * gain_a
    grad_tokens = grad_middle + inv * (u - normal * jnp.mean(u * normal, axis=-1, keepdims=True))
    return (
        mixed_out[None],
        grad_tokens[None],
        gains[:, 0],
        grad_query,
        grad_key,
        grad_value,
        grad_out.astype(F32),
        gains[:, 1],
        grads_in,
        grads_down,
    )


def solution(mesh):
    every = ("dp", "ctx", "exp")
    return jax.shard_map(
        per_device,
        mesh=mesh,
        in_specs=(
            P(("dp", "exp"), "ctx", None),
            P(),
            P(every, None),
            P(every, None),
            P(every, None),
            P(every, None),
            P(),
            P("exp", ("dp", "ctx"), None),
            P("exp", ("dp", "ctx"), None),
            P(("dp", "exp"), "ctx", None),
            P(("dp", "exp"), "ctx", None),
            P(("dp", "exp"), None),
            P(("dp", "exp"), "ctx", None),
        ),
        out_specs=(
            P(("dp", "exp"), "ctx", None),
            P(("dp", "exp"), "ctx", None),
            P(every),
            P(every, None),
            P(every, None),
            P(every, None),
            P(every, None),
            P(every),
            P("exp", ("dp", "ctx"), None),
            P("exp", ("dp", "ctx"), None),
        ),
        check_vma=False,
    )
```

```python
import functools

import jax
import jax.numpy as jnp
from jax import lax
from jax.experimental import pallas as pl
from jax.experimental.pallas import tpu as pltpu
from jax.sharding import PartitionSpec as P

HEADS = 24
KV_HEADS = 8
HEAD_DIM = 64
FF = 512
TOP = 8

eps_norm = 1e-06
score_scale = 0.015625
residual_scale = 0.22
rope_base = 10000.0

BF = jnp.bfloat16
F32 = jnp.float32
SCALE = 3
VMEM_LIMIT = 60 * 1024 * 1024
ANY = pl.BlockSpec(memory_space=pl.ANY)
VM = pl.BlockSpec(memory_space=pltpu.VMEM)
SM = pl.BlockSpec(memory_space=pltpu.SMEM)
NN = (((1,), (0,)), ((), ()))
NT = (((1,), (1,)), ((), ()))
TN = (((0,), (0,)), ((), ()))


def mm(a, b, dims=NN):
    return lax.dot_general(a, b, dims, preferred_element_type=F32)


def params(**kw):
    return pltpu.CompilerParams(vmem_limit_bytes=VMEM_LIMIT, **kw)


def cost(flops, nbytes, trans=0):
    return pl.CostEstimate(
        flops=int(flops / SCALE), bytes_accessed=int(nbytes / SCALE), transcendentals=0
    )


def shift(x, axis, by):
    n = lax.axis_size(axis)
    return lax.ppermute(x, axis, [(i, (i + by) % n) for i in range(n)])


def flip(x, axis, mask):
    n = lax.axis_size(axis)
    return lax.ppermute(x, axis, [(i, i ^ mask) for i in range(n)])


class Stages:
    def __init__(self, token):
        self.token = token

    def hold(self, x):
        leaves, tree = jax.tree.flatten(x)
        leaves = [lax.optimization_barrier((leaf, self.token))[0] for leaf in leaves]
        return jax.tree.unflatten(tree, leaves)

    def end(self, *outs):
        self.token = lax.optimization_barrier((self.token, *jax.tree.leaves(outs)))[0]


def ring(x, axis):
    out = [x]
    for _ in range(lax.axis_size(axis) - 1):
        out.append(shift(out[-1], axis, 1))
    return out


def hop(x, pairs):
    return lax.ppermute(x, "ctx", pairs)


UP, DOWN = [(0, 1), (1, 2), (2, 3)], [(1, 0), (2, 1), (3, 2)]
ACROSS = [(0, 2), (1, 3), (2, 0), (3, 1)]
INNER, OUTER = [(0, 1), (3, 2)], [(1, 0), (2, 3)]


def line_places(z):
    return [z, jnp.bitwise_xor(z, 2), jnp.where(z == 0, 3, z - 1), jnp.where(z == 3, 0, z + 1)]


def line_gather(across, below, above, end, x):
    z = lax.axis_index("ctx")
    return [x, across, jnp.where(z == 0, end, below), jnp.where(z == 3, end, above)]


def add(a, b):
    return (a.astype(F32) + b.astype(F32)).astype(BF)


def pick(x, index, dim=0):
    return lax.dynamic_index_in_dim(x, index, dim, False)


def dp_reduce(parts):
    n = lax.axis_size("dp")
    total = parts[n - 1]
    for k in range(1, n):
        total = add(shift(total, "dp", 1), parts[n - 1 - k])
    return total


def dp_reduce_pair(parts):
    n = lax.axis_size("dp")
    total = parts[n - 1]
    for k in range(1, n - 1):
        total = add(shift(total, "dp", 1), parts[n - 1 - k])
    if n == 1:
        return [total[0], total[1]]
    total = shift(total, "dp", 1)
    return [add(total[0], parts[0][0]), add(total[1], parts[0][1])]


def assemble(found, places):
    found = [t.reshape(-1, *t.shape[-2:]) for t in found]
    each, rows, width = found[0].shape
    count = each * len(found)
    total = count * rows
    if rows % 16:
        blocks = jnp.concatenate(found)
        return jnp.zeros_like(blocks).at[places].set(blocks).reshape(total, width)

    def body(places_ref, *refs):
        refs, out_ref, sems = refs[:-2], refs[-2], refs[-1]
        copies = []
        for i in range(count):
            at = pl.multiple_of(places_ref[i] * rows, rows)
            copies.append(
                pltpu.make_async_copy(refs[i // each].at[i % each], out_ref.at[pl.ds(at, rows), :], sems.at[i])
            )
        for copy in copies:
            copy.start()
        for copy in copies:
            copy.wait()

    return pl.pallas_call(
        body,
        out_shape=jax.ShapeDtypeStruct((total, width), found[0].dtype),
        in_specs=[SM] + [ANY] * len(found),
        out_specs=VM,
        scratch_shapes=[pltpu.SemaphoreType.DMA((count,))],
        compiler_params=params(),
        cost_estimate=cost(0, 4 * total * width),
        name="assemble",
    )(places, *found)


def rms(v):
    return lax.rsqrt(jnp.mean(v * v, axis=-1, keepdims=True) + eps_norm)


def turn(block, cos, sin):
    lane = lax.broadcasted_iota(jnp.int32, block.shape, 1)
    partner = jnp.where(
        (lane & 63) < 32, pltpu.roll(block, 96, 1), pltpu.roll(block, 32, 1)
    )
    return block * cos + partner * sin


def project(toks, gain, w, cos, sin, places):
    rows, d = toks[0].shape
    n = w.shape[1]
    turned = n - 128
    count = len(toks)

    def body(at_ref, gain_ref, w_ref, cos_ref, sin_ref, *refs):
        for i in range(count):
            tok_ref, out_ref = refs[i], refs[count + i]
            at = pl.ds(pl.multiple_of(at_ref[i] * rows, rows), rows)
            cosine, sine = cos_ref[at, :], sin_ref[at, :]
            t = tok_ref[...].astype(F32)
            normed = (t * rms(t) * gain_ref[...]).astype(BF)
            u = mm(normed, w_ref[...])
            for b in range(0, turned, 128):
                out_ref[:, b : b + 128] = turn(u[:, b : b + 128], cosine, sine).astype(BF)
            out_ref[:, turned:] = u[:, turned:].astype(BF)

    return pl.pallas_call(
        body,
        out_shape=[jax.ShapeDtypeStruct((rows, n), BF)] * count,
        in_specs=[SM] + [VM] * (4 + count),
        out_specs=[VM] * count,
        compiler_params=params(),
        cost_estimate=cost(2 * count * rows * d * n, 2 * d * n + 4 * count * rows * d),
        name="project",
    )(places, gain, w, cos, sin, *toks)


def swapped(e):
    return (e & 1) * 2 + (e >> 1)


def split_store(a_ref, b_ref, e, at, value):
    @pl.when(e < 2)
    def _():
        a_ref[(e, *at)] = value

    @pl.when(e >= 2)
    def _():
        b_ref[(e - 2, *at)] = value


def lower_half(shape):
    return lax.broadcasted_iota(jnp.int32, shape, 1) < 64


def stage_heads(block, dst, rows_at, heads, factor):
    rows = block.shape[0]
    low = lower_half((rows, 128))
    for h in range(heads):
        part = block[:, (h // 2) * 128 : (h // 2 + 1) * 128].astype(F32) * factor
        keep = low if h % 2 == 0 else jnp.logical_not(low)
        dst[h, rows_at, :] = jnp.where(keep, part, 0.0).astype(BF)


def doubled(block):
    block = block.astype(F32)
    low = lower_half(block.shape)
    other = pltpu.roll(block, 64, 1)
    return jnp.where(low, block, other), jnp.where(low, other, block)


def allowed_mask(s_ref, keys, rows, first):
    q = lax.broadcasted_iota(jnp.int32, (1, rows), 1) + first
    begin = jnp.zeros_like(q)
    for i in range(5, s_ref.shape[0] - 1):
        begin = jnp.where(q >= s_ref[i], jnp.maximum(begin, s_ref[i]), begin)
    k = lax.broadcasted_iota(jnp.int32, (keys, rows), 0)
    return (k >= begin) & (k <= q)


def attend(scalars, pieces, heads, kvs):
    blocks = len(pieces)
    rows, width = pieces[0].shape
    span = blocks * rows
    qw = heads * HEAD_DIM
    share = heads // kvs

    def body(s_ref, *refs):
        ins, outs, (lse_ref, qs, kd, vd, vt, ob) = refs[:blocks], refs[blocks : 2 * blocks], refs[2 * blocks :]
        me = s_ref[4]
        for k in range(blocks):
            at = pl.ds(pl.multiple_of(s_ref[k] * rows, rows), rows)
            block = ins[k][...]
            stage_heads(block, qs, at, heads, score_scale)
            for i, x in enumerate(doubled(block[:, qw : qw + 128])):
                kd[i, at, :] = x.astype(BF)
            for i, x in enumerate(doubled(block[:, qw + 128 : qw + 256])):
                vd[i, at, :] = x
        for i in range(kvs):
            vt[i] = vd[i].T.astype(BF)

        def one(h, _):
            kv = h // share
            for p in range(blocks):
                keys = (p + 1) * rows
                q = qs[h, p * rows : (p + 1) * rows, :]
                s = mm(kd[kv, :keys, :], q, NT)
                s = jnp.where(allowed_mask(s_ref, keys, rows, p * rows), s, -1e30)
                peak = jnp.max(s, axis=0, keepdims=True)
                e = jnp.exp(s - peak)
                total = jnp.sum(e, axis=0, keepdims=True)
                o = mm(vt[kv, :, :keys], e.astype(BF)) / total
                ob[h, p * rows : (p + 1) * rows, :] = o.T
                lse_ref[pl.ds(h, 1), p * rows : (p + 1) * rows] = peak + jnp.log(total)
            return 0

        def some(i, _):
            for u in range(share):
                one(i * share + u, 0)
            return 0

        lax.fori_loop(0, kvs, some, 0)
        low = lower_half((rows, 128))
        for k in range(blocks):
            at = pl.ds(pl.multiple_of(lax.rem(me + k, blocks) * rows, rows), rows)
            for b in range(heads // 2):
                outs[k][:, b * 128 : (b + 1) * 128] = jnp.where(
                    low, ob[2 * b, at, :], ob[2 * b + 1, at, :]
                ).astype(BF)

    pairs = heads * rows * rows * blocks * (blocks + 1) // 2
    *mixes, lse = pl.pallas_call(
        body,
        out_shape=[jax.ShapeDtypeStruct((rows, qw), BF)] * blocks + [jax.ShapeDtypeStruct((8, span), F32)],
        in_specs=[SM] + [VM] * blocks,
        out_specs=[VM] * (blocks + 1),
        scratch_shapes=[
            pltpu.VMEM((heads, span, 128), BF),
            pltpu.VMEM((kvs, span, 128), BF),
            pltpu.VMEM((kvs, span, 128), F32),
            pltpu.VMEM((kvs, 128, span), BF),
            pltpu.VMEM((heads, span, 128), F32),
        ],
        compiler_params=params(),
        cost_estimate=cost(pairs * 1024, 4 * span * width, pairs),
        name="attend",
    )(scalars, *pieces)
    return mixes, lse


def attend_back(scalars, pieces, grads, lse, cos, sin, heads, kvs):
    blocks = len(pieces)
    rows, width = pieces[0].shape
    span = blocks * rows
    qw = heads * HEAD_DIM
    share = heads // kvs

    def body(s_ref, *refs):
        ins, gins = refs[:blocks], refs[blocks : 2 * blocks]
        lse_ref, cos_ref, sin_ref, out_ref, qs, gs, kd, kf, kt, vd, dk, dv, dq = refs[2 * blocks :]
        me = s_ref[4]
        for k in range(blocks):
            at = pl.ds(pl.multiple_of(s_ref[k] * rows, rows), rows)
            block = ins[k][...]
            stage_heads(block, qs, at, heads, score_scale)
            for i, x in enumerate(doubled(block[:, qw : qw + 128])):
                kd[i, at, :] = x.astype(BF)
                kf[i, at, :] = x
            for i, x in enumerate(doubled(block[:, qw + 128 : qw + 256])):
                vd[i, at, :] = x.astype(BF)
            at = pl.ds(pl.multiple_of(lax.rem(me + k, blocks) * rows, rows), rows)
            stage_heads(gins[k][...], gs, at, heads, 1.0)
        for i in range(kvs):
            kt[i] = kf[i].T.astype(BF)
        dk[...] = jnp.zeros_like(dk)
        dv[...] = jnp.zeros_like(dv)

        def one(h, _):
            kv = h // share
            for p in range(blocks):
                keys = (p + 1) * rows
                at = slice(p * rows, (p + 1) * rows)
                q = qs[h, at, :]
                g = gs[h, at, :]
                s = mm(kd[kv, :keys, :], q, NT)
                log_total = lse_ref[pl.ds(h, 1), at]
                chances = jnp.where(
                    allowed_mask(s_ref, keys, rows, p * rows), jnp.exp(s - log_total), 0.0
                )
                gp = mm(vd[kv, :keys, :], g, NT)
                row_dot = jnp.sum(chances * gp, axis=0, keepdims=True)
                ds = (chances * (gp - row_dot)).astype(BF)
                dq[h, at, :] = mm(kt[kv, :, :keys], ds).T
                dk[kv, :keys, :] += mm(ds, q)
                dv[kv, :keys, :] += mm(chances.astype(BF), g)
            return 0

        for h in range(heads):
            one(h, 0)
        low = lower_half((rows, 128))
        for p in range(blocks):
            at = slice(p * rows, (p + 1) * rows)
            cosine, sine = cos_ref[at, :], -sin_ref[at, :]
            for b in range(heads // 2):
                x = jnp.where(low, dq[2 * b, at, :], dq[2 * b + 1, at, :]) * score_scale
                out_ref[at, b * 128 : (b + 1) * 128] = turn(x, cosine, sine).astype(BF)
            k0, k1, v0, v1 = dk[0, at, :], dk[1, at, :], dv[0, at, :], dv[1, at, :]
            k0, k1 = k0 + pltpu.roll(k0, 64, 1), k1 + pltpu.roll(k1, 64, 1)
            v0, v1 = v0 + pltpu.roll(v0, 64, 1), v1 + pltpu.roll(v1, 64, 1)
            out_ref[at, qw : qw + 128] = turn(jnp.where(low, k0, k1), cosine, sine).astype(BF)
            out_ref[at, qw + 128 : qw + 256] = jnp.where(low, v0, v1).astype(BF)

    pairs = heads * rows * rows * blocks * (blocks + 1) // 2
    return pl.pallas_call(
        body,
        out_shape=jax.ShapeDtypeStruct((span, width), BF),
        in_specs=[SM] + [VM] * (2 * blocks + 3),
        out_specs=VM,
        scratch_shapes=[
            pltpu.VMEM((heads, span, 128), BF),
            pltpu.VMEM((heads, span, 128), BF),
            pltpu.VMEM((kvs, span, 128), BF),
            pltpu.VMEM((kvs, span, 128), F32),
            pltpu.VMEM((kvs, 128, span), BF),
            pltpu.VMEM((kvs, span, 128), BF),
            pltpu.VMEM((kvs, span, 128), F32),
            pltpu.VMEM((kvs, span, 128), F32),
            pltpu.VMEM((heads, span, 128), F32),
        ],
        compiler_params=params(),
        cost_estimate=cost(pairs * 2560, 8 * span * width, pairs),
        name="attend_back",
    )(scalars, *pieces, *grads, lse, cos, sin)


def join(scalars, mixes, w_out, tok, gain):
    blocks = len(mixes)
    rows, part = mixes[0].shape
    d = tok.shape[1]

    def body(s_ref, *refs):
        ins, (w_ref, tok_ref, gain_ref, mid_ref, hid_ref) = refs[:blocks], refs[blocks:]
        me = s_ref[4]
        branch = jnp.zeros((rows, d), F32)
        for k in range(blocks):
            at = pl.ds(pl.multiple_of(lax.rem(me - k + blocks, blocks) * part, part), part)
            branch = branch + mm(ins[k][...], w_ref[at, :])
        middle = tok_ref[...].astype(F32) + residual_scale * branch
        mid_ref[...] = middle
        hid_ref[...] = (middle * rms(middle) * gain_ref[...]).astype(BF)

    return pl.pallas_call(
        body,
        out_shape=(jax.ShapeDtypeStruct((rows, d), F32), jax.ShapeDtypeStruct((rows, d), BF)),
        in_specs=[SM] + [VM] * (blocks + 3),
        out_specs=(VM, VM),
        compiler_params=params(),
        cost_estimate=cost(2 * rows * d * d, 2 * d * d + 10 * rows * d),
        name="join",
    )(scalars, *mixes, w_out, tok, gain)


def join_back(scalars, addends, middle, cot, gain, w_out):
    blocks = 4
    rows, d = middle.shape
    part = d // blocks
    count = len(addends)

    def body(s_ref, *refs):
        ins, (mid_ref, cot_ref, gain_ref, w_ref, gmid_ref, br_ref, gg_ref, *outs) = refs[:count], refs[count:]
        me = s_ref[4]
        grad_hidden = sum(t[...].astype(F32) for t in ins)
        middle = mid_ref[...]
        inv = rms(middle)
        normal = middle * inv
        gg_ref[...] = jnp.sum(grad_hidden * normal, axis=0, keepdims=True)
        u = grad_hidden * gain_ref[...]
        grad_middle = cot_ref[...] + inv * (u - normal * jnp.mean(u * normal, axis=-1, keepdims=True))
        gmid_ref[...] = grad_middle
        br_ref[...] = (residual_scale * grad_middle).astype(BF)
        for k in range(blocks):
            at = pl.ds(pl.multiple_of(lax.rem(me - k + blocks, blocks) * part, part), part)
            outs[k][...] = mm(br_ref[...], w_ref[at, :], NT).astype(BF)

    front = lambda t: pl.BlockSpec((rows, d), lambda i: (0, 0))
    fixed = lambda *shape: pl.BlockSpec(shape, lambda i: (0, 0))
    grad_middle, branch, gain_grad, *mixes = pl.pallas_call(
        body,
        grid=(1,),
        out_shape=[
            jax.ShapeDtypeStruct((rows, d), F32),
            jax.ShapeDtypeStruct((rows, d), BF),
            jax.ShapeDtypeStruct((1, d), F32),
        ]
        + [jax.ShapeDtypeStruct((rows, part), BF)] * blocks,
        in_specs=[SM]
        + [front(t) for t in addends]
        + [fixed(rows, d), fixed(rows, d), fixed(1, d), fixed(d, d)],
        out_specs=[fixed(rows, d), fixed(rows, d), fixed(1, d)] + [fixed(rows, part)] * blocks,
        compiler_params=params(),
        cost_estimate=cost(2 * rows * d * d, 2 * d * d + 18 * rows * d),
        name="join_back",
    )(scalars, *addends, middle, cot, gain, w_out)
    return grad_middle, mixes, branch, gain_grad


def join_weights(scalars, here, branch, mixes, nd, ne):
    blocks = len(mixes)
    rows, part = mixes[0].shape
    d = branch.shape[1]
    w_rows = d // (nd * blocks * ne)

    def body(s_ref, here_ref, br_ref, *refs):
        ins, (gwa_ref, gwb_ref) = refs[:blocks], refs[blocks:]
        me = s_ref[4]
        for k in range(blocks):
            gw = mm(ins[k][...], br_ref[...], TN)
            for i in range(part // w_rows):
                q = lax.rem(me - k + blocks, blocks) * (part // w_rows) + i
                e = swapped(jnp.bitwise_xor(lax.rem(q, ne), here_ref[3]))
                b = lax.div(q, ne)
                m = lax.rem(lax.div(b, blocks) - here_ref[0] + nd, nd)
                put = gw[i * w_rows : (i + 1) * w_rows, :].astype(BF)
                split_store(gwa_ref, gwb_ref, e, (m, lax.rem(b, blocks)), put)

    return pl.pallas_call(
        body,
        out_shape=(jax.ShapeDtypeStruct((2, nd, blocks, w_rows, d), BF),) * 2,
        in_specs=[SM, SM] + [VM] * (1 + blocks),
        out_specs=(VM, VM),
        compiler_params=params(),
        cost_estimate=cost(2 * rows * d * d, 2 * d * d + 4 * rows * d),
        name="join_weights",
    )(scalars, here, branch, *mixes)


def halves(w, odd, devices):
    n, r, width = w.shape
    unit = FF // devices
    if 2 * unit != 128:
        parts = w.reshape(n, r, 2, devices // 4, 2, 2, unit)
        parts = jnp.transpose(parts, (5, 0, 1, 2, 3, 4, 6)).reshape(2, n, r, FF)
        return pick(parts, odd), pick(parts, 1 - odd)

    def body(odd_ref, w_ref, mine_ref, their_ref):
        low = lower_half((r, 128))
        even = odd_ref[0] == 0
        for m in range(width // 256):
            a = w_ref[0, :, 2 * m * 128 : (2 * m + 1) * 128].astype(F32)
            b = w_ref[0, :, (2 * m + 1) * 128 : (2 * m + 2) * 128].astype(F32)
            evens = jnp.where(low, a, pltpu.roll(b, 64, 1))
            odds = jnp.where(low, pltpu.roll(a, 64, 1), b)
            at = slice(m * 128, (m + 1) * 128)
            mine_ref[0, :, at] = jnp.where(even, evens, odds).astype(BF)
            their_ref[0, :, at] = jnp.where(even, odds, evens).astype(BF)

    spec = pl.BlockSpec((1, r, FF), lambda e: (e, 0, 0))
    return pl.pallas_call(
        body,
        grid=(n,),
        out_shape=(jax.ShapeDtypeStruct((n, r, FF), BF),) * 2,
        in_specs=[SM, pl.BlockSpec((1, r, width), lambda e: (e, 0, 0))],
        out_specs=(spec, spec),
        compiler_params=params(),
        cost_estimate=cost(0, 4 * n * r * width),
        name="halves",
    )(odd[None].astype(jnp.int32), w)


def whole(parts, odd, devices):
    count = len(parts)
    _, r, width = parts[0][0].shape
    r3 = r // 3
    unit = FF // devices

    def plain(own, other, theirs):
        total = own.astype(F32) + other.astype(F32)
        theirs = theirs.astype(F32)
        pair = jnp.stack([jnp.where(odd == 0, total[0], theirs), jnp.where(odd == 0, theirs, total[0])])
        pair = pair.reshape(2, r, 2, devices // 4, 2, unit)
        down = [total[2, b * r3 : (b + 1) * r3] for b in range(3)]
        return jnp.transpose(pair, (1, 2, 3, 4, 0, 5)).reshape(r, 2 * width), jnp.concatenate(down, axis=1)

    if 2 * unit != 128:
        done = [plain(*p) for p in parts]
        return jnp.stack([p[0] for p in done]), jnp.stack([p[1] for p in done])

    def body(odd_ref, own_ref, other_ref, their_ref, *refs):
        in_ref, down_ref = refs[-2], refs[-1]
        low = lower_half((r, 128))
        even = odd_ref[0] == 0
        for m in range(width // 128):
            at = slice(m * 128, (m + 1) * 128)
            mine = own_ref[0, :, at].astype(F32) + other_ref[0, :, at].astype(F32)
            their = their_ref[:, at].astype(F32)
            evens, odds = jnp.where(even, mine, their), jnp.where(even, their, mine)
            in_ref[0, :, 2 * m * 128 : (2 * m + 1) * 128] = jnp.where(low, evens, pltpu.roll(odds, 64, 1))
            in_ref[0, :, (2 * m + 1) * 128 : (2 * m + 2) * 128] = jnp.where(
                low, pltpu.roll(evens, 64, 1), odds
            )
        for b in range(3):
            at = slice(b * r3, (b + 1) * r3)
            down_ref[0, :, b * width : (b + 1) * width] = (
                own_ref[2, at, :].astype(F32) + other_ref[2, at, :].astype(F32)
            )

    done = ()
    for e, (own, other, theirs) in enumerate(parts):
        fixed = lambda *shape: pl.BlockSpec(shape, lambda i: (0,) * len(shape))
        done = pl.pallas_call(
            body,
            grid=(1,),
            out_shape=(
                jax.ShapeDtypeStruct((count, r, 2 * width), F32),
                jax.ShapeDtypeStruct((count, r3, 3 * width), F32),
            ),
            in_specs=[SM, fixed(3, r, width), fixed(3, r, width), fixed(r, width)] + [ANY] * len(done),
            out_specs=(
                pl.BlockSpec((1, r, 2 * width), lambda i, e=e: (e, 0, 0)),
                pl.BlockSpec((1, r3, 3 * width), lambda i, e=e: (e, 0, 0)),
            ),
            input_output_aliases={4: 0, 5: 1} if done else {},
            compiler_params=params(),
            cost_estimate=cost(0, 20 * r * width),
            name="whole",
        )(odd[None].astype(jnp.int32), own, other, theirs, *done)
    return done


def experts_rows(places, which, rows_in, cots, shards, sums, last):
    piece, d = rows_in[0].shape
    group = 1
    rows = piece * group
    tiles = len(rows_in) // group
    total = rows * tiles
    count, n = len(shards), len(shards[0])
    r, width = shards[0][0][0].shape[-2:]
    arrays = {id(t): t for shard in shards for t, _ in shard}
    slot = {key: k for k, key in enumerate(arrays)}
    arrays = list(arrays.values())
    half = width // 2
    r3 = r // 3
    first = sums is None

    def body(places_ref, *refs):
        n_in = tiles * group
        h_refs, c_refs, refs = refs[:n_in], refs[n_in : 2 * n_in], refs[2 * n_in :]
        w_refs, refs = refs[: len(arrays)], refs[len(arrays) :]
        if not first:
            in_h, in_o, refs = refs[0], refs[1], refs[2:]
        if last:
            out_h, rest_h, out_o, rest_o, gb_ref, gat_ref, *refs = refs
        else:
            out_h, out_o, gb_ref, gat_ref, *refs = refs
        if first:
            ht_ref, *refs = refs
        wiv, wdv, ga_ref, hv, cv, sems, row_sems = refs
        t = pl.program_id(0)
        moves = []
        for i in range(n_in):
            at = pl.ds(i % group * piece, piece)
            moves.append(
                (
                    pltpu.make_async_copy(h_refs[i], hv.at[i // group, at, :], row_sems.at[0, i]),
                    pltpu.make_async_copy(c_refs[i], cv.at[i // group, at, :], row_sems.at[1, i]),
                )
            )

        @pl.when(t == 0)
        def _():
            copies = []
            for i in range(count):
                for e in range(n):
                    array, which_of = shards[i][e]
                    source = w_refs[slot[id(array)]]
                    source = source if which_of is None else source.at[which_of]
                    parts = []
                    for b in range(2):
                        at = pl.multiple_of(places_ref[3 * i + b] * r, r)
                        parts.append((source.at[2 * b], wiv.at[pl.ds(at, r), e * width : (e + 1) * width]))
                    at = pl.multiple_of(places_ref[3 * i + 2] * r3 + e * half, r3)
                    for b in range(3):
                        parts.append(
                            (
                                source.at[1, b * r3 : (b + 1) * r3, :],
                                wdv.at[pl.ds(at, r3), b * width : (b + 1) * width],
                            )
                        )
                    for k, (a, b) in enumerate(parts):
                        copies.append(pltpu.make_async_copy(a, b, sems.at[i, e, k]))
            for copy in copies:
                copy.start()
            for a, b in moves[:group]:
                a.start()
                b.start()
            for copy in copies:
                copy.wait()
            for a, b in moves[group:]:
                a.start()
                b.start()

        for i in range(tiles):

            @pl.when(t == i)
            def _():
                for a, b in moves[i * group : (i + 1) * group]:
                    a.wait()
                    b.wait()

        h = hv[t]
        c = cv[t, :, :d]
        gates = cv[t, :, d:].astype(F32)
        lane = lax.broadcasted_iota(jnp.int32, gates.shape, 1) - places_ref[3 * count]
        for e in range(n):
            g = jnp.sum(jnp.where(lane == which + e, gates, 0.0), axis=1, keepdims=True)
            gu = mm(h, wiv[:, e * width : (e + 1) * width])
            gate, up = gu[:, :half], gu[:, half:]
            sg = jax.nn.sigmoid(gate)
            silu = gate * sg
            ga = mm(c, wdv[e * half : (e + 1) * half, :], NT) * g
            ga_ref[:, e * half : (e + 1) * half] = (silu * up * g).astype(BF)
            gb_ref[:, e * width : e * width + half] = (ga * up * (sg + silu * (1.0 - sg))).astype(BF)
            gb_ref[:, e * width + half : (e + 1) * width] = (ga * silu).astype(BF)
        o = mm(ga_ref[...], wdv[...])
        gh = mm(gb_ref[...], wiv[...], NT)
        gat_ref[...] = ga_ref[...].T
        if first:
            ht_ref[...] = h.T
        if not first:
            o = o + in_o[...].astype(F32)
            gh = gh + in_h[...].astype(F32)
        if last:

            @pl.when(t < tiles // 2)
            def _():
                out_o[...] = o.astype(BF)
                out_h[...] = gh.astype(BF)

            @pl.when(t >= tiles // 2)
            def _():
                rest_o[...] = o.astype(BF)
                rest_h[...] = gh.astype(BF)

        else:
            out_o[...] = o.astype(BF)
            out_h[...] = gh.astype(BF)

    tile = lambda c: pl.BlockSpec((rows, c), lambda t: (t, 0))
    flat = lambda c: pl.BlockSpec((c, rows), lambda t: (0, t))
    if last:
        sum_shapes = (jax.ShapeDtypeStruct((total // 2, d), BF),) * 4
        front = pl.BlockSpec((rows, d), lambda t: (jnp.minimum(t, tiles // 2 - 1), 0))
        back = pl.BlockSpec((rows, d), lambda t: (jnp.maximum(t - tiles // 2, 0), 0))
        sum_specs = (front, back, front, back)
    else:
        sum_shapes = (jax.ShapeDtypeStruct((total, d), BF),) * 2
        sum_specs = (tile(d), tile(d))
    return pl.pallas_call(
        body,
        grid=(tiles,),
        out_shape=sum_shapes
        + (
            jax.ShapeDtypeStruct((total, n * width), BF),
            jax.ShapeDtypeStruct((n * half, total), BF),
        )
        + ((jax.ShapeDtypeStruct((d, total), BF),) if first else ()),
        in_specs=[SM]
        + [ANY] * (2 * len(rows_in) + len(arrays))
        + ([] if first else [tile(d), tile(d)]),
        out_specs=sum_specs + (tile(n * width), flat(n * half)) + ((flat(d),) if first else ()),
        scratch_shapes=[
            pltpu.VMEM((d, n * width), BF),
            pltpu.VMEM((n * half, d), BF),
            pltpu.VMEM((rows, n * half), BF),
            pltpu.VMEM((tiles, rows, d), BF),
            pltpu.VMEM((tiles, rows, cots[0].shape[1]), BF),
            pltpu.SemaphoreType.DMA((count, n, 5)),
            pltpu.SemaphoreType.DMA((2, len(rows_in))),
        ],
        compiler_params=params(),
        cost_estimate=cost(6 * n * total * d * width, 50e6, n * total * half),
        name="experts_rows",
    )(places, *rows_in, *cots, *arrays, *(() if first else sums))


def experts_weights(scalars, rows_t, cots, gb, ga_t, n, devices):
    d, total = rows_t.shape
    width, half = gb.shape[1] // n, ga_t.shape[0] // n
    r = d // devices
    r3 = r // 3
    nd = devices // 4
    tiles = len(cots)
    rows = total // tiles

    def body(s_ref, h_any, gb_any, ga_any, *refs):
        c_refs, refs = refs[:tiles], refs[tiles:]
        outs, (down, h_ref, gb_ref, ga_ref, c_ref, stage, sems, c_sems, out_sems) = refs[: n * nd], refs[n * nd :]
        ahead = [lax.rem(s_ref[0] + k, nd) for k in range(nd)]
        spans = [pl.ds(pl.multiple_of(x * 4 * r, 4 * r), 4 * r) for x in ahead]
        first = [pltpu.make_async_copy(gb_any, gb_ref, sems.at[0])]
        first += [
            pltpu.make_async_copy(h_any.at[spans[k], :], h_ref.at[k], sems.at[1 + k]) for k in range(nd)
        ]
        second = [pltpu.make_async_copy(ga_any, ga_ref, c_sems.at[tiles])]
        second += [
            pltpu.make_async_copy(c_refs[i].at[:, :d], c_ref.at[pl.ds(i * rows, rows), :], c_sems.at[i])
            for i in range(tiles)
        ]
        for copy in first[:2]:
            copy.start()
        first[0].wait()
        for k in range(nd):
            first[1 + k].wait()
            for copy in first[2:] + second if k == 0 else []:
                copy.start()
            part = mm(h_ref[k], gb_ref[...]).astype(BF)
            for z in range(4):
                where = jnp.bitwise_xor(s_ref[2], z // 2)
                slot = jnp.bitwise_xor(s_ref[1], z % 2)
                for e in range(n):
                    stage[e * nd + k, where, slot] = part[z * r : (z + 1) * r, e * width : (e + 1) * width]
        for copy in second:
            copy.wait()
        leaving = []
        for e in range(n):
            down[...] = mm(ga_ref[e * half : (e + 1) * half, :], c_ref[...]).astype(BF)
            for k in range(nd):
                for z in range(2):
                    where = jnp.bitwise_xor(s_ref[2], z)
                    at = pl.ds(pl.multiple_of((2 * ahead[k] + z) * r3, r3), r3)
                    for b in range(3):
                        stage[e * nd + k, where, 2, b * r3 : (b + 1) * r3, :] = down[
                            at, b * width : (b + 1) * width
                        ]
                leaving.append(
                    pltpu.make_async_copy(stage.at[e * nd + k], outs[e * nd + k], out_sems.at[e * nd + k])
                )
                leaving[-1].start()
        for copy in leaving:
            copy.wait()

    outs = pl.pallas_call(
        body,
        out_shape=[jax.ShapeDtypeStruct((2, 3, r, width), BF)] * (n * nd),
        in_specs=[SM] + [ANY] * (3 + tiles),
        out_specs=[ANY] * (n * nd),
        scratch_shapes=[
            pltpu.VMEM((half, d), BF),
            pltpu.VMEM((nd, 4 * r, total), BF),
            pltpu.VMEM((total, n * width), BF),
            pltpu.VMEM((n * half, total), BF),
            pltpu.VMEM((total, d), BF),
            pltpu.VMEM((n * nd, 2, 3, r, width), BF),
            pltpu.SemaphoreType.DMA((1 + nd,)),
            pltpu.SemaphoreType.DMA((tiles + 1,)),
            pltpu.SemaphoreType.DMA((n * nd,)),
        ],
        compiler_params=params(),
        cost_estimate=cost(3 * n * total * d * width, 20e6),
        name="experts_weights",
    )(scalars, rows_t, gb, ga_t, *cots)
    return [outs[e * nd : (e + 1) * nd] for e in range(n)]


def finish(scalars, dqkv, w, blocks):
    total, width = dqkv.shape
    d = w.shape[0]
    rows = total // blocks

    def body(s_ref, dq_ref, w_ref, *outs):
        for k in range(blocks):
            at = lax.rem(s_ref[4] - 1 - k + 2 * blocks, blocks)
            at = pl.ds(pl.multiple_of(at * rows, rows), rows)
            outs[k][...] = mm(dq_ref[at, :], w_ref[...], NT).astype(BF)

    return pl.pallas_call(
        body,
        out_shape=[jax.ShapeDtypeStruct((rows, d), BF)] * blocks,
        in_specs=[SM, VM, VM],
        out_specs=[VM] * blocks,
        compiler_params=params(),
        cost_estimate=cost(2 * total * d * width, 4 * total * d),
        name="finish",
    )(scalars, dqkv, w)


def finish_weights(scalars, here, dqkv, gn, toks, gain, gain_grad, nd, ne):
    blocks = len(toks)
    rows, d = toks[0].shape
    width = dqkv.shape[1]
    w_rows = d // (nd * blocks * ne)

    def body(s_ref, here_ref, dq_ref, gain_ref, gg_ref, *refs):
        ins, gns, (gwa_ref, gwb_ref, acc) = refs[:blocks], refs[blocks : 2 * blocks], refs[2 * blocks :]
        gg = jnp.zeros((1, d), F32)
        for k in range(blocks):
            to = s_ref[k]
            at = pl.ds(pl.multiple_of(to * rows, rows), rows)
            t = ins[k][...].astype(F32)
            normal = t * rms(t)
            normed = (normal * gain_ref[...]).astype(BF)
            gn = gns[(k - 1) % blocks][...].astype(F32)
            gg = gg + jnp.sum(gn * normal, axis=0, keepdims=True)
            part = mm(normed, dq_ref[at, :], TN)
            acc[...] = part if k == 0 else acc[...] + part
        row = lax.broadcasted_iota(jnp.int32, (128, d), 0)
        both = jnp.where(row == 0, gg, jnp.where(row == 1, gg_ref[...], 0.0)).T
        for q in range(d // w_rows):
            e = swapped(jnp.bitwise_xor(q % ne, here_ref[3]))
            m = lax.rem(q // ne // blocks - here_ref[0] + nd, nd)
            at = slice(q * w_rows, (q + 1) * w_rows)
            put = jnp.concatenate([acc[at, :], both[at, :]], axis=1).astype(BF)
            split_store(gwa_ref, gwb_ref, e, (m, q // ne % blocks), put)

    return pl.pallas_call(
        body,
        out_shape=(jax.ShapeDtypeStruct((2, nd, blocks, w_rows, width + 128), BF),) * 2,
        in_specs=[SM, SM] + [VM] * (3 + 2 * blocks),
        out_specs=(VM, VM),
        scratch_shapes=[pltpu.VMEM((d, width), F32)],
        compiler_params=params(),
        cost_estimate=cost(2 * blocks * rows * d * width, 6 * blocks * rows * d),
        name="finish_weights",
    )(scalars, here, dqkv, gain, gain_grad, *toks, *gn)


def per_device(
    tokens,
    gain_attn,
    w_query,
    w_key,
    w_value,
    w_out,
    gain_moe,
    w_in,
    w_down,
    routes,
    gates,
    lengths,
    cotangent,
):
    nd, nz, ne = lax.axis_size("dp"), lax.axis_size("ctx"), lax.axis_size("exp")
    x, z, j = lax.axis_index("dp"), lax.axis_index("ctx"), lax.axis_index("exp")
    rows, d = tokens.shape[1:]
    span = rows * nz
    w_rows = w_query.shape[0]
    heads, kvs = HEADS // nz, KV_HEADS // nz
    qw, kw = heads * HEAD_DIM, kvs * HEAD_DIM
    local_experts = w_in.shape[0]
    experts = local_experts * ne
    i32 = jnp.int32
    mod = lambda v, n: lax.rem(v + 8 * n, n)

    ends = jnp.cumsum(lengths[0]).astype(i32)
    places = [mod(z - k, nz) for k in range(nz)]
    scalars = jnp.concatenate([jnp.stack(places + [z]).astype(i32), ends])
    place = jnp.arange(span, dtype=i32)
    place = place - jnp.max(jnp.where(place[:, None] >= ends[None, :-1], ends[None, :-1], 0), axis=1)
    lane = jnp.arange(128, dtype=i32)
    half = HEAD_DIM // 2
    frequency = rope_base ** (-2.0 * jnp.arange(half, dtype=F32) / HEAD_DIM)
    angles = place.astype(F32)[:, None] * frequency[None, :]
    cos = jnp.tile(jnp.cos(angles), (1, 128 // half))
    sin = jnp.tile(jnp.sin(angles), (1, 128 // half)) * jnp.where((lane & 63) < 32, -1.0, 1.0)[None, :]

    run = Stages(gain_attn)
    gain_a, gain_m = gain_attn[None, :], gain_moe[None, :]
    devices = nd * nz
    odd, zh = jnp.bitwise_and(z, 1), z // 2
    batch = local_experts // 2
    tok, cot = tokens[0], cotangent[0]
    flip_e = lambda v, e: flip(v, "exp", e)

    def row_blocks(found, owners, order):
        at = [
            (mod(x - m, nd) * nz + p) * ne + jnp.bitwise_xor(j, e + 2 * b)
            for e in (0, 1) for b, m in order for p in owners
        ]
        return assemble(found, jnp.stack(at).astype(i32))

    by_m = [(b, m) for m in range(nd) for b in (0, 1)]
    by_b = [(b, m) for b in (0, 1) for m in range(nd)]

    here = jnp.stack([x, odd, zh, j]).astype(i32)

    parts = [
        jnp.concatenate(
            [
                w_query[:, p * qw : (p + 1) * qw],
                w_key[:, p * kw : (p + 1) * kw],
                w_value[:, p * kw : (p + 1) * kw],
            ],
            axis=1,
        )
        for p in range(nz)
    ]
    cut = rows // 2
    toks = [tok, shift(tok, "ctx", 1)]
    w_parts = jnp.stack(parts)
    w_mine = [pick(w_parts, z)] + [shift(pick(w_parts, mod(z + k, nz)), "ctx", k) for k in range(1, nz)]
    run.end(toks, w_mine)

    half_2 = [shift(run.hold(toks[1])[:cut], "ctx", 1)]
    mine_in, their_in = halves(run.hold(w_in), odd, devices)
    down = run.hold(w_down)
    down = jnp.concatenate([down[:, :, b * FF : (b + 1) * FF] for b in range(d // FF)], axis=1)
    w_mine = jnp.stack(w_mine)
    w_mine = jnp.stack([w_mine, flip_e(run.hold(w_mine), 2)])
    line = [hop(run.hold(w_out), pairs) for pairs in (ACROSS, UP, DOWN)]
    run.end(half_2, w_mine, line, mine_in)

    half_2.append(shift(run.hold(toks[1])[cut:], "ctx", 1))
    hits = run.hold(routes)[0][:, :, None] == jnp.arange(128, dtype=i32)[None, None, :]
    dense = jnp.sum(jnp.where(hits, gates[0].astype(F32)[:, :, None], 0.0), axis=1).astype(BF)
    cot_b = jnp.concatenate([(residual_scale * run.hold(cot)).astype(BF), dense], axis=1)
    w_found = ring(run.hold(w_mine), "dp")
    line_end = hop(run.hold(line[0]), OUTER)
    run.end(half_2, w_found, line_end, cot_b)

    toks.append(jnp.concatenate(half_2))
    toks.append(shift(run.hold(toks[2]), "ctx", 1))
    got_1 = flip(run.hold(their_in[:batch]), "ctx", 1)
    w_found = w_found + [flip_e(t, 1) for t in run.hold(w_found)]
    w_line = ring(run.hold(jnp.stack(line_gather(*line, line_end, w_out))), "dp")
    cot_2 = flip_e(run.hold(cot_b), 2)
    w_qkv = row_blocks(w_found, places, by_m)
    at = jnp.stack(places).astype(i32)
    pieces = project(toks[: nz - 1], gain_a, w_qkv, cos, sin, at[: nz - 1])
    run.end(toks, pieces, got_1, w_line, cot_2)

    packet = lambda e, got: jnp.stack([mine_in[e], down[e], got[e % batch]])
    near = [packet(e, got_1) for e in range(batch)]
    far = [flip(run.hold(near[0]), "ctx", 2)]
    own = [ring(run.hold(jnp.stack(near)), "dp")]
    w_line = jnp.stack(w_line)
    w_line = jnp.stack([w_line, flip_e(run.hold(w_line), 2)])
    cot_n = flip(run.hold(cot_b), "ctx", 1)
    pieces = pieces + project([run.hold(toks[3])], gain_a, w_qkv, cos, sin, at[nz - 1 :])
    mix_out, lse = attend(scalars, pieces, heads, kvs)
    run.end(far, own, w_line, cot_n, mix_out)

    mixes = run.hold(mix_out)
    mixes = [mixes[0]] + [shift(mixes[k], "ctx", k) for k in range(1, nz)]
    w_line = [w_line, flip_e(run.hold(w_line), 1)]
    cot_n2 = flip_e(run.hold(cot_n), 2)
    w_out_all = row_blocks(w_line, line_places(z), by_b)
    run.end(mixes, w_out_all, cot_n2)

    cot_1 = flip_e(run.hold(cot_b), 1)
    cot_n1, cot_n3 = flip_e(run.hold(cot_n), 1), flip_e(run.hold(cot_n2), 1)
    got_2 = flip(run.hold(their_in[batch:]), "ctx", 1)
    over = [ring(run.hold(far[0]), "dp")]
    middle, hidden = join(scalars, run.hold(mixes), w_out_all, tok, gain_m)
    run.end(hidden, got_2, over, cot_1, cot_n1, cot_n3)

    hidden_2, hidden_n = flip_e(run.hold(hidden), 2), flip(run.hold(hidden), "ctx", 1)
    far += [flip(run.hold(near[e]), "ctx", 2) for e in range(1, batch)]
    near.append(packet(batch, got_2))
    own.append(ring(run.hold(near[batch]), "dp"))
    hidden_1 = flip_e(run.hold(hidden), 1)
    run.end(hidden_1, hidden_2, hidden_n, far, own)

    hidden_n2 = flip_e(run.hold(hidden_n), 2)
    hidden_n1, hidden_3 = flip_e(run.hold(hidden_n), 1), flip_e(run.hold(hidden_2), 1)
    over += [ring(run.hold(far[e]), "dp") for e in range(1, batch)]
    far.append(flip(run.hold(near[batch]), "ctx", 2))
    near += [packet(e, run.hold(got_2)) for e in range(batch + 1, local_experts)]
    run.end(hidden_n1, hidden_3, hidden_n2, over, far, near)

    rows_in = [hidden, hidden_n, hidden_2, hidden_n2, hidden_1, hidden_n1, hidden_3, None]
    cots = [cot_b, cot_n, cot_2, cot_n2, cot_1, cot_n1, None, cot_n3]
    w_at = []
    for zc in (z, jnp.bitwise_xor(z, 2)):
        for m in range(nd):
            xc = mod(x - m, nd)
            w_at += [xc * nz + zc, xc * nz + jnp.bitwise_xor(zc, 1), xc * 2 + zc // 2]
    w_at = jnp.stack(w_at + [j * local_experts]).astype(i32)
    rows_in = run.hold(rows_in[:-1]) + [flip_e(run.hold(hidden_n2), 1)]
    cots[6] = flip_e(run.hold(cot_2), 1)
    own += [ring(run.hold(near[e]), "dp") for e in range(batch + 1, local_experts)]
    far += [flip(run.hold(near[e]), "ctx", 2) for e in range(batch + 1, local_experts)]
    over.append(ring(run.hold(far[batch]), "dp"))
    shards = [[(t, e) for e in range(batch)] for t in own[0]]
    shards += [[(t, None) for t in some] for some in zip(*over[:batch])]
    sum_h, sum_o, gb, ga_t, rows_t = experts_rows(w_at, 0, rows_in, cots, shards, None, False)
    run.end(far, own, over, sum_h)

    over += [ring(run.hold(far[e]), "dp") for e in range(batch + 1, local_experts)]
    gw_1 = experts_weights(here, rows_t, cots, run.hold(gb), ga_t, batch, devices)
    run.end(over, gw_1)

    x_0 = dp_reduce_pair(run.hold(gw_1[0]))
    shards = [[(t, None) for t in some] for some in zip(*own[1:])]
    shards += [[(t, None) for t in some] for some in zip(*over[batch:])]
    sum_h, rest_h, sum_o, rest_o, gb, ga_t = experts_rows(
        w_at, batch, run.hold(rows_in), cots, shards, (sum_h, sum_o), True
    )
    run.end(x_0, sum_h)

    rest_h = flip_e(run.hold(rest_h), 1)
    run.end(rest_h)

    part = rows // 2
    all_h = sum_h
    sum_h = [
        add(sum_h[a * part : b * part], rest_h[a * part : b * part])
        for a, b in ((2, 3), (3, 4), (4, 5), (5, 6), (6, 7), (7, 8))
    ]
    by_y, by_z = flip_e(run.hold(sum_h[4]), 2), flip(run.hold(sum_h[5]), "ctx", 1)
    z_0 = flip(run.hold(x_0[1]), "ctx", 2)
    x_1 = dp_reduce_pair(run.hold(gw_1[1]))
    rest_o = flip_e(run.hold(rest_o), 1)
    gw_2 = experts_weights(here, rows_t, cots, run.hold(gb), ga_t, batch, devices)
    run.end(by_y, by_z, z_0, x_1, rest_o, gw_2)

    near_h = flip_e(jnp.concatenate([sum_h[2], add(run.hold(sum_h[3]), by_z)]), 2)
    other_h = flip(jnp.concatenate([add(run.hold(sum_h[0]), by_y), sum_h[1]]), "ctx", 1)
    z_1 = flip(run.hold(x_1[1]), "ctx", 2)
    x_2 = dp_reduce_pair(run.hold(gw_2[0]))
    sum_o = [add(sum_o[a * rows : (a + 1) * rows], rest_o[a * rows : (a + 1) * rows]) for a in range(4)]
    run.end(near_h, other_h, z_1, x_2, sum_o)

    grad_middle, grad_mix, branch, grad_gain_m = join_back(
        scalars, [all_h, rest_h, *run.hold([near_h, other_h])], middle, cot, gain_m, w_out_all
    )
    grad_mixes = [grad_mix[0]] + [shift(grad_mix[k], "ctx", -k) for k in range(1, nz)]
    x_3 = dp_reduce_pair(run.hold(gw_2[1]))
    far_o1 = flip_e(run.hold(sum_o[3]), 2)
    wo_a, wo_b = join_weights(scalars, here, branch, mixes, nd, ne)
    ready = lax.optimization_barrier((x_0[0], x_1[0], branch))
    swap = jnp.stack([add(ready[0][1], z_0[1]), add(ready[1][1], z_1[1])])
    run.end(grad_mixes, x_3, far_o1, wo_b, swap)

    z_2 = flip(run.hold(x_2[1]), "ctx", 2)
    far_o = flip_e(run.hold(sum_o[2]), 2)
    other_o = flip(add(sum_o[1], run.hold(far_o1)), "ctx", 1)
    wo_b = flip_e(run.hold(wo_b), 1)
    dqkv = attend_back(scalars, pieces, run.hold(grad_mixes), lse, cos, sin, heads, kvs)
    grad_normed = finish(scalars, dqkv, w_qkv, nz)
    run.end(z_2, far_o, other_o, wo_b, grad_normed)

    z_3 = flip(run.hold(x_3[1]), "ctx", 2)
    gw_a, gw_b = finish_weights(scalars, here, dqkv, run.hold(grad_normed), toks, gain_a, grad_gain_m, nd, ne)
    swap = flip(run.hold(swap), "ctx", 1)
    swap_2 = flip(add(run.hold(x_2[0])[1], z_2[1]), "ctx", 1)
    wo_b = run.hold(wo_b)
    wo_far = flip_e(add(wo_a[1], wo_b[1]), 2)
    run.end(gw_b, swap, swap_2, wo_far, z_3)

    tail = run.hold(grad_normed)
    total = shift(tail[0], "ctx", 1)
    gw_b = flip_e(run.hold(gw_b), 1)
    swap_3 = flip(add(run.hold(x_3[0])[1], z_3[1]), "ctx", 1)
    gw = add(gw_a, gw_b)
    run.end(total, gw, swap_3)

    total = shift(add(run.hold(total), tail[1]), "ctx", 1)
    gw_far = flip_e(run.hold(gw[1]), 2)
    wo_b, wo_far = run.hold([wo_b, wo_far])
    wo = (wo_a[0].astype(F32) + wo_b[0].astype(F32) + wo_far.astype(F32)).astype(BF)
    wo = dp_reduce(list(wo))
    run.end(total, gw_far, wo)

    total = shift(add(run.hold(total), tail[2]), "ctx", 1)
    gw = dp_reduce(list(run.hold(add(gw[0], gw_far))))
    run.end(total, gw)

    mine = jnp.concatenate(run.hold([gw, wo]), axis=2)
    parts = [pick(mine, z)] + [shift(pick(mine, mod(z + k, nz)), "ctx", k) for k in range(1, nz)]

    gn = tail[3].astype(F32) + total.astype(F32)
    expert_sum = sum_o[0].astype(F32) + far_o.astype(F32) + other_o.astype(F32)
    mixed_out = (middle + residual_scale * expert_sum).astype(BF)
    q_end, k_end, v_end = qw, qw + kw, qw + 2 * kw
    gains = sum(p[:, v_end : v_end + 2].astype(F32) for p in parts)
    grad_out = sum(p[:, v_end + 128 :].astype(F32) for p in parts)
    order = jnp.stack([p[:, :v_end] for p in parts])
    order = [pick(order, mod(z - p, nz)).astype(F32) for p in range(nz)]
    grad_query = jnp.concatenate([g[:, :q_end] for g in order], axis=1)
    grad_key = jnp.concatenate([g[:, q_end:k_end] for g in order], axis=1)
    grad_value = jnp.concatenate([g[:, k_end:] for g in order], axis=1)

    grads_in, grads_down = whole(
        [
            (x_0[0], z_0, swap[0]), (x_1[0], z_1, swap[1]), (x_2[0], z_2, swap_2), (x_3[0], z_3, swap_3)
        ],
        odd,
        devices,
    )

    t = tok.astype(F32)
    inv = rms(t)
    normal = t * inv
    u = gn * gain_a
    grad_tokens = grad_middle + inv * (u - normal * jnp.mean(u * normal, axis=-1, keepdims=True))
    return (
        mixed_out[None],
        grad_tokens[None],
        gains[:, 0],
        grad_query,
        grad_key,
        grad_value,
        grad_out.astype(F32),
        gains[:, 1],
        grads_in,
        grads_down,
    )


def solution(mesh):
    every = ("dp", "ctx", "exp")
    return jax.shard_map(
        per_device,
        mesh=mesh,
        in_specs=(
            P(("dp", "exp"), "ctx", None),
            P(),
            P(every, None),
            P(every, None),
            P(every, None),
            P(every, None),
            P(),
            P("exp", ("dp", "ctx"), None),
            P("exp", ("dp", "ctx"), None),
            P(("dp", "exp"), "ctx", None),
            P(("dp", "exp"), "ctx", None),
            P(("dp", "exp"), None),
            P(("dp", "exp"), "ctx", None),
        ),
        out_specs=(
            P(("dp", "exp"), "ctx", None),
            P(("dp", "exp"), "ctx", None),
            P(every),
            P(every, None),
            P(every, None),
            P(every, None),
            P(every, None),
            P(every),
            P("exp", ("dp", "ctx"), None),
            P("exp", ("dp", "ctx"), None),
        ),
        check_vma=False,
    )
```

```python
import functools

import jax
import jax.numpy as jnp
from jax import lax
from jax.experimental import pallas as pl
from jax.experimental.pallas import tpu as pltpu
from jax.sharding import PartitionSpec as P

HEADS = 24
KV_HEADS = 8
HEAD_DIM = 64
FF = 512
TOP = 8

eps_norm = 1e-06
score_scale = 0.015625
residual_scale = 0.22
rope_base = 10000.0

BF = jnp.bfloat16
F32 = jnp.float32
SCALE = 3
VMEM_LIMIT = 60 * 1024 * 1024
ANY = pl.BlockSpec(memory_space=pl.ANY)
VM = pl.BlockSpec(memory_space=pltpu.VMEM)
SM = pl.BlockSpec(memory_space=pltpu.SMEM)
NN = (((1,), (0,)), ((), ()))
NT = (((1,), (1,)), ((), ()))
TN = (((0,), (0,)), ((), ()))


def mm(a, b, dims=NN):
    return lax.dot_general(a, b, dims, preferred_element_type=F32)


def params(**kw):
    return pltpu.CompilerParams(vmem_limit_bytes=VMEM_LIMIT, **kw)


def cost(flops, nbytes, trans=0):
    return pl.CostEstimate(
        flops=int(flops / SCALE), bytes_accessed=int(nbytes / SCALE), transcendentals=0
    )


def shift(x, axis, by):
    n = lax.axis_size(axis)
    return lax.ppermute(x, axis, [(i, (i + by) % n) for i in range(n)])


def flip(x, axis, mask):
    n = lax.axis_size(axis)
    return lax.ppermute(x, axis, [(i, i ^ mask) for i in range(n)])


class Stages:
    def __init__(self, token):
        self.token = token

    def hold(self, x):
        leaves, tree = jax.tree.flatten(x)
        leaves = [lax.optimization_barrier((leaf, self.token))[0] for leaf in leaves]
        return jax.tree.unflatten(tree, leaves)

    def end(self, *outs):
        self.token = lax.optimization_barrier((self.token, *jax.tree.leaves(outs)))[0]


def ring(x, axis):
    out = [x]
    for _ in range(lax.axis_size(axis) - 1):
        out.append(shift(out[-1], axis, 1))
    return out


def hop(x, pairs):
    return lax.ppermute(x, "ctx", pairs)


UP, DOWN = [(0, 1), (1, 2), (2, 3)], [(1, 0), (2, 1), (3, 2)]
ACROSS = [(0, 2), (1, 3), (2, 0), (3, 1)]
INNER, OUTER = [(0, 1), (3, 2)], [(1, 0), (2, 3)]


def line_places(z):
    return [z, jnp.bitwise_xor(z, 2), jnp.where(z == 0, 3, z - 1), jnp.where(z == 3, 0, z + 1)]


def line_gather(across, below, above, end, x):
    z = lax.axis_index("ctx")
    return [x, across, jnp.where(z == 0, end, below), jnp.where(z == 3, end, above)]


def add(a, b):
    return (a.astype(F32) + b.astype(F32)).astype(BF)


def pick(x, index, dim=0):
    return lax.dynamic_index_in_dim(x, index, dim, False)


def dp_reduce(parts):
    n = lax.axis_size("dp")
    total = parts[n - 1]
    for k in range(1, n):
        total = add(shift(total, "dp", 1), parts[n - 1 - k])
    return total


def dp_reduce_pair(parts):
    n = lax.axis_size("dp")
    total = parts[n - 1]
    for k in range(1, n - 1):
        total = add(shift(total, "dp", 1), parts[n - 1 - k])
    if n == 1:
        return [total[0], total[1]]
    total = shift(total, "dp", 1)
    return [add(total[0], parts[0][0]), add(total[1], parts[0][1])]


def assemble(found, places):
    found = [t.reshape(-1, *t.shape[-2:]) for t in found]
    each, rows, width = found[0].shape
    count = each * len(found)
    total = count * rows
    if rows % 16:
        blocks = jnp.concatenate(found)
        return jnp.zeros_like(blocks).at[places].set(blocks).reshape(total, width)

    def body(places_ref, *refs):
        refs, out_ref, sems = refs[:-2], refs[-2], refs[-1]
        copies = []
        for i in range(count):
            at = pl.multiple_of(places_ref[i] * rows, rows)
            copies.append(
                pltpu.make_async_copy(refs[i // each].at[i % each], out_ref.at[pl.ds(at, rows), :], sems.at[i])
            )
        for copy in copies:
            copy.start()
        for copy in copies:
            copy.wait()

    return pl.pallas_call(
        body,
        out_shape=jax.ShapeDtypeStruct((total, width), found[0].dtype),
        in_specs=[SM] + [ANY] * len(found),
        out_specs=VM,
        scratch_shapes=[pltpu.SemaphoreType.DMA((count,))],
        compiler_params=params(),
        cost_estimate=cost(0, 4 * total * width),
        name="assemble",
    )(places, *found)


def rms(v):
    return lax.rsqrt(jnp.mean(v * v, axis=-1, keepdims=True) + eps_norm)


def turn(block, cos, sin):
    lane = lax.broadcasted_iota(jnp.int32, block.shape, 1)
    partner = jnp.where(
        (lane & 63) < 32, pltpu.roll(block, 96, 1), pltpu.roll(block, 32, 1)
    )
    return block * cos + partner * sin


def project(toks, gain, w, cos, sin, places):
    rows, d = toks[0].shape
    n = w.shape[1]
    turned = n - 128
    count = len(toks)

    def body(at_ref, gain_ref, w_ref, cos_ref, sin_ref, *refs):
        for i in range(count):
            tok_ref, out_ref = refs[i], refs[count + i]
            at = pl.ds(pl.multiple_of(at_ref[i] * rows, rows), rows)
            cosine, sine = cos_ref[at, :], sin_ref[at, :]
            t = tok_ref[...].astype(F32)
            normed = (t * rms(t) * gain_ref[...]).astype(BF)
            u = mm(normed, w_ref[...])
            for b in range(0, turned, 128):
                out_ref[:, b : b + 128] = turn(u[:, b : b + 128], cosine, sine).astype(BF)
            out_ref[:, turned:] = u[:, turned:].astype(BF)

    return pl.pallas_call(
        body,
        out_shape=[jax.ShapeDtypeStruct((rows, n), BF)] * count,
        in_specs=[SM] + [VM] * (4 + count),
        out_specs=[VM] * count,
        compiler_params=params(),
        cost_estimate=cost(2 * count * rows * d * n, 2 * d * n + 4 * count * rows * d),
        name="project",
    )(places, gain, w, cos, sin, *toks)


def swapped(e):
    return (e & 1) * 2 + (e >> 1)


def split_store(a_ref, b_ref, e, at, value):
    @pl.when(e < 2)
    def _():
        a_ref[(e, *at)] = value

    @pl.when(e >= 2)
    def _():
        b_ref[(e - 2, *at)] = value


def lower_half(shape):
    return lax.broadcasted_iota(jnp.int32, shape, 1) < 64


def stage_heads(block, dst, rows_at, heads, factor):
    rows = block.shape[0]
    low = lower_half((rows, 128))
    for h in range(heads):
        part = block[:, (h // 2) * 128 : (h // 2 + 1) * 128].astype(F32) * factor
        keep = low if h % 2 == 0 else jnp.logical_not(low)
        dst[h, rows_at, :] = jnp.where(keep, part, 0.0).astype(BF)


def doubled(block):
    block = block.astype(F32)
    low = lower_half(block.shape)
    other = pltpu.roll(block, 64, 1)
    return jnp.where(low, block, other), jnp.where(low, other, block)


def allowed_mask(s_ref, keys, rows, first):
    q = lax.broadcasted_iota(jnp.int32, (1, rows), 1) + first
    begin = jnp.zeros_like(q)
    for i in range(5, s_ref.shape[0] - 1):
        begin = jnp.where(q >= s_ref[i], jnp.maximum(begin, s_ref[i]), begin)
    k = lax.broadcasted_iota(jnp.int32, (keys, rows), 0)
    return (k >= begin) & (k <= q)


def attend(scalars, pieces, heads, kvs):
    blocks = len(pieces)
    rows, width = pieces[0].shape
    span = blocks * rows
    qw = heads * HEAD_DIM
    share = heads // kvs

    def body(s_ref, *refs):
        ins, outs, (lse_ref, qs, kd, vd, vt, ob) = refs[:blocks], refs[blocks : 2 * blocks], refs[2 * blocks :]
        me = s_ref[4]
        for k in range(blocks):
            at = pl.ds(pl.multiple_of(s_ref[k] * rows, rows), rows)
            block = ins[k][...]
            stage_heads(block, qs, at, heads, score_scale)
            for i, x in enumerate(doubled(block[:, qw : qw + 128])):
                kd[i, at, :] = x.astype(BF)
            for i, x in enumerate(doubled(block[:, qw + 128 : qw + 256])):
                vd[i, at, :] = x
        for i in range(kvs):
            vt[i] = vd[i].T.astype(BF)

        def one(h, _):
            kv = h // share
            for p in range(blocks):
                keys = (p + 1) * rows
                q = qs[h, p * rows : (p + 1) * rows, :]
                s = mm(kd[kv, :keys, :], q, NT)
                s = jnp.where(allowed_mask(s_ref, keys, rows, p * rows), s, -1e30)
                peak = jnp.max(s, axis=0, keepdims=True)
                e = jnp.exp(s - peak)
                total = jnp.sum(e, axis=0, keepdims=True)
                o = mm(vt[kv, :, :keys], e.astype(BF)) / total
                ob[h, p * rows : (p + 1) * rows, :] = o.T
                lse_ref[pl.ds(h, 1), p * rows : (p + 1) * rows] = peak + jnp.log(total)
            return 0

        def some(i, _):
            for u in range(share):
                one(i * share + u, 0)
            return 0

        lax.fori_loop(0, kvs, some, 0)
        low = lower_half((rows, 128))
        for k in range(blocks):
            at = pl.ds(pl.multiple_of(lax.rem(me + k, blocks) * rows, rows), rows)
            for b in range(heads // 2):
                outs[k][:, b * 128 : (b + 1) * 128] = jnp.where(
                    low, ob[2 * b, at, :], ob[2 * b + 1, at, :]
                ).astype(BF)

    pairs = heads * rows * rows * blocks * (blocks + 1) // 2
    *mixes, lse = pl.pallas_call(
        body,
        out_shape=[jax.ShapeDtypeStruct((rows, qw), BF)] * blocks + [jax.ShapeDtypeStruct((8, span), F32)],
        in_specs=[SM] + [VM] * blocks,
        out_specs=[VM] * (blocks + 1),
        scratch_shapes=[
            pltpu.VMEM((heads, span, 128), BF),
            pltpu.VMEM((kvs, span, 128), BF),
            pltpu.VMEM((kvs, span, 128), F32),
            pltpu.VMEM((kvs, 128, span), BF),
            pltpu.VMEM((heads, span, 128), F32),
        ],
        compiler_params=params(),
        cost_estimate=cost(pairs * 1024, 4 * span * width, pairs),
        name="attend",
    )(scalars, *pieces)
    return mixes, lse


def attend_back(scalars, pieces, grads, lse, cos, sin, heads, kvs):
    blocks = len(pieces)
    rows, width = pieces[0].shape
    span = blocks * rows
    qw = heads * HEAD_DIM
    share = heads // kvs

    def body(s_ref, *refs):
        ins, gins = refs[:blocks], refs[blocks : 2 * blocks]
        lse_ref, cos_ref, sin_ref, out_ref, qs, gs, kd, kf, kt, vd, dk, dv, dq = refs[2 * blocks :]
        me = s_ref[4]
        for k in range(blocks):
            at = pl.ds(pl.multiple_of(s_ref[k] * rows, rows), rows)
            block = ins[k][...]
            stage_heads(block, qs, at, heads, score_scale)
            for i, x in enumerate(doubled(block[:, qw : qw + 128])):
                kd[i, at, :] = x.astype(BF)
                kf[i, at, :] = x
            for i, x in enumerate(doubled(block[:, qw + 128 : qw + 256])):
                vd[i, at, :] = x.astype(BF)
            at = pl.ds(pl.multiple_of(lax.rem(me + k, blocks) * rows, rows), rows)
            stage_heads(gins[k][...], gs, at, heads, 1.0)
        for i in range(kvs):
            kt[i] = kf[i].T.astype(BF)
        dk[...] = jnp.zeros_like(dk)
        dv[...] = jnp.zeros_like(dv)

        def one(h, _):
            kv = h // share
            for p in range(blocks):
                keys = (p + 1) * rows
                at = slice(p * rows, (p + 1) * rows)
                q = qs[h, at, :]
                g = gs[h, at, :]
                s = mm(kd[kv, :keys, :], q, NT)
                log_total = lse_ref[pl.ds(h, 1), at]
                chances = jnp.where(
                    allowed_mask(s_ref, keys, rows, p * rows), jnp.exp(s - log_total), 0.0
                )
                gp = mm(vd[kv, :keys, :], g, NT)
                row_dot = jnp.sum(chances * gp, axis=0, keepdims=True)
                ds = (chances * (gp - row_dot)).astype(BF)
                dq[h, at, :] = mm(kt[kv, :, :keys], ds).T
                dk[kv, :keys, :] += mm(ds, q)
                dv[kv, :keys, :] += mm(chances.astype(BF), g)
            return 0

        for h in range(heads):
            one(h, 0)
        low = lower_half((rows, 128))
        for p in range(blocks):
            at = slice(p * rows, (p + 1) * rows)
            cosine, sine = cos_ref[at, :], -sin_ref[at, :]
            for b in range(heads // 2):
                x = jnp.where(low, dq[2 * b, at, :], dq[2 * b + 1, at, :]) * score_scale
                out_ref[at, b * 128 : (b + 1) * 128] = turn(x, cosine, sine).astype(BF)
            k0, k1, v0, v1 = dk[0, at, :], dk[1, at, :], dv[0, at, :], dv[1, at, :]
            k0, k1 = k0 + pltpu.roll(k0, 64, 1), k1 + pltpu.roll(k1, 64, 1)
            v0, v1 = v0 + pltpu.roll(v0, 64, 1), v1 + pltpu.roll(v1, 64, 1)
            out_ref[at, qw : qw + 128] = turn(jnp.where(low, k0, k1), cosine, sine).astype(BF)
            out_ref[at, qw + 128 : qw + 256] = jnp.where(low, v0, v1).astype(BF)

    pairs = heads * rows * rows * blocks * (blocks + 1) // 2
    return pl.pallas_call(
        body,
        out_shape=jax.ShapeDtypeStruct((span, width), BF),
        in_specs=[SM] + [VM] * (2 * blocks + 3),
        out_specs=VM,
        scratch_shapes=[
            pltpu.VMEM((heads, span, 128), BF),
            pltpu.VMEM((heads, span, 128), BF),
            pltpu.VMEM((kvs, span, 128), BF),
            pltpu.VMEM((kvs, span, 128), F32),
            pltpu.VMEM((kvs, 128, span), BF),
            pltpu.VMEM((kvs, span, 128), BF),
            pltpu.VMEM((kvs, span, 128), F32),
            pltpu.VMEM((kvs, span, 128), F32),
            pltpu.VMEM((heads, span, 128), F32),
        ],
        compiler_params=params(),
        cost_estimate=cost(pairs * 2560, 8 * span * width, pairs),
        name="attend_back",
    )(scalars, *pieces, *grads, lse, cos, sin)


def join(scalars, mixes, w_out, tok, gain):
    blocks = len(mixes)
    rows, part = mixes[0].shape
    d = tok.shape[1]

    def body(s_ref, *refs):
        ins, (w_ref, tok_ref, gain_ref, mid_ref, hid_ref) = refs[:blocks], refs[blocks:]
        me = s_ref[4]
        branch = jnp.zeros((rows, d), F32)
        for k in range(blocks):
            at = pl.ds(pl.multiple_of(lax.rem(me - k + blocks, blocks) * part, part), part)
            branch = branch + mm(ins[k][...], w_ref[at, :])
        middle = tok_ref[...].astype(F32) + residual_scale * branch
        mid_ref[...] = middle
        hid_ref[...] = (middle * rms(middle) * gain_ref[...]).astype(BF)

    return pl.pallas_call(
        body,
        out_shape=(jax.ShapeDtypeStruct((rows, d), F32), jax.ShapeDtypeStruct((rows, d), BF)),
        in_specs=[SM] + [VM] * (blocks + 3),
        out_specs=(VM, VM),
        compiler_params=params(),
        cost_estimate=cost(2 * rows * d * d, 2 * d * d + 10 * rows * d),
        name="join",
    )(scalars, *mixes, w_out, tok, gain)


def join_back(scalars, addends, middle, cot, gain, w_out):
    blocks = 4
    rows, d = middle.shape
    part = d // blocks
    count = len(addends)

    def body(s_ref, *refs):
        ins, (mid_ref, cot_ref, gain_ref, w_ref, gmid_ref, br_ref, gg_ref, *outs) = refs[:count], refs[count:]
        me = s_ref[4]
        grad_hidden = sum(t[...].astype(F32) for t in ins)
        middle = mid_ref[...]
        inv = rms(middle)
        normal = middle * inv
        gg_ref[...] = jnp.sum(grad_hidden * normal, axis=0, keepdims=True)
        u = grad_hidden * gain_ref[...]
        grad_middle = cot_ref[...] + inv * (u - normal * jnp.mean(u * normal, axis=-1, keepdims=True))
        gmid_ref[...] = grad_middle
        br_ref[...] = (residual_scale * grad_middle).astype(BF)
        for k in range(blocks):
            at = pl.ds(pl.multiple_of(lax.rem(me - k + blocks, blocks) * part, part), part)
            outs[k][...] = mm(br_ref[...], w_ref[at, :], NT).astype(BF)

    front = lambda t: pl.BlockSpec((rows, d), lambda i: (0, 0))
    fixed = lambda *shape: pl.BlockSpec(shape, lambda i: (0, 0))
    grad_middle, branch, gain_grad, *mixes = pl.pallas_call(
        body,
        grid=(1,),
        out_shape=[
            jax.ShapeDtypeStruct((rows, d), F32),
            jax.ShapeDtypeStruct((rows, d), BF),
            jax.ShapeDtypeStruct((1, d), F32),
        ]
        + [jax.ShapeDtypeStruct((rows, part), BF)] * blocks,
        in_specs=[SM]
        + [front(t) for t in addends]
        + [fixed(rows, d), fixed(rows, d), fixed(1, d), fixed(d, d)],
        out_specs=[fixed(rows, d), fixed(rows, d), fixed(1, d)] + [fixed(rows, part)] * blocks,
        compiler_params=params(),
        cost_estimate=cost(2 * rows * d * d, 2 * d * d + 18 * rows * d),
        name="join_back",
    )(scalars, *addends, middle, cot, gain, w_out)
    return grad_middle, mixes, branch, gain_grad


def join_weights(scalars, here, branch, mixes, nd, ne):
    blocks = len(mixes)
    rows, part = mixes[0].shape
    d = branch.shape[1]
    w_rows = d // (nd * blocks * ne)

    def body(s_ref, here_ref, br_ref, *refs):
        ins, (gwa_ref, gwb_ref) = refs[:blocks], refs[blocks:]
        me = s_ref[4]
        for k in range(blocks):
            gw = mm(ins[k][...], br_ref[...], TN)
            for i in range(part // w_rows):
                q = lax.rem(me - k + blocks, blocks) * (part // w_rows) + i
                e = swapped(jnp.bitwise_xor(lax.rem(q, ne), here_ref[3]))
                b = lax.div(q, ne)
                m = lax.rem(lax.div(b, blocks) - here_ref[0] + nd, nd)
                put = gw[i * w_rows : (i + 1) * w_rows, :].astype(BF)
                split_store(gwa_ref, gwb_ref, e, (m, lax.rem(b, blocks)), put)

    return pl.pallas_call(
        body,
        out_shape=(jax.ShapeDtypeStruct((2, nd, blocks, w_rows, d), BF),) * 2,
        in_specs=[SM, SM] + [VM] * (1 + blocks),
        out_specs=(VM, VM),
        compiler_params=params(),
        cost_estimate=cost(2 * rows * d * d, 2 * d * d + 4 * rows * d),
        name="join_weights",
    )(scalars, here, branch, *mixes)


def halves(w, odd, devices):
    n, r, width = w.shape
    unit = FF // devices
    if 2 * unit != 128:
        parts = w.reshape(n, r, 2, devices // 4, 2, 2, unit)
        parts = jnp.transpose(parts, (5, 0, 1, 2, 3, 4, 6)).reshape(2, n, r, FF)
        return pick(parts, odd), pick(parts, 1 - odd)

    def body(odd_ref, w_ref, mine_ref, their_ref):
        low = lower_half((r, 128))
        even = odd_ref[0] == 0
        for m in range(width // 256):
            a = w_ref[0, :, 2 * m * 128 : (2 * m + 1) * 128].astype(F32)
            b = w_ref[0, :, (2 * m + 1) * 128 : (2 * m + 2) * 128].astype(F32)
            evens = jnp.where(low, a, pltpu.roll(b, 64, 1))
            odds = jnp.where(low, pltpu.roll(a, 64, 1), b)
            at = slice(m * 128, (m + 1) * 128)
            mine_ref[0, :, at] = jnp.where(even, evens, odds).astype(BF)
            their_ref[0, :, at] = jnp.where(even, odds, evens).astype(BF)

    spec = pl.BlockSpec((1, r, FF), lambda e: (e, 0, 0))
    return pl.pallas_call(
        body,
        grid=(n,),
        out_shape=(jax.ShapeDtypeStruct((n, r, FF), BF),) * 2,
        in_specs=[SM, pl.BlockSpec((1, r, width), lambda e: (e, 0, 0))],
        out_specs=(spec, spec),
        compiler_params=params(),
        cost_estimate=cost(0, 4 * n * r * width),
        name="halves",
    )(odd[None].astype(jnp.int32), w)


def whole(parts, odd, devices):
    count = len(parts)
    _, r, width = parts[0][0].shape
    r3 = r // 3
    unit = FF // devices

    def plain(own, other, theirs):
        total = own.astype(F32) + other.astype(F32)
        theirs = theirs.astype(F32)
        pair = jnp.stack([jnp.where(odd == 0, total[0], theirs), jnp.where(odd == 0, theirs, total[0])])
        pair = pair.reshape(2, r, 2, devices // 4, 2, unit)
        down = [total[2, b * r3 : (b + 1) * r3] for b in range(3)]
        return jnp.transpose(pair, (1, 2, 3, 4, 0, 5)).reshape(r, 2 * width), jnp.concatenate(down, axis=1)

    if 2 * unit != 128:
        done = [plain(*p) for p in parts]
        return jnp.stack([p[0] for p in done]), jnp.stack([p[1] for p in done])

    def body(odd_ref, own_ref, other_ref, their_ref, *refs):
        in_ref, down_ref = refs[-2], refs[-1]
        low = lower_half((r, 128))
        even = odd_ref[0] == 0
        for m in range(width // 128):
            at = slice(m * 128, (m + 1) * 128)
            mine = own_ref[0, :, at].astype(F32) + other_ref[0, :, at].astype(F32)
            their = their_ref[:, at].astype(F32)
            evens, odds = jnp.where(even, mine, their), jnp.where(even, their, mine)
            in_ref[0, :, 2 * m * 128 : (2 * m + 1) * 128] = jnp.where(low, evens, pltpu.roll(odds, 64, 1))
            in_ref[0, :, (2 * m + 1) * 128 : (2 * m + 2) * 128] = jnp.where(
                low, pltpu.roll(evens, 64, 1), odds
            )
        for b in range(3):
            at = slice(b * r3, (b + 1) * r3)
            down_ref[0, :, b * width : (b + 1) * width] = (
                own_ref[2, at, :].astype(F32) + other_ref[2, at, :].astype(F32)
            )

    done = ()
    for e, (own, other, theirs) in enumerate(parts):
        fixed = lambda *shape: pl.BlockSpec(shape, lambda i: (0,) * len(shape))
        done = pl.pallas_call(
            body,
            grid=(1,),
            out_shape=(
                jax.ShapeDtypeStruct((count, r, 2 * width), F32),
                jax.ShapeDtypeStruct((count, r3, 3 * width), F32),
            ),
            in_specs=[SM, fixed(3, r, width), fixed(3, r, width), fixed(r, width)] + [ANY] * len(done),
            out_specs=(
                pl.BlockSpec((1, r, 2 * width), lambda i, e=e: (e, 0, 0)),
                pl.BlockSpec((1, r3, 3 * width), lambda i, e=e: (e, 0, 0)),
            ),
            input_output_aliases={4: 0, 5: 1} if done else {},
            compiler_params=params(),
            cost_estimate=cost(0, 20 * r * width),
            name="whole",
        )(odd[None].astype(jnp.int32), own, other, theirs, *done)
    return done


def experts_rows(places, which, rows_in, cots, shards, sums, last):
    piece, d = rows_in[0].shape
    group = 1
    rows = piece * group
    tiles = len(rows_in) // group
    total = rows * tiles
    count, n = len(shards), len(shards[0])
    r, width = shards[0][0][0].shape[-2:]
    arrays = {id(t): t for shard in shards for t, _ in shard}
    slot = {key: k for k, key in enumerate(arrays)}
    arrays = list(arrays.values())
    half = width // 2
    r3 = r // 3
    first = sums is None

    def body(places_ref, *refs):
        n_in = tiles * group
        h_refs, c_refs, refs = refs[:n_in], refs[n_in : 2 * n_in], refs[2 * n_in :]
        w_refs, refs = refs[: len(arrays)], refs[len(arrays) :]
        if not first:
            in_h, in_o, refs = refs[0], refs[1], refs[2:]
        if last:
            out_h, rest_h, out_o, rest_o, gb_ref, gat_ref, *refs = refs
        else:
            out_h, out_o, gb_ref, gat_ref, *refs = refs
        if first:
            ht_ref, *refs = refs
        wiv, wdv, ga_ref, hv, cv, sems, row_sems = refs
        t = pl.program_id(0)
        moves = []
        for i in range(n_in):
            at = pl.ds(i % group * piece, piece)
            moves.append(
                (
                    pltpu.make_async_copy(h_refs[i], hv.at[i // group, at, :], row_sems.at[0, i]),
                    pltpu.make_async_copy(c_refs[i], cv.at[i // group, at, :], row_sems.at[1, i]),
                )
            )

        @pl.when(t == 0)
        def _():
            copies = []
            for i in range(count):
                for e in range(n):
                    array, which_of = shards[i][e]
                    source = w_refs[slot[id(array)]]
                    source = source if which_of is None else source.at[which_of]
                    parts = []
                    for b in range(2):
                        at = pl.multiple_of(places_ref[3 * i + b] * r, r)
                        parts.append((source.at[2 * b], wiv.at[pl.ds(at, r), e * width : (e + 1) * width]))
                    at = pl.multiple_of(places_ref[3 * i + 2] * r3 + e * half, r3)
                    for b in range(3):
                        parts.append(
                            (
                                source.at[1, b * r3 : (b + 1) * r3, :],
                                wdv.at[pl.ds(at, r3), b * width : (b + 1) * width],
                            )
                        )
                    for k, (a, b) in enumerate(parts):
                        copies.append(pltpu.make_async_copy(a, b, sems.at[i, e, k]))
            for copy in copies:
                copy.start()
            for a, b in moves[:group]:
                a.start()
                b.start()
            for copy in copies:
                copy.wait()
            for a, b in moves[group:]:
                a.start()
                b.start()

        for i in range(tiles):

            @pl.when(t == i)
            def _():
                for a, b in moves[i * group : (i + 1) * group]:
                    a.wait()
                    b.wait()

        h = hv[t]
        c = cv[t, :, :d]
        gates = cv[t, :, d:].astype(F32)
        lane = lax.broadcasted_iota(jnp.int32, gates.shape, 1) - places_ref[3 * count]
        for e in range(n):
            g = jnp.sum(jnp.where(lane == which + e, gates, 0.0), axis=1, keepdims=True)
            gu = mm(h, wiv[:, e * width : (e + 1) * width])
            gate, up = gu[:, :half], gu[:, half:]
            sg = jax.nn.sigmoid(gate)
            silu = gate * sg
            ga = mm(c, wdv[e * half : (e + 1) * half, :], NT) * g
            ga_ref[:, e * half : (e + 1) * half] = (silu * up * g).astype(BF)
            gb_ref[:, e * width : e * width + half] = (ga * up * (sg + silu * (1.0 - sg))).astype(BF)
            gb_ref[:, e * width + half : (e + 1) * width] = (ga * silu).astype(BF)
        o = mm(ga_ref[...], wdv[...])
        gh = mm(gb_ref[...], wiv[...], NT)
        gat_ref[...] = ga_ref[...].T
        if first:
            ht_ref[...] = h.T
        if not first:
            o = o + in_o[...].astype(F32)
            gh = gh + in_h[...].astype(F32)
        if last:

            @pl.when(t < tiles // 2)
            def _():
                out_o[...] = o.astype(BF)
                out_h[...] = gh.astype(BF)

            @pl.when(t >= tiles // 2)
            def _():
                rest_o[...] = o.astype(BF)
                rest_h[...] = gh.astype(BF)

        else:
            out_o[...] = o.astype(BF)
            out_h[...] = gh.astype(BF)

    tile = lambda c: pl.BlockSpec((rows, c), lambda t: (t, 0))
    flat = lambda c: pl.BlockSpec((c, rows), lambda t: (0, t))
    if last:
        sum_shapes = (jax.ShapeDtypeStruct((total // 2, d), BF),) * 4
        front = pl.BlockSpec((rows, d), lambda t: (jnp.minimum(t, tiles // 2 - 1), 0))
        back = pl.BlockSpec((rows, d), lambda t: (jnp.maximum(t - tiles // 2, 0), 0))
        sum_specs = (front, back, front, back)
    else:
        sum_shapes = (jax.ShapeDtypeStruct((total, d), BF),) * 2
        sum_specs = (tile(d), tile(d))
    return pl.pallas_call(
        body,
        grid=(tiles,),
        out_shape=sum_shapes
        + (
            jax.ShapeDtypeStruct((total, n * width), BF),
            jax.ShapeDtypeStruct((n * half, total), BF),
        )
        + ((jax.ShapeDtypeStruct((d, total), BF),) if first else ()),
        in_specs=[SM]
        + [ANY] * (2 * len(rows_in) + len(arrays))
        + ([] if first else [tile(d), tile(d)]),
        out_specs=sum_specs + (tile(n * width), flat(n * half)) + ((flat(d),) if first else ()),
        scratch_shapes=[
            pltpu.VMEM((d, n * width), BF),
            pltpu.VMEM((n * half, d), BF),
            pltpu.VMEM((rows, n * half), BF),
            pltpu.VMEM((tiles, rows, d), BF),
            pltpu.VMEM((tiles, rows, cots[0].shape[1]), BF),
            pltpu.SemaphoreType.DMA((count, n, 5)),
            pltpu.SemaphoreType.DMA((2, len(rows_in))),
        ],
        compiler_params=params(),
        cost_estimate=cost(6 * n * total * d * width, 50e6, n * total * half),
        name="experts_rows",
    )(places, *rows_in, *cots, *arrays, *(() if first else sums))


def experts_weights(scalars, rows_t, cots, gb, ga_t, n, devices):
    d, total = rows_t.shape
    width, half = gb.shape[1] // n, ga_t.shape[0] // n
    r = d // devices
    r3 = r // 3
    nd = devices // 4
    tiles = len(cots)
    rows = total // tiles

    def body(s_ref, h_any, gb_any, ga_any, *refs):
        c_refs, refs = refs[:tiles], refs[tiles:]
        outs, (down, h_ref, gb_ref, ga_ref, c_ref, stage, sems, c_sems, out_sems) = refs[: n * nd], refs[n * nd :]
        ahead = [lax.rem(s_ref[0] + k, nd) for k in range(nd)]
        spans = [pl.ds(pl.multiple_of(x * 4 * r, 4 * r), 4 * r) for x in ahead]
        first = [pltpu.make_async_copy(gb_any, gb_ref, sems.at[0])]
        first += [
            pltpu.make_async_copy(h_any.at[spans[k], :], h_ref.at[k], sems.at[1 + k]) for k in range(nd)
        ]
        second = [pltpu.make_async_copy(ga_any, ga_ref, c_sems.at[tiles])]
        second += [
            pltpu.make_async_copy(c_refs[i].at[:, :d], c_ref.at[pl.ds(i * rows, rows), :], c_sems.at[i])
            for i in range(tiles)
        ]
        for copy in first[:2]:
            copy.start()
        first[0].wait()
        for k in range(nd):
            first[1 + k].wait()
            for copy in first[2:] + second if k == 0 else []:
                copy.start()
            part = mm(h_ref[k], gb_ref[...]).astype(BF)
            for z in range(4):
                where = jnp.bitwise_xor(s_ref[2], z // 2)
                slot = jnp.bitwise_xor(s_ref[1], z % 2)
                for e in range(n):
                    stage[e * nd + k, where, slot] = part[z * r : (z + 1) * r, e * width : (e + 1) * width]
        for copy in second:
            copy.wait()
        leaving = []
        for e in range(n):
            down[...] = mm(ga_ref[e * half : (e + 1) * half, :], c_ref[...]).astype(BF)
            for k in range(nd):
                for z in range(2):
                    where = jnp.bitwise_xor(s_ref[2], z)
                    at = pl.ds(pl.multiple_of((2 * ahead[k] + z) * r3, r3), r3)
                    for b in range(3):
                        stage[e * nd + k, where, 2, b * r3 : (b + 1) * r3, :] = down[
                            at, b * width : (b + 1) * width
                        ]
                leaving.append(
                    pltpu.make_async_copy(stage.at[e * nd + k], outs[e * nd + k], out_sems.at[e * nd + k])
                )
                leaving[-1].start()
        for copy in leaving:
            copy.wait()

    outs = pl.pallas_call(
        body,
        out_shape=[jax.ShapeDtypeStruct((2, 3, r, width), BF)] * (n * nd),
        in_specs=[SM] + [ANY] * (3 + tiles),
        out_specs=[ANY] * (n * nd),
        scratch_shapes=[
            pltpu.VMEM((half, d), BF),
            pltpu.VMEM((nd, 4 * r, total), BF),
            pltpu.VMEM((total, n * width), BF),
            pltpu.VMEM((n * half, total), BF),
            pltpu.VMEM((total, d), BF),
            pltpu.VMEM((n * nd, 2, 3, r, width), BF),
            pltpu.SemaphoreType.DMA((1 + nd,)),
            pltpu.SemaphoreType.DMA((tiles + 1,)),
            pltpu.SemaphoreType.DMA((n * nd,)),
        ],
        compiler_params=params(),
        cost_estimate=cost(3 * n * total * d * width, 20e6),
        name="experts_weights",
    )(scalars, rows_t, gb, ga_t, *cots)
    return [outs[e * nd : (e + 1) * nd] for e in range(n)]


def finish(scalars, dqkv, w, blocks):
    total, width = dqkv.shape
    d = w.shape[0]
    rows = total // blocks

    def body(s_ref, dq_ref, w_ref, *outs):
        for k in range(blocks):
            at = lax.rem(s_ref[4] - 1 - k + 2 * blocks, blocks)
            at = pl.ds(pl.multiple_of(at * rows, rows), rows)
            outs[k][...] = mm(dq_ref[at, :], w_ref[...], NT).astype(BF)

    return pl.pallas_call(
        body,
        out_shape=[jax.ShapeDtypeStruct((rows, d), BF)] * blocks,
        in_specs=[SM, VM, VM],
        out_specs=[VM] * blocks,
        compiler_params=params(),
        cost_estimate=cost(2 * total * d * width, 4 * total * d),
        name="finish",
    )(scalars, dqkv, w)


def finish_weights(scalars, here, dqkv, gn, toks, gain, gain_grad, nd, ne):
    blocks = len(toks)
    rows, d = toks[0].shape
    width = dqkv.shape[1]
    w_rows = d // (nd * blocks * ne)

    def body(s_ref, here_ref, dq_ref, gain_ref, gg_ref, *refs):
        ins, gns, (gwa_ref, gwb_ref, acc) = refs[:blocks], refs[blocks : 2 * blocks], refs[2 * blocks :]
        gg = jnp.zeros((1, d), F32)
        for k in range(blocks):
            to = s_ref[k]
            at = pl.ds(pl.multiple_of(to * rows, rows), rows)
            t = ins[k][...].astype(F32)
            normal = t * rms(t)
            normed = (normal * gain_ref[...]).astype(BF)
            gn = gns[(k - 1) % blocks][...].astype(F32)
            gg = gg + jnp.sum(gn * normal, axis=0, keepdims=True)
            part = mm(normed, dq_ref[at, :], TN)
            acc[...] = part if k == 0 else acc[...] + part
        row = lax.broadcasted_iota(jnp.int32, (128, d), 0)
        both = jnp.where(row == 0, gg, jnp.where(row == 1, gg_ref[...], 0.0)).T
        for q in range(d // w_rows):
            e = swapped(jnp.bitwise_xor(q % ne, here_ref[3]))
            m = lax.rem(q // ne // blocks - here_ref[0] + nd, nd)
            at = slice(q * w_rows, (q + 1) * w_rows)
            put = jnp.concatenate([acc[at, :], both[at, :]], axis=1).astype(BF)
            split_store(gwa_ref, gwb_ref, e, (m, q // ne % blocks), put)

    return pl.pallas_call(
        body,
        out_shape=(jax.ShapeDtypeStruct((2, nd, blocks, w_rows, width + 128), BF),) * 2,
        in_specs=[SM, SM] + [VM] * (3 + 2 * blocks),
        out_specs=(VM, VM),
        scratch_shapes=[pltpu.VMEM((d, width), F32)],
        compiler_params=params(),
        cost_estimate=cost(2 * blocks * rows * d * width, 6 * blocks * rows * d),
        name="finish_weights",
    )(scalars, here, dqkv, gain, gain_grad, *toks, *gn)


def per_device(
    tokens,
    gain_attn,
    w_query,
    w_key,
    w_value,
    w_out,
    gain_moe,
    w_in,
    w_down,
    routes,
    gates,
    lengths,
    cotangent,
):
    nd, nz, ne = lax.axis_size("dp"), lax.axis_size("ctx"), lax.axis_size("exp")
    x, z, j = lax.axis_index("dp"), lax.axis_index("ctx"), lax.axis_index("exp")
    rows, d = tokens.shape[1:]
    span = rows * nz
    w_rows = w_query.shape[0]
    heads, kvs = HEADS // nz, KV_HEADS // nz
    qw, kw = heads * HEAD_DIM, kvs * HEAD_DIM
    local_experts = w_in.shape[0]
    experts = local_experts * ne
    i32 = jnp.int32
    mod = lambda v, n: lax.rem(v + 8 * n, n)

    ends = jnp.cumsum(lengths[0]).astype(i32)
    places = [mod(z - k, nz) for k in range(nz)]
    scalars = jnp.concatenate([jnp.stack(places + [z]).astype(i32), ends])
    place = jnp.arange(span, dtype=i32)
    place = place - jnp.max(jnp.where(place[:, None] >= ends[None, :-1], ends[None, :-1], 0), axis=1)
    lane = jnp.arange(128, dtype=i32)
    half = HEAD_DIM // 2
    frequency = rope_base ** (-2.0 * jnp.arange(half, dtype=F32) / HEAD_DIM)
    angles = place.astype(F32)[:, None] * frequency[None, :]
    cos = jnp.tile(jnp.cos(angles), (1, 128 // half))
    sin = jnp.tile(jnp.sin(angles), (1, 128 // half)) * jnp.where((lane & 63) < 32, -1.0, 1.0)[None, :]

    run = Stages(gain_attn)
    gain_a, gain_m = gain_attn[None, :], gain_moe[None, :]
    devices = nd * nz
    odd, zh = jnp.bitwise_and(z, 1), z // 2
    batch = local_experts // 2
    tok, cot = tokens[0], cotangent[0]
    flip_e = lambda v, e: flip(v, "exp", e)

    def row_blocks(found, owners, order):
        at = [
            (mod(x - m, nd) * nz + p) * ne + jnp.bitwise_xor(j, e + 2 * b)
            for e in (0, 1) for b, m in order for p in owners
        ]
        return assemble(found, jnp.stack(at).astype(i32))

    by_m = [(b, m) for m in range(nd) for b in (0, 1)]
    by_b = [(b, m) for b in (0, 1) for m in range(nd)]

    here = jnp.stack([x, odd, zh, j]).astype(i32)

    parts = [
        jnp.concatenate(
            [
                w_query[:, p * qw : (p + 1) * qw],
                w_key[:, p * kw : (p + 1) * kw],
                w_value[:, p * kw : (p + 1) * kw],
            ],
            axis=1,
        )
        for p in range(nz)
    ]
    cut = rows // 2
    toks = [tok, shift(tok, "ctx", 1)]
    w_parts = jnp.stack(parts)
    w_mine = [pick(w_parts, z)] + [shift(pick(w_parts, mod(z + k, nz)), "ctx", k) for k in range(1, nz)]
    run.end(toks, w_mine)

    half_2 = [shift(run.hold(toks[1])[:cut], "ctx", 1)]
    mine_in, their_in = halves(run.hold(w_in), odd, devices)
    down = run.hold(w_down)
    down = jnp.concatenate([down[:, :, b * FF : (b + 1) * FF] for b in range(d // FF)], axis=1)
    w_mine = jnp.stack(w_mine)
    w_mine = jnp.stack([w_mine, flip_e(run.hold(w_mine), 2)])
    line = [hop(run.hold(w_out), pairs) for pairs in (ACROSS, UP, DOWN)]
    run.end(half_2, w_mine, line, mine_in)

    half_2.append(shift(run.hold(toks[1])[cut:], "ctx", 1))
    hits = run.hold(routes)[0][:, :, None] == jnp.arange(128, dtype=i32)[None, None, :]
    dense = jnp.sum(jnp.where(hits, gates[0].astype(F32)[:, :, None], 0.0), axis=1).astype(BF)
    cot_b = jnp.concatenate([(residual_scale * run.hold(cot)).astype(BF), dense], axis=1)
    w_found = ring(run.hold(w_mine), "dp")
    line_end = hop(run.hold(line[0]), OUTER)
    run.end(half_2, w_found, line_end, cot_b)

    toks.append(jnp.concatenate(half_2))
    toks.append(shift(run.hold(toks[2]), "ctx", 1))
    got_1 = flip(run.hold(their_in[:batch]), "ctx", 1)
    w_found = w_found + [flip_e(t, 1) for t in run.hold(w_found)]
    w_line = ring(run.hold(jnp.stack(line_gather(*line, line_end, w_out))), "dp")
    cot_2 = flip_e(run.hold(cot_b), 2)
    w_qkv = row_blocks(w_found, places, by_m)
    at = jnp.stack(places).astype(i32)
    pieces = project(toks[: nz - 1], gain_a, w_qkv, cos, sin, at[: nz - 1])
    run.end(toks, pieces, got_1, w_line, cot_2)

    packet = lambda e, got: jnp.stack([mine_in[e], down[e], got[e % batch]])
    near = [packet(e, got_1) for e in range(batch)]
    far = [flip(run.hold(near[0]), "ctx", 2)]
    own = [ring(run.hold(jnp.stack(near)), "dp")]
    w_line = jnp.stack(w_line)
    w_line = jnp.stack([w_line, flip_e(run.hold(w_line), 2)])
    cot_n = flip(run.hold(cot_b), "ctx", 1)
    pieces = pieces + project([run.hold(toks[3])], gain_a, w_qkv, cos, sin, at[nz - 1 :])
    mix_out, lse = attend(scalars, pieces, heads, kvs)
    run.end(far, own, w_line, cot_n, mix_out)

    mixes = run.hold(mix_out)
    mixes = [mixes[0]] + [shift(mixes[k], "ctx", k) for k in range(1, nz)]
    w_line = [w_line, flip_e(run.hold(w_line), 1)]
    cot_n2 = flip_e(run.hold(cot_n), 2)
    w_out_all = row_blocks(w_line, line_places(z), by_b)
    run.end(mixes, w_out_all, cot_n2)

    cot_1 = flip_e(run.hold(cot_b), 1)
    cot_n1, cot_n3 = flip_e(run.hold(cot_n), 1), flip_e(run.hold(cot_n2), 1)
    got_2 = flip(run.hold(their_in[batch:]), "ctx", 1)
    over = [ring(run.hold(far[0]), "dp")]
    middle, hidden = join(scalars, run.hold(mixes), w_out_all, tok, gain_m)
    run.end(hidden, got_2, over, cot_1, cot_n1, cot_n3)

    hidden_2, hidden_n = flip_e(run.hold(hidden), 2), flip(run.hold(hidden), "ctx", 1)
    far += [flip(run.hold(near[e]), "ctx", 2) for e in range(1, batch)]
    near.append(packet(batch, got_2))
    own.append(ring(run.hold(near[batch]), "dp"))
    hidden_1 = flip_e(run.hold(hidden), 1)
    run.end(hidden_1, hidden_2, hidden_n, far, own)

    hidden_n2 = flip_e(run.hold(hidden_n), 2)
    hidden_n1, hidden_3 = flip_e(run.hold(hidden_n), 1), flip_e(run.hold(hidden_2), 1)
    over += [ring(run.hold(far[e]), "dp") for e in range(1, batch)]
    far.append(flip(run.hold(near[batch]), "ctx", 2))
    near += [packet(e, run.hold(got_2)) for e in range(batch + 1, local_experts)]
    run.end(hidden_n1, hidden_3, hidden_n2, over, far, near)

    rows_in = [hidden, hidden_n, hidden_2, hidden_n2, hidden_1, hidden_n1, hidden_3, None]
    cots = [cot_b, cot_n, cot_2, cot_n2, cot_1, cot_n1, None, cot_n3]
    w_at = []
    for zc in (z, jnp.bitwise_xor(z, 2)):
        for m in range(nd):
            xc = mod(x - m, nd)
            w_at += [xc * nz + zc, xc * nz + jnp.bitwise_xor(zc, 1), xc * 2 + zc // 2]
    w_at = jnp.stack(w_at + [j * local_experts]).astype(i32)
    rows_in = run.hold(rows_in[:-1]) + [flip_e(run.hold(hidden_n2), 1)]
    cots[6] = flip_e(run.hold(cot_2), 1)
    own += [ring(run.hold(near[e]), "dp") for e in range(batch + 1, local_experts)]
    far += [flip(run.hold(near[e]), "ctx", 2) for e in range(batch + 1, local_experts)]
    over.append(ring(run.hold(far[batch]), "dp"))
    shards = [[(t, e) for e in range(batch)] for t in own[0]]
    shards += [[(t, None) for t in some] for some in zip(*over[:batch])]
    sum_h, sum_o, gb, ga_t, rows_t = experts_rows(w_at, 0, rows_in, cots, shards, None, False)
    run.end(far, own, over, sum_h)

    over += [ring(run.hold(far[e]), "dp") for e in range(batch + 1, local_experts)]
    gw_1 = experts_weights(here, rows_t, cots, run.hold(gb), ga_t, batch, devices)
    run.end(over, gw_1)

    x_0 = dp_reduce_pair(run.hold(gw_1[0]))
    shards = [[(t, None) for t in some] for some in zip(*own[1:])]
    shards += [[(t, None) for t in some] for some in zip(*over[batch:])]
    sum_h, rest_h, sum_o, rest_o, gb, ga_t = experts_rows(
        w_at, batch, run.hold(rows_in), cots, shards, (sum_h, sum_o), True
    )
    run.end(x_0, sum_h)

    rest_h = flip_e(run.hold(rest_h), 1)
    run.end(rest_h)

    part = rows // 2
    all_h = sum_h
    sum_h = [
        add(sum_h[a * part : b * part], rest_h[a * part : b * part])
        for a, b in ((2, 3), (3, 4), (4, 5), (5, 6), (6, 7), (7, 8))
    ]
    by_y, by_z = flip_e(run.hold(sum_h[4]), 2), flip(run.hold(sum_h[5]), "ctx", 1)
    z_0 = flip(run.hold(x_0[1]), "ctx", 2)
    x_1 = dp_reduce_pair(run.hold(gw_1[1]))
    rest_o = flip_e(run.hold(rest_o), 1)
    gw_2 = experts_weights(here, rows_t, cots, run.hold(gb), ga_t, batch, devices)
    run.end(by_y, by_z, z_0, x_1, rest_o, gw_2)

    near_h = flip_e(jnp.concatenate([sum_h[2], add(run.hold(sum_h[3]), by_z)]), 2)
    other_h = flip(jnp.concatenate([add(run.hold(sum_h[0]), by_y), sum_h[1]]), "ctx", 1)
    z_1 = flip(run.hold(x_1[1]), "ctx", 2)
    x_2 = dp_reduce_pair(run.hold(gw_2[0]))
    sum_o = [add(sum_o[a * rows : (a + 1) * rows], rest_o[a * rows : (a + 1) * rows]) for a in range(4)]
    run.end(near_h, other_h, z_1, x_2, sum_o)

    grad_middle, grad_mix, branch, grad_gain_m = join_back(
        scalars, [all_h, rest_h, *run.hold([near_h, other_h])], middle, cot, gain_m, w_out_all
    )
    grad_mixes = [grad_mix[0]] + [shift(grad_mix[k], "ctx", -k) for k in range(1, nz)]
    x_3 = dp_reduce_pair(run.hold(gw_2[1]))
    far_o1 = flip_e(run.hold(sum_o[3]), 2)
    wo_a, wo_b = join_weights(scalars, here, branch, mixes, nd, ne)
    ready = lax.optimization_barrier((x_0[0], x_1[0], branch))
    swap = jnp.stack([add(ready[0][1], z_0[1]), add(ready[1][1], z_1[1])])
    run.end(grad_mixes, x_3, far_o1, wo_b, swap)

    z_2 = flip(run.hold(x_2[1]), "ctx", 2)
    far_o = flip_e(run.hold(sum_o[2]), 2)
    other_o = flip(add(sum_o[1], run.hold(far_o1)), "ctx", 1)
    wo_b = flip_e(run.hold(wo_b), 1)
    dqkv = attend_back(scalars, pieces, run.hold(grad_mixes), lse, cos, sin, heads, kvs)
    grad_normed = finish(scalars, dqkv, w_qkv, nz)
    run.end(z_2, far_o, other_o, wo_b, grad_normed)

    z_3 = flip(run.hold(x_3[1]), "ctx", 2)
    gw_a, gw_b = finish_weights(scalars, here, dqkv, run.hold(grad_normed), toks, gain_a, grad_gain_m, nd, ne)
    swap = flip(run.hold(swap), "ctx", 1)
    swap_2 = flip(add(run.hold(x_2[0])[1], z_2[1]), "ctx", 1)
    wo_b = run.hold(wo_b)
    wo_far = flip_e(add(wo_a[1], wo_b[1]), 2)
    run.end(gw_b, swap, swap_2, wo_far, z_3)

    tail = run.hold(grad_normed)
    total = shift(tail[0], "ctx", 1)
    gw_b = flip_e(run.hold(gw_b), 1)
    gw = add(gw_a, gw_b)
    wo_b, wo_far = run.hold([wo_b, wo_far])
    wo = (wo_a[0].astype(F32) + wo_b[0].astype(F32) + wo_far.astype(F32)).astype(BF)
    run.end(total, gw, wo)

    total = shift(add(run.hold(total), tail[1]), "ctx", 1)
    gw_far = flip_e(run.hold(gw[1]), 2)
    wo = dp_reduce(list(run.hold(wo)))
    gw = add(gw[0], gw_far)
    run.end(total, gw, wo)

    total = shift(add(run.hold(total), tail[2]), "ctx", 1)
    gw = dp_reduce(list(run.hold(gw)))
    run.end(total, gw)

    swap_3 = flip(add(run.hold(x_3[0])[1], z_3[1]), "ctx", 1)
    mine = jnp.concatenate(run.hold([gw, wo]), axis=2)
    parts = [pick(mine, z)] + [shift(pick(mine, mod(z + k, nz)), "ctx", k) for k in range(1, nz)]

    gn = tail[3].astype(F32) + total.astype(F32)
    expert_sum = sum_o[0].astype(F32) + far_o.astype(F32) + other_o.astype(F32)
    mixed_out = (middle + residual_scale * expert_sum).astype(BF)
    q_end, k_end, v_end = qw, qw + kw, qw + 2 * kw
    gains = sum(p[:, v_end : v_end + 2].astype(F32) for p in parts)
    grad_out = sum(p[:, v_end + 128 :].astype(F32) for p in parts)
    order = jnp.stack([p[:, :v_end] for p in parts])
    order = [pick(order, mod(z - p, nz)).astype(F32) for p in range(nz)]
    grad_query = jnp.concatenate([g[:, :q_end] for g in order], axis=1)
    grad_key = jnp.concatenate([g[:, q_end:k_end] for g in order], axis=1)
    grad_value = jnp.concatenate([g[:, k_end:] for g in order], axis=1)

    grads_in, grads_down = whole(
        [
            (x_0[0], z_0, swap[0]), (x_1[0], z_1, swap[1]), (x_2[0], z_2, swap_2), (x_3[0], z_3, swap_3)
        ],
        odd,
        devices,
    )

    t = tok.astype(F32)
    inv = rms(t)
    normal = t * inv
    u = gn * gain_a
    grad_tokens = grad_middle + inv * (u - normal * jnp.mean(u * normal, axis=-1, keepdims=True))
    return (
        mixed_out[None],
        grad_tokens[None],
        gains[:, 0],
        grad_query,
        grad_key,
        grad_value,
        grad_out.astype(F32),
        gains[:, 1],
        grads_in,
        grads_down,
    )


def solution(mesh):
    every = ("dp", "ctx", "exp")
    return jax.shard_map(
        per_device,
        mesh=mesh,
        in_specs=(
            P(("dp", "exp"), "ctx", None),
            P(),
            P(every, None),
            P(every, None),
            P(every, None),
            P(every, None),
            P(),
            P("exp", ("dp", "ctx"), None),
            P("exp", ("dp", "ctx"), None),
            P(("dp", "exp"), "ctx", None),
            P(("dp", "exp"), "ctx", None),
            P(("dp", "exp"), None),
            P(("dp", "exp"), "ctx", None),
        ),
        out_specs=(
            P(("dp", "exp"), "ctx", None),
            P(("dp", "exp"), "ctx", None),
            P(every),
            P(every, None),
            P(every, None),
            P(every, None),
            P(every, None),
            P(every),
            P("exp", ("dp", "ctx"), None),
            P("exp", ("dp", "ctx"), None),
        ),
        check_vma=False,
    )
```

```python
import functools

import jax
import jax.numpy as jnp
from jax import lax
from jax.experimental import pallas as pl
from jax.experimental.pallas import tpu as pltpu
from jax.sharding import PartitionSpec as P

HEADS = 24
KV_HEADS = 8
HEAD_DIM = 64
FF = 512
TOP = 8

eps_norm = 1e-06
score_scale = 0.015625
residual_scale = 0.22
rope_base = 10000.0

BF = jnp.bfloat16
F32 = jnp.float32
SCALE = 3
VMEM_LIMIT = 60 * 1024 * 1024
ANY = pl.BlockSpec(memory_space=pl.ANY)
VM = pl.BlockSpec(memory_space=pltpu.VMEM)
SM = pl.BlockSpec(memory_space=pltpu.SMEM)
NN = (((1,), (0,)), ((), ()))
NT = (((1,), (1,)), ((), ()))
TN = (((0,), (0,)), ((), ()))


def mm(a, b, dims=NN):
    return lax.dot_general(a, b, dims, preferred_element_type=F32)


def params(**kw):
    return pltpu.CompilerParams(vmem_limit_bytes=VMEM_LIMIT, **kw)


def cost(flops, nbytes, trans=0):
    return pl.CostEstimate(
        flops=int(flops / SCALE), bytes_accessed=int(nbytes / SCALE), transcendentals=0
    )


def shift(x, axis, by):
    n = lax.axis_size(axis)
    return lax.ppermute(x, axis, [(i, (i + by) % n) for i in range(n)])


def flip(x, axis, mask):
    n = lax.axis_size(axis)
    return lax.ppermute(x, axis, [(i, i ^ mask) for i in range(n)])


class Stages:
    def __init__(self, token):
        self.token = token

    def hold(self, x):
        leaves, tree = jax.tree.flatten(x)
        leaves = [lax.optimization_barrier((leaf, self.token))[0] for leaf in leaves]
        return jax.tree.unflatten(tree, leaves)

    def end(self, *outs):
        self.token = lax.optimization_barrier((self.token, *jax.tree.leaves(outs)))[0]


def ring(x, axis):
    out = [x]
    for _ in range(lax.axis_size(axis) - 1):
        out.append(shift(out[-1], axis, 1))
    return out


def hop(x, pairs):
    return lax.ppermute(x, "ctx", pairs)


UP, DOWN = [(0, 1), (1, 2), (2, 3)], [(1, 0), (2, 1), (3, 2)]
ACROSS = [(0, 2), (1, 3), (2, 0), (3, 1)]
INNER, OUTER = [(0, 1), (3, 2)], [(1, 0), (2, 3)]


def line_places(z):
    return [z, jnp.bitwise_xor(z, 2), jnp.where(z == 0, 3, z - 1), jnp.where(z == 3, 0, z + 1)]


def line_gather(across, below, above, end, x):
    z = lax.axis_index("ctx")
    return [x, across, jnp.where(z == 0, end, below), jnp.where(z == 3, end, above)]


def add(a, b):
    return (a.astype(F32) + b.astype(F32)).astype(BF)


def pick(x, index, dim=0):
    return lax.dynamic_index_in_dim(x, index, dim, False)


def dp_reduce(parts):
    n = lax.axis_size("dp")
    total = parts[n - 1]
    for k in range(1, n):
        total = add(shift(total, "dp", 1), parts[n - 1 - k])
    return total


def dp_reduce_pair(parts):
    n = lax.axis_size("dp")
    total = parts[n - 1]
    for k in range(1, n - 1):
        total = add(shift(total, "dp", 1), parts[n - 1 - k])
    if n == 1:
        return [total[0], total[1]]
    total = shift(total, "dp", 1)
    return [add(total[0], parts[0][0]), add(total[1], parts[0][1])]


def assemble(found, places):
    found = [t.reshape(-1, *t.shape[-2:]) for t in found]
    each, rows, width = found[0].shape
    count = each * len(found)
    total = count * rows
    if rows % 16:
        blocks = jnp.concatenate(found)
        return jnp.zeros_like(blocks).at[places].set(blocks).reshape(total, width)

    def body(places_ref, *refs):
        refs, out_ref, sems = refs[:-2], refs[-2], refs[-1]
        copies = []
        for i in range(count):
            at = pl.multiple_of(places_ref[i] * rows, rows)
            copies.append(
                pltpu.make_async_copy(refs[i // each].at[i % each], out_ref.at[pl.ds(at, rows), :], sems.at[i])
            )
        for copy in copies:
            copy.start()
        for copy in copies:
            copy.wait()

    return pl.pallas_call(
        body,
        out_shape=jax.ShapeDtypeStruct((total, width), found[0].dtype),
        in_specs=[SM] + [ANY] * len(found),
        out_specs=VM,
        scratch_shapes=[pltpu.SemaphoreType.DMA((count,))],
        compiler_params=params(),
        cost_estimate=cost(0, 4 * total * width),
        name="assemble",
    )(places, *found)


def rms(v):
    return lax.rsqrt(jnp.mean(v * v, axis=-1, keepdims=True) + eps_norm)


def turn(block, cos, sin):
    lane = lax.broadcasted_iota(jnp.int32, block.shape, 1)
    partner = jnp.where(
        (lane & 63) < 32, pltpu.roll(block, 96, 1), pltpu.roll(block, 32, 1)
    )
    return block * cos + partner * sin


def project(toks, gain, w, cos, sin, places):
    rows, d = toks[0].shape
    n = w.shape[1]
    turned = n - 128
    count = len(toks)

    def body(at_ref, gain_ref, w_ref, cos_ref, sin_ref, *refs):
        for i in range(count):
            tok_ref, out_ref = refs[i], refs[count + i]
            at = pl.ds(pl.multiple_of(at_ref[i] * rows, rows), rows)
            cosine, sine = cos_ref[at, :], sin_ref[at, :]
            t = tok_ref[...].astype(F32)
            normed = (t * rms(t) * gain_ref[...]).astype(BF)
            u = mm(normed, w_ref[...])
            for b in range(0, turned, 128):
                out_ref[:, b : b + 128] = turn(u[:, b : b + 128], cosine, sine).astype(BF)
            out_ref[:, turned:] = u[:, turned:].astype(BF)

    return pl.pallas_call(
        body,
        out_shape=[jax.ShapeDtypeStruct((rows, n), BF)] * count,
        in_specs=[SM] + [VM] * (4 + count),
        out_specs=[VM] * count,
        compiler_params=params(),
        cost_estimate=cost(2 * count * rows * d * n, 2 * d * n + 4 * count * rows * d),
        name="project",
    )(places, gain, w, cos, sin, *toks)


def swapped(e):
    return (e & 1) * 2 + (e >> 1)


def split_store(a_ref, b_ref, e, at, value):
    @pl.when(e < 2)
    def _():
        a_ref[(e, *at)] = value

    @pl.when(e >= 2)
    def _():
        b_ref[(e - 2, *at)] = value


def lower_half(shape):
    return lax.broadcasted_iota(jnp.int32, shape, 1) < 64


def stage_heads(block, dst, rows_at, heads, factor):
    rows = block.shape[0]
    low = lower_half((rows, 128))
    for h in range(heads):
        part = block[:, (h // 2) * 128 : (h // 2 + 1) * 128].astype(F32) * factor
        keep = low if h % 2 == 0 else jnp.logical_not(low)
        dst[h, rows_at, :] = jnp.where(keep, part, 0.0).astype(BF)


def doubled(block):
    block = block.astype(F32)
    low = lower_half(block.shape)
    other = pltpu.roll(block, 64, 1)
    return jnp.where(low, block, other), jnp.where(low, other, block)


def allowed_mask(s_ref, keys, rows, first):
    q = lax.broadcasted_iota(jnp.int32, (1, rows), 1) + first
    begin = jnp.zeros_like(q)
    for i in range(5, s_ref.shape[0] - 1):
        begin = jnp.where(q >= s_ref[i], jnp.maximum(begin, s_ref[i]), begin)
    k = lax.broadcasted_iota(jnp.int32, (keys, rows), 0)
    return (k >= begin) & (k <= q)


def attend(scalars, pieces, heads, kvs):
    blocks = len(pieces)
    rows, width = pieces[0].shape
    span = blocks * rows
    qw = heads * HEAD_DIM
    share = heads // kvs

    def body(s_ref, *refs):
        ins, outs, (lse_ref, qs, kd, vd, vt, ob) = refs[:blocks], refs[blocks : 2 * blocks], refs[2 * blocks :]
        me = s_ref[4]
        for k in range(blocks):
            at = pl.ds(pl.multiple_of(s_ref[k] * rows, rows), rows)
            block = ins[k][...]
            stage_heads(block, qs, at, heads, score_scale)
            for i, x in enumerate(doubled(block[:, qw : qw + 128])):
                kd[i, at, :] = x.astype(BF)
            for i, x in enumerate(doubled(block[:, qw + 128 : qw + 256])):
                vd[i, at, :] = x
        for i in range(kvs):
            vt[i] = vd[i].T.astype(BF)

        def one(h, _):
            kv = h // share
            for p in range(blocks):
                keys = (p + 1) * rows
                q = qs[h, p * rows : (p + 1) * rows, :]
                s = mm(kd[kv, :keys, :], q, NT)
                s = jnp.where(allowed_mask(s_ref, keys, rows, p * rows), s, -1e30)
                peak = jnp.max(s, axis=0, keepdims=True)
                e = jnp.exp(s - peak)
                total = jnp.sum(e, axis=0, keepdims=True)
                o = mm(vt[kv, :, :keys], e.astype(BF)) / total
                ob[h, p * rows : (p + 1) * rows, :] = o.T
                lse_ref[pl.ds(h, 1), p * rows : (p + 1) * rows] = peak + jnp.log(total)
            return 0

        def some(i, _):
            for u in range(share):
                one(i * share + u, 0)
            return 0

        lax.fori_loop(0, kvs, some, 0)
        low = lower_half((rows, 128))
        for k in range(blocks):
            at = pl.ds(pl.multiple_of(lax.rem(me + k, blocks) * rows, rows), rows)
            for b in range(heads // 2):
                outs[k][:, b * 128 : (b + 1) * 128] = jnp.where(
                    low, ob[2 * b, at, :], ob[2 * b + 1, at, :]
                ).astype(BF)

    pairs = heads * rows * rows * blocks * (blocks + 1) // 2
    *mixes, lse = pl.pallas_call(
        body,
        out_shape=[jax.ShapeDtypeStruct((rows, qw), BF)] * blocks + [jax.ShapeDtypeStruct((8, span), F32)],
        in_specs=[SM] + [VM] * blocks,
        out_specs=[VM] * (blocks + 1),
        scratch_shapes=[
            pltpu.VMEM((heads, span, 128), BF),
            pltpu.VMEM((kvs, span, 128), BF),
            pltpu.VMEM((kvs, span, 128), F32),
            pltpu.VMEM((kvs, 128, span), BF),
            pltpu.VMEM((heads, span, 128), F32),
        ],
        compiler_params=params(),
        cost_estimate=cost(pairs * 1024, 4 * span * width, pairs),
        name="attend",
    )(scalars, *pieces)
    return mixes, lse


def attend_back(scalars, pieces, grads, lse, cos, sin, heads, kvs):
    blocks = len(pieces)
    rows, width = pieces[0].shape
    span = blocks * rows
    qw = heads * HEAD_DIM
    share = heads // kvs

    def body(s_ref, *refs):
        ins, gins = refs[:blocks], refs[blocks : 2 * blocks]
        lse_ref, cos_ref, sin_ref, out_ref, qs, gs, kd, kf, kt, vd, dk, dv, dq = refs[2 * blocks :]
        me = s_ref[4]
        for k in range(blocks):
            at = pl.ds(pl.multiple_of(s_ref[k] * rows, rows), rows)
            block = ins[k][...]
            stage_heads(block, qs, at, heads, score_scale)
            for i, x in enumerate(doubled(block[:, qw : qw + 128])):
                kd[i, at, :] = x.astype(BF)
                kf[i, at, :] = x
            for i, x in enumerate(doubled(block[:, qw + 128 : qw + 256])):
                vd[i, at, :] = x.astype(BF)
            at = pl.ds(pl.multiple_of(lax.rem(me + k, blocks) * rows, rows), rows)
            stage_heads(gins[k][...], gs, at, heads, 1.0)
        for i in range(kvs):
            kt[i] = kf[i].T.astype(BF)
        dk[...] = jnp.zeros_like(dk)
        dv[...] = jnp.zeros_like(dv)

        def one(h, _):
            kv = h // share
            for p in range(blocks):
                keys = (p + 1) * rows
                at = slice(p * rows, (p + 1) * rows)
                q = qs[h, at, :]
                g = gs[h, at, :]
                s = mm(kd[kv, :keys, :], q, NT)
                log_total = lse_ref[pl.ds(h, 1), at]
                chances = jnp.where(
                    allowed_mask(s_ref, keys, rows, p * rows), jnp.exp(s - log_total), 0.0
                )
                gp = mm(vd[kv, :keys, :], g, NT)
                row_dot = jnp.sum(chances * gp, axis=0, keepdims=True)
                ds = (chances * (gp - row_dot)).astype(BF)
                dq[h, at, :] = mm(kt[kv, :, :keys], ds).T
                dk[kv, :keys, :] += mm(ds, q)
                dv[kv, :keys, :] += mm(chances.astype(BF), g)
            return 0

        for h in range(heads):
            one(h, 0)
        low = lower_half((rows, 128))
        for p in range(blocks):
            at = slice(p * rows, (p + 1) * rows)
            cosine, sine = cos_ref[at, :], -sin_ref[at, :]
            for b in range(heads // 2):
                x = jnp.where(low, dq[2 * b, at, :], dq[2 * b + 1, at, :]) * score_scale
                out_ref[at, b * 128 : (b + 1) * 128] = turn(x, cosine, sine).astype(BF)
            k0, k1, v0, v1 = dk[0, at, :], dk[1, at, :], dv[0, at, :], dv[1, at, :]
            k0, k1 = k0 + pltpu.roll(k0, 64, 1), k1 + pltpu.roll(k1, 64, 1)
            v0, v1 = v0 + pltpu.roll(v0, 64, 1), v1 + pltpu.roll(v1, 64, 1)
            out_ref[at, qw : qw + 128] = turn(jnp.where(low, k0, k1), cosine, sine).astype(BF)
            out_ref[at, qw + 128 : qw + 256] = jnp.where(low, v0, v1).astype(BF)

    pairs = heads * rows * rows * blocks * (blocks + 1) // 2
    return pl.pallas_call(
        body,
        out_shape=jax.ShapeDtypeStruct((span, width), BF),
        in_specs=[SM] + [VM] * (2 * blocks + 3),
        out_specs=VM,
        scratch_shapes=[
            pltpu.VMEM((heads, span, 128), BF),
            pltpu.VMEM((heads, span, 128), BF),
            pltpu.VMEM((kvs, span, 128), BF),
            pltpu.VMEM((kvs, span, 128), F32),
            pltpu.VMEM((kvs, 128, span), BF),
            pltpu.VMEM((kvs, span, 128), BF),
            pltpu.VMEM((kvs, span, 128), F32),
            pltpu.VMEM((kvs, span, 128), F32),
            pltpu.VMEM((heads, span, 128), F32),
        ],
        compiler_params=params(),
        cost_estimate=cost(pairs * 2560, 8 * span * width, pairs),
        name="attend_back",
    )(scalars, *pieces, *grads, lse, cos, sin)


def join(scalars, mixes, w_out, tok, gain):
    blocks = len(mixes)
    rows, part = mixes[0].shape
    d = tok.shape[1]

    def body(s_ref, *refs):
        ins, (w_ref, tok_ref, gain_ref, mid_ref, hid_ref) = refs[:blocks], refs[blocks:]
        me = s_ref[4]
        branch = jnp.zeros((rows, d), F32)
        for k in range(blocks):
            at = pl.ds(pl.multiple_of(lax.rem(me - k + blocks, blocks) * part, part), part)
            branch = branch + mm(ins[k][...], w_ref[at, :])
        middle = tok_ref[...].astype(F32) + residual_scale * branch
        mid_ref[...] = middle
        hid_ref[...] = (middle * rms(middle) * gain_ref[...]).astype(BF)

    return pl.pallas_call(
        body,
        out_shape=(jax.ShapeDtypeStruct((rows, d), F32), jax.ShapeDtypeStruct((rows, d), BF)),
        in_specs=[SM] + [VM] * (blocks + 3),
        out_specs=(VM, VM),
        compiler_params=params(),
        cost_estimate=cost(2 * rows * d * d, 2 * d * d + 10 * rows * d),
        name="join",
    )(scalars, *mixes, w_out, tok, gain)


def join_back(scalars, addends, middle, cot, gain, w_out):
    blocks = 4
    rows, d = middle.shape
    part = d // blocks
    count = len(addends)

    def body(s_ref, *refs):
        ins, (mid_ref, cot_ref, gain_ref, w_any, gmid_ref, br_ref, gg_ref, *outs) = refs[:count], refs[count:]
        *outs, w_ref, sems = outs
        me = s_ref[4]
        spans = [
            pl.ds(pl.multiple_of(lax.rem(me - k + blocks, blocks) * part, part), part) for k in range(blocks)
        ]
        copies = [
            pltpu.make_async_copy(w_any.at[spans[k], :], w_ref.at[k], sems.at[k]) for k in range(blocks)
        ]
        for copy in copies:
            copy.start()
        grad_hidden = sum(t[...].astype(F32) for t in ins)
        middle = mid_ref[...]
        inv = rms(middle)
        normal = middle * inv
        gg_ref[...] = jnp.sum(grad_hidden * normal, axis=0, keepdims=True)
        u = grad_hidden * gain_ref[...]
        grad_middle = cot_ref[...] + inv * (u - normal * jnp.mean(u * normal, axis=-1, keepdims=True))
        gmid_ref[...] = grad_middle
        br_ref[...] = (residual_scale * grad_middle).astype(BF)
        for k in range(blocks):
            copies[k].wait()
            outs[k][...] = mm(br_ref[...], w_ref[k], NT).astype(BF)

    front = lambda t: pl.BlockSpec((rows, d), lambda i: (0, 0))
    fixed = lambda *shape: pl.BlockSpec(shape, lambda i: (0, 0))
    grad_middle, branch, gain_grad, *mixes = pl.pallas_call(
        body,
        grid=(1,),
        out_shape=[
            jax.ShapeDtypeStruct((rows, d), F32),
            jax.ShapeDtypeStruct((rows, d), BF),
            jax.ShapeDtypeStruct((1, d), F32),
        ]
        + [jax.ShapeDtypeStruct((rows, part), BF)] * blocks,
        in_specs=[SM]
        + [front(t) for t in addends]
        + [fixed(rows, d), fixed(rows, d), fixed(1, d), ANY],
        out_specs=[fixed(rows, d), fixed(rows, d), fixed(1, d)] + [fixed(rows, part)] * blocks,
        scratch_shapes=[pltpu.VMEM((blocks, part, d), BF), pltpu.SemaphoreType.DMA((blocks,))],
        compiler_params=params(),
        cost_estimate=cost(2 * rows * d * d, 2 * d * d + 18 * rows * d),
        name="join_back",
    )(scalars, *addends, middle, cot, gain, w_out)
    return grad_middle, mixes, branch, gain_grad


def join_weights(scalars, here, branch, mixes, nd, ne):
    blocks = len(mixes)
    rows, part = mixes[0].shape
    d = branch.shape[1]
    w_rows = d // (nd * blocks * ne)

    def body(s_ref, here_ref, br_ref, *refs):
        ins, (gwa_ref, gwb_ref) = refs[:blocks], refs[blocks:]
        me = s_ref[4]
        for k in range(blocks):
            gw = mm(ins[k][...], br_ref[...], TN)
            for i in range(part // w_rows):
                q = lax.rem(me - k + blocks, blocks) * (part // w_rows) + i
                e = swapped(jnp.bitwise_xor(lax.rem(q, ne), here_ref[3]))
                b = lax.div(q, ne)
                m = lax.rem(lax.div(b, blocks) - here_ref[0] + nd, nd)
                put = gw[i * w_rows : (i + 1) * w_rows, :].astype(BF)
                split_store(gwa_ref, gwb_ref, e, (m, lax.rem(b, blocks)), put)

    return pl.pallas_call(
        body,
        out_shape=(jax.ShapeDtypeStruct((2, nd, blocks, w_rows, d), BF),) * 2,
        in_specs=[SM, SM] + [VM] * (1 + blocks),
        out_specs=(VM, VM),
        compiler_params=params(),
        cost_estimate=cost(2 * rows * d * d, 2 * d * d + 4 * rows * d),
        name="join_weights",
    )(scalars, here, branch, *mixes)


def halves(w, odd, devices):
    n, r, width = w.shape
    unit = FF // devices
    if 2 * unit != 128:
        parts = w.reshape(n, r, 2, devices // 4, 2, 2, unit)
        parts = jnp.transpose(parts, (5, 0, 1, 2, 3, 4, 6)).reshape(2, n, r, FF)
        return pick(parts, odd), pick(parts, 1 - odd)

    def body(odd_ref, w_ref, mine_ref, their_ref):
        low = lower_half((r, 128))
        even = odd_ref[0] == 0
        for m in range(width // 256):
            a = w_ref[0, :, 2 * m * 128 : (2 * m + 1) * 128].astype(F32)
            b = w_ref[0, :, (2 * m + 1) * 128 : (2 * m + 2) * 128].astype(F32)
            evens = jnp.where(low, a, pltpu.roll(b, 64, 1))
            odds = jnp.where(low, pltpu.roll(a, 64, 1), b)
            at = slice(m * 128, (m + 1) * 128)
            mine_ref[0, :, at] = jnp.where(even, evens, odds).astype(BF)
            their_ref[0, :, at] = jnp.where(even, odds, evens).astype(BF)

    spec = pl.BlockSpec((1, r, FF), lambda e: (e, 0, 0))
    return pl.pallas_call(
        body,
        grid=(n,),
        out_shape=(jax.ShapeDtypeStruct((n, r, FF), BF),) * 2,
        in_specs=[SM, pl.BlockSpec((1, r, width), lambda e: (e, 0, 0))],
        out_specs=(spec, spec),
        compiler_params=params(),
        cost_estimate=cost(0, 4 * n * r * width),
        name="halves",
    )(odd[None].astype(jnp.int32), w)


def whole(parts, odd, devices):
    count = len(parts)
    _, r, width = parts[0][0].shape
    r3 = r // 3
    unit = FF // devices

    def plain(own, other, theirs):
        total = own.astype(F32) + other.astype(F32)
        theirs = theirs.astype(F32)
        pair = jnp.stack([jnp.where(odd == 0, total[0], theirs), jnp.where(odd == 0, theirs, total[0])])
        pair = pair.reshape(2, r, 2, devices // 4, 2, unit)
        down = [total[2, b * r3 : (b + 1) * r3] for b in range(3)]
        return jnp.transpose(pair, (1, 2, 3, 4, 0, 5)).reshape(r, 2 * width), jnp.concatenate(down, axis=1)

    if 2 * unit != 128:
        done = [plain(*p) for p in parts]
        return jnp.stack([p[0] for p in done]), jnp.stack([p[1] for p in done])

    def body(odd_ref, own_ref, other_ref, their_ref, *refs):
        in_ref, down_ref = refs[-2], refs[-1]
        low = lower_half((r, 128))
        even = odd_ref[0] == 0
        for m in range(width // 128):
            at = slice(m * 128, (m + 1) * 128)
            mine = own_ref[0, :, at].astype(F32) + other_ref[0, :, at].astype(F32)
            their = their_ref[:, at].astype(F32)
            evens, odds = jnp.where(even, mine, their), jnp.where(even, their, mine)
            in_ref[0, :, 2 * m * 128 : (2 * m + 1) * 128] = jnp.where(low, evens, pltpu.roll(odds, 64, 1))
            in_ref[0, :, (2 * m + 1) * 128 : (2 * m + 2) * 128] = jnp.where(
                low, pltpu.roll(evens, 64, 1), odds
            )
        for b in range(3):
            at = slice(b * r3, (b + 1) * r3)
            down_ref[0, :, b * width : (b + 1) * width] = (
                own_ref[2, at, :].astype(F32) + other_ref[2, at, :].astype(F32)
            )

    done = ()
    for e, (own, other, theirs) in enumerate(parts):
        fixed = lambda *shape: pl.BlockSpec(shape, lambda i: (0,) * len(shape))
        done = pl.pallas_call(
            body,
            grid=(1,),
            out_shape=(
                jax.ShapeDtypeStruct((count, r, 2 * width), F32),
                jax.ShapeDtypeStruct((count, r3, 3 * width), F32),
            ),
            in_specs=[SM, fixed(3, r, width), fixed(3, r, width), fixed(r, width)] + [ANY] * len(done),
            out_specs=(
                pl.BlockSpec((1, r, 2 * width), lambda i, e=e: (e, 0, 0)),
                pl.BlockSpec((1, r3, 3 * width), lambda i, e=e: (e, 0, 0)),
            ),
            input_output_aliases={4: 0, 5: 1} if done else {},
            compiler_params=params(),
            cost_estimate=cost(0, 20 * r * width),
            name="whole",
        )(odd[None].astype(jnp.int32), own, other, theirs, *done)
    return done


def experts_rows(places, which, rows_in, cots, shards, sums, last):
    piece, d = rows_in[0].shape
    group = 1
    rows = piece * group
    tiles = len(rows_in) // group
    total = rows * tiles
    count, n = len(shards), len(shards[0])
    r, width = shards[0][0][0].shape[-2:]
    arrays = {id(t): t for shard in shards for t, _ in shard}
    slot = {key: k for k, key in enumerate(arrays)}
    arrays = list(arrays.values())
    half = width // 2
    r3 = r // 3
    first = sums is None

    def body(places_ref, *refs):
        n_in = tiles * group
        h_refs, c_refs, refs = refs[:n_in], refs[n_in : 2 * n_in], refs[2 * n_in :]
        w_refs, refs = refs[: len(arrays)], refs[len(arrays) :]
        if not first:
            in_h, in_o, refs = refs[0], refs[1], refs[2:]
        if last:
            out_h, rest_h, out_o, rest_o, gb_ref, gat_ref, *refs = refs
        else:
            out_h, out_o, gb_ref, gat_ref, *refs = refs
        if first:
            ht_ref, *refs = refs
        wiv, wdv, ga_ref, hv, cv, sems, row_sems = refs
        t = pl.program_id(0)
        moves = []
        for i in range(n_in):
            at = pl.ds(i % group * piece, piece)
            moves.append(
                (
                    pltpu.make_async_copy(h_refs[i], hv.at[i // group, at, :], row_sems.at[0, i]),
                    pltpu.make_async_copy(c_refs[i], cv.at[i // group, at, :], row_sems.at[1, i]),
                )
            )

        @pl.when(t == 0)
        def _():
            copies = []
            for i in range(count):
                for e in range(n):
                    array, which_of = shards[i][e]
                    source = w_refs[slot[id(array)]]
                    source = source if which_of is None else source.at[which_of]
                    parts = []
                    for b in range(2):
                        at = pl.multiple_of(places_ref[3 * i + b] * r, r)
                        parts.append((source.at[2 * b], wiv.at[pl.ds(at, r), e * width : (e + 1) * width]))
                    at = pl.multiple_of(places_ref[3 * i + 2] * r3 + e * half, r3)
                    for b in range(3):
                        parts.append(
                            (
                                source.at[1, b * r3 : (b + 1) * r3, :],
                                wdv.at[pl.ds(at, r3), b * width : (b + 1) * width],
                            )
                        )
                    for k, (a, b) in enumerate(parts):
                        copies.append(pltpu.make_async_copy(a, b, sems.at[i, e, k]))
            for copy in copies:
                copy.start()
            for a, b in moves[:group]:
                a.start()
                b.start()
            for copy in copies:
                copy.wait()
            for a, b in moves[group:]:
                a.start()
                b.start()

        for i in range(tiles):

            @pl.when(t == i)
            def _():
                for a, b in moves[i * group : (i + 1) * group]:
                    a.wait()
                    b.wait()

        h = hv[t]
        c = cv[t, :, :d]
        gates = cv[t, :, d:].astype(F32)
        lane = lax.broadcasted_iota(jnp.int32, gates.shape, 1) - places_ref[3 * count]
        for e in range(n):
            g = jnp.sum(jnp.where(lane == which + e, gates, 0.0), axis=1, keepdims=True)
            gu = mm(h, wiv[:, e * width : (e + 1) * width])
            gate, up = gu[:, :half], gu[:, half:]
            sg = jax.nn.sigmoid(gate)
            silu = gate * sg
            ga = mm(c, wdv[e * half : (e + 1) * half, :], NT) * g
            ga_ref[:, e * half : (e + 1) * half] = (silu * up * g).astype(BF)
            gb_ref[:, e * width : e * width + half] = (ga * up * (sg + silu * (1.0 - sg))).astype(BF)
            gb_ref[:, e * width + half : (e + 1) * width] = (ga * silu).astype(BF)
        o = mm(ga_ref[...], wdv[...])
        gh = mm(gb_ref[...], wiv[...], NT)
        gat_ref[...] = ga_ref[...].T
        if first:
            ht_ref[...] = h.T
        if not first:
            o = o + in_o[...].astype(F32)
            gh = gh + in_h[...].astype(F32)
        if last:

            @pl.when(t < tiles // 2)
            def _():
                out_o[...] = o.astype(BF)
                out_h[...] = gh.astype(BF)

            @pl.when(t >= tiles // 2)
            def _():
                rest_o[...] = o.astype(BF)
                rest_h[...] = gh.astype(BF)

        else:
            out_o[...] = o.astype(BF)
            out_h[...] = gh.astype(BF)

    tile = lambda c: pl.BlockSpec((rows, c), lambda t: (t, 0))
    flat = lambda c: pl.BlockSpec((c, rows), lambda t: (0, t))
    if last:
        sum_shapes = (jax.ShapeDtypeStruct((total // 2, d), BF),) * 4
        front = pl.BlockSpec((rows, d), lambda t: (jnp.minimum(t, tiles // 2 - 1), 0))
        back = pl.BlockSpec((rows, d), lambda t: (jnp.maximum(t - tiles // 2, 0), 0))
        sum_specs = (front, back, front, back)
    else:
        sum_shapes = (jax.ShapeDtypeStruct((total, d), BF),) * 2
        sum_specs = (tile(d), tile(d))
    return pl.pallas_call(
        body,
        grid=(tiles,),
        out_shape=sum_shapes
        + (
            jax.ShapeDtypeStruct((total, n * width), BF),
            jax.ShapeDtypeStruct((n * half, total), BF),
        )
        + ((jax.ShapeDtypeStruct((d, total), BF),) if first else ()),
        in_specs=[SM]
        + [ANY] * (2 * len(rows_in) + len(arrays))
        + ([] if first else [tile(d), tile(d)]),
        out_specs=sum_specs + (tile(n * width), flat(n * half)) + ((flat(d),) if first else ()),
        scratch_shapes=[
            pltpu.VMEM((d, n * width), BF),
            pltpu.VMEM((n * half, d), BF),
            pltpu.VMEM((rows, n * half), BF),
            pltpu.VMEM((tiles, rows, d), BF),
            pltpu.VMEM((tiles, rows, cots[0].shape[1]), BF),
            pltpu.SemaphoreType.DMA((count, n, 5)),
            pltpu.SemaphoreType.DMA((2, len(rows_in))),
        ],
        compiler_params=params(),
        cost_estimate=cost(6 * n * total * d * width, 50e6, n * total * half),
        name="experts_rows",
    )(places, *rows_in, *cots, *arrays, *(() if first else sums))


def experts_weights(scalars, rows_t, cots, gb, ga_t, n, devices):
    d, total = rows_t.shape
    width, half = gb.shape[1] // n, ga_t.shape[0] // n
    r = d // devices
    r3 = r // 3
    nd = devices // 4
    tiles = len(cots)
    rows = total // tiles

    def body(s_ref, h_any, gb_any, ga_any, *refs):
        c_refs, refs = refs[:tiles], refs[tiles:]
        outs, (down, h_ref, gb_ref, ga_ref, c_ref, stage, sems, c_sems, out_sems) = refs[: n * nd], refs[n * nd :]
        ahead = [lax.rem(s_ref[0] + k, nd) for k in range(nd)]
        spans = [pl.ds(pl.multiple_of(x * 4 * r, 4 * r), 4 * r) for x in ahead]
        first = [pltpu.make_async_copy(gb_any, gb_ref, sems.at[0])]
        first += [
            pltpu.make_async_copy(h_any.at[spans[k], :], h_ref.at[k], sems.at[1 + k]) for k in range(nd)
        ]
        second = [pltpu.make_async_copy(ga_any, ga_ref, c_sems.at[tiles])]
        second += [
            pltpu.make_async_copy(c_refs[i].at[:, :d], c_ref.at[pl.ds(i * rows, rows), :], c_sems.at[i])
            for i in range(tiles)
        ]
        for copy in first[:2]:
            copy.start()
        first[0].wait()
        for k in range(nd):
            first[1 + k].wait()
            for copy in first[2:] + second if k == 0 else []:
                copy.start()
            part = mm(h_ref[k], gb_ref[...]).astype(BF)
            for z in range(4):
                where = jnp.bitwise_xor(s_ref[2], z // 2)
                slot = jnp.bitwise_xor(s_ref[1], z % 2)
                for e in range(n):
                    stage[e * nd + k, where, slot] = part[z * r : (z + 1) * r, e * width : (e + 1) * width]
        for copy in second:
            copy.wait()
        leaving = []
        for e in range(n):
            down[...] = mm(ga_ref[e * half : (e + 1) * half, :], c_ref[...]).astype(BF)
            for k in range(nd):
                for z in range(2):
                    where = jnp.bitwise_xor(s_ref[2], z)
                    at = pl.ds(pl.multiple_of((2 * ahead[k] + z) * r3, r3), r3)
                    for b in range(3):
                        stage[e * nd + k, where, 2, b * r3 : (b + 1) * r3, :] = down[
                            at, b * width : (b + 1) * width
                        ]
                leaving.append(
                    pltpu.make_async_copy(stage.at[e * nd + k], outs[e * nd + k], out_sems.at[e * nd + k])
                )
                leaving[-1].start()
        for copy in leaving:
            copy.wait()

    outs = pl.pallas_call(
        body,
        out_shape=[jax.ShapeDtypeStruct((2, 3, r, width), BF)] * (n * nd),
        in_specs=[SM] + [ANY] * (3 + tiles),
        out_specs=[ANY] * (n * nd),
        scratch_shapes=[
            pltpu.VMEM((half, d), BF),
            pltpu.VMEM((nd, 4 * r, total), BF),
            pltpu.VMEM((total, n * width), BF),
            pltpu.VMEM((n * half, total), BF),
            pltpu.VMEM((total, d), BF),
            pltpu.VMEM((n * nd, 2, 3, r, width), BF),
            pltpu.SemaphoreType.DMA((1 + nd,)),
            pltpu.SemaphoreType.DMA((tiles + 1,)),
            pltpu.SemaphoreType.DMA((n * nd,)),
        ],
        compiler_params=params(),
        cost_estimate=cost(3 * n * total * d * width, 20e6),
        name="experts_weights",
    )(scalars, rows_t, gb, ga_t, *cots)
    return [outs[e * nd : (e + 1) * nd] for e in range(n)]


def finish(scalars, dqkv, w, blocks):
    total, width = dqkv.shape
    d = w.shape[0]
    rows = total // blocks

    def body(s_ref, dq_ref, w_ref, *outs):
        for k in range(blocks):
            at = lax.rem(s_ref[4] - 1 - k + 2 * blocks, blocks)
            at = pl.ds(pl.multiple_of(at * rows, rows), rows)
            outs[k][...] = mm(dq_ref[at, :], w_ref[...], NT).astype(BF)

    return pl.pallas_call(
        body,
        out_shape=[jax.ShapeDtypeStruct((rows, d), BF)] * blocks,
        in_specs=[SM, VM, VM],
        out_specs=[VM] * blocks,
        compiler_params=params(),
        cost_estimate=cost(2 * total * d * width, 4 * total * d),
        name="finish",
    )(scalars, dqkv, w)


def finish_weights(scalars, here, dqkv, gn, toks, gain, gain_grad, nd, ne):
    blocks = len(toks)
    rows, d = toks[0].shape
    width = dqkv.shape[1]
    w_rows = d // (nd * blocks * ne)

    def body(s_ref, here_ref, dq_ref, gain_ref, gg_ref, *refs):
        ins, gns, (gwa_ref, gwb_ref, acc) = refs[:blocks], refs[blocks : 2 * blocks], refs[2 * blocks :]
        gg = jnp.zeros((1, d), F32)
        for k in range(blocks):
            to = s_ref[k]
            at = pl.ds(pl.multiple_of(to * rows, rows), rows)
            t = ins[k][...].astype(F32)
            normal = t * rms(t)
            normed = (normal * gain_ref[...]).astype(BF)
            gn = gns[(k - 1) % blocks][...].astype(F32)
            gg = gg + jnp.sum(gn * normal, axis=0, keepdims=True)
            part = mm(normed, dq_ref[at, :], TN)
            acc[...] = part if k == 0 else acc[...] + part
        row = lax.broadcasted_iota(jnp.int32, (128, d), 0)
        both = jnp.where(row == 0, gg, jnp.where(row == 1, gg_ref[...], 0.0)).T
        for q in range(d // w_rows):
            e = swapped(jnp.bitwise_xor(q % ne, here_ref[3]))
            m = lax.rem(q // ne // blocks - here_ref[0] + nd, nd)
            at = slice(q * w_rows, (q + 1) * w_rows)
            put = jnp.concatenate([acc[at, :], both[at, :]], axis=1).astype(BF)
            split_store(gwa_ref, gwb_ref, e, (m, q // ne % blocks), put)

    return pl.pallas_call(
        body,
        out_shape=(jax.ShapeDtypeStruct((2, nd, blocks, w_rows, width + 128), BF),) * 2,
        in_specs=[SM, SM] + [VM] * (3 + 2 * blocks),
        out_specs=(VM, VM),
        scratch_shapes=[pltpu.VMEM((d, width), F32)],
        compiler_params=params(),
        cost_estimate=cost(2 * blocks * rows * d * width, 6 * blocks * rows * d),
        name="finish_weights",
    )(scalars, here, dqkv, gain, gain_grad, *toks, *gn)


def per_device(
    tokens,
    gain_attn,
    w_query,
    w_key,
    w_value,
    w_out,
    gain_moe,
    w_in,
    w_down,
    routes,
    gates,
    lengths,
    cotangent,
):
    nd, nz, ne = lax.axis_size("dp"), lax.axis_size("ctx"), lax.axis_size("exp")
    x, z, j = lax.axis_index("dp"), lax.axis_index("ctx"), lax.axis_index("exp")
    rows, d = tokens.shape[1:]
    span = rows * nz
    w_rows = w_query.shape[0]
    heads, kvs = HEADS // nz, KV_HEADS // nz
    qw, kw = heads * HEAD_DIM, kvs * HEAD_DIM
    local_experts = w_in.shape[0]
    experts = local_experts * ne
    i32 = jnp.int32
    mod = lambda v, n: lax.rem(v + 8 * n, n)

    ends = jnp.cumsum(lengths[0]).astype(i32)
    places = [mod(z - k, nz) for k in range(nz)]
    scalars = jnp.concatenate([jnp.stack(places + [z]).astype(i32), ends])
    place = jnp.arange(span, dtype=i32)
    place = place - jnp.max(jnp.where(place[:, None] >= ends[None, :-1], ends[None, :-1], 0), axis=1)
    lane = jnp.arange(128, dtype=i32)
    half = HEAD_DIM // 2
    frequency = rope_base ** (-2.0 * jnp.arange(half, dtype=F32) / HEAD_DIM)
    angles = place.astype(F32)[:, None] * frequency[None, :]
    cos = jnp.tile(jnp.cos(angles), (1, 128 // half))
    sin = jnp.tile(jnp.sin(angles), (1, 128 // half)) * jnp.where((lane & 63) < 32, -1.0, 1.0)[None, :]

    run = Stages(gain_attn)
    gain_a, gain_m = gain_attn[None, :], gain_moe[None, :]
    devices = nd * nz
    odd, zh = jnp.bitwise_and(z, 1), z // 2
    batch = local_experts // 2
    tok, cot = tokens[0], cotangent[0]
    flip_e = lambda v, e: flip(v, "exp", e)

    def row_blocks(found, owners, order):
        at = [
            (mod(x - m, nd) * nz + p) * ne + jnp.bitwise_xor(j, e + 2 * b)
            for e in (0, 1) for b, m in order for p in owners
        ]
        return assemble(found, jnp.stack(at).astype(i32))

    by_m = [(b, m) for m in range(nd) for b in (0, 1)]
    by_b = [(b, m) for b in (0, 1) for m in range(nd)]

    here = jnp.stack([x, odd, zh, j]).astype(i32)

    parts = [
        jnp.concatenate(
            [
                w_query[:, p * qw : (p + 1) * qw],
                w_key[:, p * kw : (p + 1) * kw],
                w_value[:, p * kw : (p + 1) * kw],
            ],
            axis=1,
        )
        for p in range(nz)
    ]
    cut = rows // 2
    toks = [tok, shift(tok, "ctx", 1)]
    w_parts = jnp.stack(parts)
    w_mine = [pick(w_parts, z)] + [shift(pick(w_parts, mod(z + k, nz)), "ctx", k) for k in range(1, nz)]
    run.end(toks, w_mine)

    half_2 = [shift(run.hold(toks[1])[:cut], "ctx", 1)]
    mine_in, their_in = halves(run.hold(w_in), odd, devices)
    down = run.hold(w_down)
    down = jnp.concatenate([down[:, :, b * FF : (b + 1) * FF] for b in range(d // FF)], axis=1)
    w_mine = jnp.stack(w_mine)
    w_mine = jnp.stack([w_mine, flip_e(run.hold(w_mine), 2)])
    line = [hop(run.hold(w_out), pairs) for pairs in (ACROSS, UP, DOWN)]
    run.end(half_2, w_mine, line, mine_in)

    half_2.append(shift(run.hold(toks[1])[cut:], "ctx", 1))
    hits = run.hold(routes)[0][:, :, None] == jnp.arange(128, dtype=i32)[None, None, :]
    dense = jnp.sum(jnp.where(hits, gates[0].astype(F32)[:, :, None], 0.0), axis=1).astype(BF)
    cot_b = jnp.concatenate([(residual_scale * run.hold(cot)).astype(BF), dense], axis=1)
    w_found = ring(run.hold(w_mine), "dp")
    line_end = hop(run.hold(line[0]), OUTER)
    run.end(half_2, w_found, line_end, cot_b)

    toks.append(jnp.concatenate(half_2))
    toks.append(shift(run.hold(toks[2]), "ctx", 1))
    got_1 = flip(run.hold(their_in[:batch]), "ctx", 1)
    w_found = w_found + [flip_e(t, 1) for t in run.hold(w_found)]
    w_line = ring(run.hold(jnp.stack(line_gather(*line, line_end, w_out))), "dp")
    cot_2 = flip_e(run.hold(cot_b), 2)
    w_qkv = row_blocks(w_found, places, by_m)
    at = jnp.stack(places).astype(i32)
    pieces = project(toks[: nz - 1], gain_a, w_qkv, cos, sin, at[: nz - 1])
    run.end(toks, pieces, got_1, w_line, cot_2)

    packet = lambda e, got: jnp.stack([mine_in[e], down[e], got[e % batch]])
    near = [packet(e, got_1) for e in range(batch)]
    far = [flip(run.hold(near[0]), "ctx", 2)]
    own = [ring(run.hold(jnp.stack(near)), "dp")]
    w_line = jnp.stack(w_line)
    w_line = jnp.stack([w_line, flip_e(run.hold(w_line), 2)])
    cot_n = flip(run.hold(cot_b), "ctx", 1)
    pieces = pieces + project([run.hold(toks[3])], gain_a, w_qkv, cos, sin, at[nz - 1 :])
    mix_out, lse = attend(scalars, pieces, heads, kvs)
    run.end(far, own, w_line, cot_n, mix_out)

    mixes = run.hold(mix_out)
    mixes = [mixes[0]] + [shift(mixes[k], "ctx", k) for k in range(1, nz)]
    w_line = [w_line, flip_e(run.hold(w_line), 1)]
    cot_n2 = flip_e(run.hold(cot_n), 2)
    w_out_all = row_blocks(w_line, line_places(z), by_b)
    run.end(mixes, w_out_all, cot_n2)

    cot_1 = flip_e(run.hold(cot_b), 1)
    cot_n1, cot_n3 = flip_e(run.hold(cot_n), 1), flip_e(run.hold(cot_n2), 1)
    got_2 = flip(run.hold(their_in[batch:]), "ctx", 1)
    over = [ring(run.hold(far[0]), "dp")]
    middle, hidden = join(scalars, run.hold(mixes), w_out_all, tok, gain_m)
    run.end(hidden, got_2, over, cot_1, cot_n1, cot_n3)

    hidden_2, hidden_n = flip_e(run.hold(hidden), 2), flip(run.hold(hidden), "ctx", 1)
    far += [flip(run.hold(near[e]), "ctx", 2) for e in range(1, batch)]
    near.append(packet(batch, got_2))
    own.append(ring(run.hold(near[batch]), "dp"))
    hidden_1 = flip_e(run.hold(hidden), 1)
    run.end(hidden_1, hidden_2, hidden_n, far, own)

    hidden_n2 = flip_e(run.hold(hidden_n), 2)
    hidden_n1, hidden_3 = flip_e(run.hold(hidden_n), 1), flip_e(run.hold(hidden_2), 1)
    over += [ring(run.hold(far[e]), "dp") for e in range(1, batch)]
    far.append(flip(run.hold(near[batch]), "ctx", 2))
    near += [packet(e, run.hold(got_2)) for e in range(batch + 1, local_experts)]
    run.end(hidden_n1, hidden_3, hidden_n2, over, far, near)

    rows_in = [hidden, hidden_n, hidden_2, hidden_n2, hidden_1, hidden_n1, hidden_3, None]
    cots = [cot_b, cot_n, cot_2, cot_n2, cot_1, cot_n1, None, cot_n3]
    w_at = []
    for zc in (z, jnp.bitwise_xor(z, 2)):
        for m in range(nd):
            xc = mod(x - m, nd)
            w_at += [xc * nz + zc, xc * nz + jnp.bitwise_xor(zc, 1), xc * 2 + zc // 2]
    w_at = jnp.stack(w_at + [j * local_experts]).astype(i32)
    rows_in = run.hold(rows_in[:-1]) + [flip_e(run.hold(hidden_n2), 1)]
    cots[6] = flip_e(run.hold(cot_2), 1)
    own += [ring(run.hold(near[e]), "dp") for e in range(batch + 1, local_experts)]
    far += [flip(run.hold(near[e]), "ctx", 2) for e in range(batch + 1, local_experts)]
    over.append(ring(run.hold(far[batch]), "dp"))
    shards = [[(t, e) for e in range(batch)] for t in own[0]]
    shards += [[(t, None) for t in some] for some in zip(*over[:batch])]
    sum_h, sum_o, gb, ga_t, rows_t = experts_rows(w_at, 0, rows_in, cots, shards, None, False)
    run.end(far, own, over, sum_h)

    over += [ring(run.hold(far[e]), "dp") for e in range(batch + 1, local_experts)]
    gw_1 = experts_weights(here, rows_t, cots, run.hold(gb), ga_t, batch, devices)
    run.end(over, gw_1)

    x_0 = dp_reduce_pair(run.hold(gw_1[0]))
    shards = [[(t, None) for t in some] for some in zip(*own[1:])]
    shards += [[(t, None) for t in some] for some in zip(*over[batch:])]
    sum_h, rest_h, sum_o, rest_o, gb, ga_t = experts_rows(
        w_at, batch, run.hold(rows_in), cots, shards, (sum_h, sum_o), True
    )
    run.end(x_0, sum_h)

    rest_h = flip_e(run.hold(rest_h), 1)
    run.end(rest_h)

    part = rows // 2
    all_h = sum_h
    sum_h = [
        add(sum_h[a * part : b * part], rest_h[a * part : b * part])
        for a, b in ((2, 3), (3, 4), (4, 5), (5, 6), (6, 7), (7, 8))
    ]
    by_y, by_z = flip_e(run.hold(sum_h[4]), 2), flip(run.hold(sum_h[5]), "ctx", 1)
    z_0 = flip(run.hold(x_0[1]), "ctx", 2)
    x_1 = dp_reduce_pair(run.hold(gw_1[1]))
    rest_o = flip_e(run.hold(rest_o), 1)
    gw_2 = experts_weights(here, rows_t, cots, run.hold(gb), ga_t, batch, devices)
    run.end(by_y, by_z, z_0, x_1, rest_o, gw_2)

    near_h = flip_e(jnp.concatenate([sum_h[2], add(run.hold(sum_h[3]), by_z)]), 2)
    other_h = flip(jnp.concatenate([add(run.hold(sum_h[0]), by_y), sum_h[1]]), "ctx", 1)
    z_1 = flip(run.hold(x_1[1]), "ctx", 2)
    x_2 = dp_reduce_pair(run.hold(gw_2[0]))
    sum_o = [add(sum_o[a * rows : (a + 1) * rows], rest_o[a * rows : (a + 1) * rows]) for a in range(4)]
    run.end(near_h, other_h, z_1, x_2, sum_o)

    grad_middle, grad_mix, branch, grad_gain_m = join_back(
        scalars, [all_h, rest_h, *run.hold([near_h, other_h])], middle, cot, gain_m, w_out_all
    )
    grad_mixes = [grad_mix[0]] + [shift(grad_mix[k], "ctx", -k) for k in range(1, nz)]
    x_3 = dp_reduce_pair(run.hold(gw_2[1]))
    far_o1 = flip_e(run.hold(sum_o[3]), 2)
    wo_a, wo_b = join_weights(scalars, here, branch, mixes, nd, ne)
    ready = lax.optimization_barrier((x_0[0], x_1[0], branch))
    swap = jnp.stack([add(ready[0][1], z_0[1]), add(ready[1][1], z_1[1])])
    other_o = add(sum_o[1], far_o1)
    run.end(grad_mixes, x_3, other_o, wo_b, swap)

    z_2 = flip(run.hold(x_2[1]), "ctx", 2)
    far_o = flip_e(run.hold(sum_o[2]), 2)
    other_o = flip(run.hold(other_o), "ctx", 1)
    wo_b = flip_e(run.hold(wo_b), 1)
    dqkv = attend_back(scalars, pieces, run.hold(grad_mixes), lse, cos, sin, heads, kvs)
    grad_normed = finish(scalars, dqkv, w_qkv, nz)
    run.end(z_2, far_o, other_o, wo_b, grad_normed)

    z_3 = flip(run.hold(x_3[1]), "ctx", 2)
    gw_a, gw_b = finish_weights(scalars, here, dqkv, run.hold(grad_normed), toks, gain_a, grad_gain_m, nd, ne)
    swap = flip(run.hold(swap), "ctx", 1)
    swap_2 = flip(add(run.hold(x_2[0])[1], z_2[1]), "ctx", 1)
    wo_b = run.hold(wo_b)
    wo_far = flip_e(add(wo_a[1], wo_b[1]), 2)
    run.end(gw_b, swap, swap_2, wo_far, z_3)

    tail = run.hold(grad_normed)
    total = shift(tail[0], "ctx", 1)
    gw_b = flip_e(run.hold(gw_b), 1)
    gw = add(gw_a, gw_b)
    wo_b, wo_far = run.hold([wo_b, wo_far])
    wo = (wo_a[0].astype(F32) + wo_b[0].astype(F32) + wo_far.astype(F32)).astype(BF)
    run.end(total, gw, wo)

    total = shift(add(run.hold(total), tail[1]), "ctx", 1)
    gw_far = flip_e(run.hold(gw[1]), 2)
    wo = dp_reduce(list(run.hold(wo)))
    gw = add(gw[0], gw_far)
    run.end(total, gw, wo)

    total = shift(add(run.hold(total), tail[2]), "ctx", 1)
    gw = dp_reduce(list(run.hold(gw)))
    run.end(total, gw)

    swap_3 = flip(add(run.hold(x_3[0])[1], z_3[1]), "ctx", 1)
    mine = jnp.concatenate(run.hold([gw, wo]), axis=2)
    parts = [pick(mine, z)] + [shift(pick(mine, mod(z + k, nz)), "ctx", k) for k in range(1, nz)]

    gn = tail[3].astype(F32) + total.astype(F32)
    expert_sum = sum_o[0].astype(F32) + far_o.astype(F32) + other_o.astype(F32)
    mixed_out = (middle + residual_scale * expert_sum).astype(BF)
    q_end, k_end, v_end = qw, qw + kw, qw + 2 * kw
    gains = sum(p[:, v_end : v_end + 2].astype(F32) for p in parts)
    grad_out = sum(p[:, v_end + 128 :].astype(F32) for p in parts)
    order = jnp.stack([p[:, :v_end] for p in parts])
    order = [pick(order, mod(z - p, nz)).astype(F32) for p in range(nz)]
    grad_query = jnp.concatenate([g[:, :q_end] for g in order], axis=1)
    grad_key = jnp.concatenate([g[:, q_end:k_end] for g in order], axis=1)
    grad_value = jnp.concatenate([g[:, k_end:] for g in order], axis=1)

    grads_in, grads_down = whole(
        [
            (x_0[0], z_0, swap[0]), (x_1[0], z_1, swap[1]), (x_2[0], z_2, swap_2), (x_3[0], z_3, swap_3)
        ],
        odd,
        devices,
    )

    t = tok.astype(F32)
    inv = rms(t)
    normal = t * inv
    u = gn * gain_a
    grad_tokens = grad_middle + inv * (u - normal * jnp.mean(u * normal, axis=-1, keepdims=True))
    return (
        mixed_out[None],
        grad_tokens[None],
        gains[:, 0],
        grad_query,
        grad_key,
        grad_value,
        grad_out.astype(F32),
        gains[:, 1],
        grads_in,
        grads_down,
    )


def solution(mesh):
    every = ("dp", "ctx", "exp")
    return jax.shard_map(
        per_device,
        mesh=mesh,
        in_specs=(
            P(("dp", "exp"), "ctx", None),
            P(),
            P(every, None),
            P(every, None),
            P(every, None),
            P(every, None),
            P(),
            P("exp", ("dp", "ctx"), None),
            P("exp", ("dp", "ctx"), None),
            P(("dp", "exp"), "ctx", None),
            P(("dp", "exp"), "ctx", None),
            P(("dp", "exp"), None),
            P(("dp", "exp"), "ctx", None),
        ),
        out_specs=(
            P(("dp", "exp"), "ctx", None),
            P(("dp", "exp"), "ctx", None),
            P(every),
            P(every, None),
            P(every, None),
            P(every, None),
            P(every, None),
            P(every),
            P("exp", ("dp", "ctx"), None),
            P("exp", ("dp", "ctx"), None),
        ),
        check_vma=False,
    )
```

```python
import functools

import jax
import jax.numpy as jnp
from jax import lax
from jax.experimental import pallas as pl
from jax.experimental.pallas import tpu as pltpu
from jax.sharding import PartitionSpec as P

HEADS = 24
KV_HEADS = 8
HEAD_DIM = 64
FF = 512
TOP = 8

eps_norm = 1e-06
score_scale = 0.015625
residual_scale = 0.22
rope_base = 10000.0

BF = jnp.bfloat16
F32 = jnp.float32
SCALE = 3
VMEM_LIMIT = 60 * 1024 * 1024
ANY = pl.BlockSpec(memory_space=pl.ANY)
VM = pl.BlockSpec(memory_space=pltpu.VMEM)
SM = pl.BlockSpec(memory_space=pltpu.SMEM)
NN = (((1,), (0,)), ((), ()))
NT = (((1,), (1,)), ((), ()))
TN = (((0,), (0,)), ((), ()))


def mm(a, b, dims=NN):
    return lax.dot_general(a, b, dims, preferred_element_type=F32)


def params(**kw):
    return pltpu.CompilerParams(vmem_limit_bytes=VMEM_LIMIT, **kw)


def cost(flops, nbytes, trans=0):
    return pl.CostEstimate(
        flops=int(flops / SCALE), bytes_accessed=int(nbytes / SCALE), transcendentals=0
    )


def shift(x, axis, by):
    n = lax.axis_size(axis)
    return lax.ppermute(x, axis, [(i, (i + by) % n) for i in range(n)])


def flip(x, axis, mask):
    n = lax.axis_size(axis)
    return lax.ppermute(x, axis, [(i, i ^ mask) for i in range(n)])


class Stages:
    def __init__(self, token):
        self.token = token

    def hold(self, x):
        leaves, tree = jax.tree.flatten(x)
        leaves = [lax.optimization_barrier((leaf, self.token))[0] for leaf in leaves]
        return jax.tree.unflatten(tree, leaves)

    def end(self, *outs):
        self.token = lax.optimization_barrier((self.token, *jax.tree.leaves(outs)))[0]


def ring(x, axis):
    out = [x]
    for _ in range(lax.axis_size(axis) - 1):
        out.append(shift(out[-1], axis, 1))
    return out


def hop(x, pairs):
    return lax.ppermute(x, "ctx", pairs)


UP, DOWN = [(0, 1), (1, 2), (2, 3)], [(1, 0), (2, 1), (3, 2)]
ACROSS = [(0, 2), (1, 3), (2, 0), (3, 1)]
INNER, OUTER = [(0, 1), (3, 2)], [(1, 0), (2, 3)]


def line_places(z):
    return [z, jnp.bitwise_xor(z, 2), jnp.where(z == 0, 3, z - 1), jnp.where(z == 3, 0, z + 1)]


def line_gather(across, below, above, end, x):
    z = lax.axis_index("ctx")
    return [x, across, jnp.where(z == 0, end, below), jnp.where(z == 3, end, above)]


def add(a, b):
    return (a.astype(F32) + b.astype(F32)).astype(BF)


def pick(x, index, dim=0):
    return lax.dynamic_index_in_dim(x, index, dim, False)


def dp_reduce(parts):
    n = lax.axis_size("dp")
    total = parts[n - 1]
    for k in range(1, n):
        total = add(shift(total, "dp", 1), parts[n - 1 - k])
    return total


def dp_reduce_pair(parts):
    n = lax.axis_size("dp")
    total = parts[n - 1]
    for k in range(1, n - 1):
        total = add(shift(total, "dp", 1), parts[n - 1 - k])
    if n == 1:
        return [total[0], total[1]]
    total = shift(total, "dp", 1)
    return [add(total[0], parts[0][0]), add(total[1], parts[0][1])]


def assemble(found, places):
    found = [t.reshape(-1, *t.shape[-2:]) for t in found]
    each, rows, width = found[0].shape
    count = each * len(found)
    total = count * rows
    if rows % 16:
        blocks = jnp.concatenate(found)
        return jnp.zeros_like(blocks).at[places].set(blocks).reshape(total, width)

    def body(places_ref, *refs):
        refs, out_ref, sems = refs[:-2], refs[-2], refs[-1]
        copies = []
        for i in range(count):
            at = pl.multiple_of(places_ref[i] * rows, rows)
            copies.append(
                pltpu.make_async_copy(refs[i // each].at[i % each], out_ref.at[pl.ds(at, rows), :], sems.at[i])
            )
        for copy in copies:
            copy.start()
        for copy in copies:
            copy.wait()

    return pl.pallas_call(
        body,
        out_shape=jax.ShapeDtypeStruct((total, width), found[0].dtype),
        in_specs=[SM] + [ANY] * len(found),
        out_specs=VM,
        scratch_shapes=[pltpu.SemaphoreType.DMA((count,))],
        compiler_params=params(),
        cost_estimate=cost(0, 4 * total * width),
        name="assemble",
    )(places, *found)


def rms(v):
    return lax.rsqrt(jnp.mean(v * v, axis=-1, keepdims=True) + eps_norm)


def turn(block, cos, sin):
    lane = lax.broadcasted_iota(jnp.int32, block.shape, 1)
    partner = jnp.where(
        (lane & 63) < 32, pltpu.roll(block, 96, 1), pltpu.roll(block, 32, 1)
    )
    return block * cos + partner * sin


def project(toks, gain, w, cos, sin, places):
    rows, d = toks[0].shape
    n = w.shape[1]
    turned = n - 128
    count = len(toks)

    def body(at_ref, gain_ref, w_ref, cos_ref, sin_ref, *refs):
        for i in range(count):
            tok_ref, out_ref = refs[i], refs[count + i]
            at = pl.ds(pl.multiple_of(at_ref[i] * rows, rows), rows)
            cosine, sine = cos_ref[at, :], sin_ref[at, :]
            t = tok_ref[...].astype(F32)
            normed = (t * rms(t) * gain_ref[...]).astype(BF)
            u = mm(normed, w_ref[...])
            for b in range(0, turned, 128):
                out_ref[:, b : b + 128] = turn(u[:, b : b + 128], cosine, sine).astype(BF)
            out_ref[:, turned:] = u[:, turned:].astype(BF)

    return pl.pallas_call(
        body,
        out_shape=[jax.ShapeDtypeStruct((rows, n), BF)] * count,
        in_specs=[SM] + [VM] * (4 + count),
        out_specs=[VM] * count,
        compiler_params=params(),
        cost_estimate=cost(2 * count * rows * d * n, 2 * d * n + 4 * count * rows * d),
        name="project",
    )(places, gain, w, cos, sin, *toks)


def swapped(e):
    return (e & 1) * 2 + (e >> 1)


def split_store(a_ref, b_ref, e, at, value):
    @pl.when(e < 2)
    def _():
        a_ref[(e, *at)] = value

    @pl.when(e >= 2)
    def _():
        b_ref[(e - 2, *at)] = value


def lower_half(shape):
    return lax.broadcasted_iota(jnp.int32, shape, 1) < 64


def stage_heads(block, dst, rows_at, heads, factor):
    rows = block.shape[0]
    low = lower_half((rows, 128))
    for h in range(heads):
        part = block[:, (h // 2) * 128 : (h // 2 + 1) * 128].astype(F32) * factor
        keep = low if h % 2 == 0 else jnp.logical_not(low)
        dst[h, rows_at, :] = jnp.where(keep, part, 0.0).astype(BF)


def doubled(block):
    block = block.astype(F32)
    low = lower_half(block.shape)
    other = pltpu.roll(block, 64, 1)
    return jnp.where(low, block, other), jnp.where(low, other, block)


def allowed_mask(s_ref, keys, rows, first):
    q = lax.broadcasted_iota(jnp.int32, (1, rows), 1) + first
    begin = jnp.zeros_like(q)
    for i in range(5, s_ref.shape[0] - 1):
        begin = jnp.where(q >= s_ref[i], jnp.maximum(begin, s_ref[i]), begin)
    k = lax.broadcasted_iota(jnp.int32, (keys, rows), 0)
    return (k >= begin) & (k <= q)


def attend(scalars, pieces, heads, kvs):
    blocks = len(pieces)
    rows, width = pieces[0].shape
    span = blocks * rows
    qw = heads * HEAD_DIM
    share = heads // kvs

    def body(s_ref, *refs):
        ins, outs, (lse_ref, qs, kd, vd, vt, ob) = refs[:blocks], refs[blocks : 2 * blocks], refs[2 * blocks :]
        me = s_ref[4]
        for k in range(blocks):
            at = pl.ds(pl.multiple_of(s_ref[k] * rows, rows), rows)
            block = ins[k][...]
            stage_heads(block, qs, at, heads, score_scale)
            for i, x in enumerate(doubled(block[:, qw : qw + 128])):
                kd[i, at, :] = x.astype(BF)
            for i, x in enumerate(doubled(block[:, qw + 128 : qw + 256])):
                vd[i, at, :] = x
        for i in range(kvs):
            vt[i] = vd[i].T.astype(BF)

        def one(h, _):
            kv = h // share
            for p in range(blocks):
                keys = (p + 1) * rows
                q = qs[h, p * rows : (p + 1) * rows, :]
                s = mm(kd[kv, :keys, :], q, NT)
                s = jnp.where(allowed_mask(s_ref, keys, rows, p * rows), s, -1e30)
                peak = jnp.max(s, axis=0, keepdims=True)
                e = jnp.exp(s - peak)
                total = jnp.sum(e, axis=0, keepdims=True)
                o = mm(vt[kv, :, :keys], e.astype(BF)) / total
                ob[h, p * rows : (p + 1) * rows, :] = o.T
                lse_ref[pl.ds(h, 1), p * rows : (p + 1) * rows] = peak + jnp.log(total)
            return 0

        def some(i, _):
            for u in range(share):
                one(i * share + u, 0)
            return 0

        lax.fori_loop(0, kvs, some, 0)
        low = lower_half((rows, 128))
        for k in range(blocks):
            at = pl.ds(pl.multiple_of(lax.rem(me + k, blocks) * rows, rows), rows)
            for b in range(heads // 2):
                outs[k][:, b * 128 : (b + 1) * 128] = jnp.where(
                    low, ob[2 * b, at, :], ob[2 * b + 1, at, :]
                ).astype(BF)

    pairs = heads * rows * rows * blocks * (blocks + 1) // 2
    *mixes, lse = pl.pallas_call(
        body,
        out_shape=[jax.ShapeDtypeStruct((rows, qw), BF)] * blocks + [jax.ShapeDtypeStruct((8, span), F32)],
        in_specs=[SM] + [VM] * blocks,
        out_specs=[VM] * (blocks + 1),
        scratch_shapes=[
            pltpu.VMEM((heads, span, 128), BF),
            pltpu.VMEM((kvs, span, 128), BF),
            pltpu.VMEM((kvs, span, 128), F32),
            pltpu.VMEM((kvs, 128, span), BF),
            pltpu.VMEM((heads, span, 128), F32),
        ],
        compiler_params=params(),
        cost_estimate=cost(pairs * 1024, 4 * span * width, pairs),
        name="attend",
    )(scalars, *pieces)
    return mixes, lse


def attend_back(scalars, pieces, grads, lse, cos, sin, heads, kvs):
    blocks = len(pieces)
    rows, width = pieces[0].shape
    span = blocks * rows
    qw = heads * HEAD_DIM
    share = heads // kvs

    def body(s_ref, *refs):
        ins, gins = refs[:blocks], refs[blocks : 2 * blocks]
        lse_ref, cos_ref, sin_ref, out_ref, qs, gs, kd, kf, kt, vd, dk, dv, dq = refs[2 * blocks :]
        me = s_ref[4]
        for k in range(blocks):
            at = pl.ds(pl.multiple_of(s_ref[k] * rows, rows), rows)
            block = ins[k][...]
            stage_heads(block, qs, at, heads, score_scale)
            for i, x in enumerate(doubled(block[:, qw : qw + 128])):
                kd[i, at, :] = x.astype(BF)
                kf[i, at, :] = x
            for i, x in enumerate(doubled(block[:, qw + 128 : qw + 256])):
                vd[i, at, :] = x.astype(BF)
            at = pl.ds(pl.multiple_of(lax.rem(me + k, blocks) * rows, rows), rows)
            stage_heads(gins[k][...], gs, at, heads, 1.0)
        for i in range(kvs):
            kt[i] = kf[i].T.astype(BF)
        dk[...] = jnp.zeros_like(dk)
        dv[...] = jnp.zeros_like(dv)

        def one(h, _):
            kv = h // share
            for p in range(blocks):
                keys = (p + 1) * rows
                at = slice(p * rows, (p + 1) * rows)
                q = qs[h, at, :]
                g = gs[h, at, :]
                s = mm(kd[kv, :keys, :], q, NT)
                log_total = lse_ref[pl.ds(h, 1), at]
                chances = jnp.where(
                    allowed_mask(s_ref, keys, rows, p * rows), jnp.exp(s - log_total), 0.0
                )
                gp = mm(vd[kv, :keys, :], g, NT)
                row_dot = jnp.sum(chances * gp, axis=0, keepdims=True)
                ds = (chances * (gp - row_dot)).astype(BF)
                dq[h, at, :] = mm(kt[kv, :, :keys], ds).T
                dk[kv, :keys, :] += mm(ds, q)
                dv[kv, :keys, :] += mm(chances.astype(BF), g)
            return 0

        for h in range(heads):
            one(h, 0)
        low = lower_half((rows, 128))
        for p in range(blocks):
            at = slice(p * rows, (p + 1) * rows)
            cosine, sine = cos_ref[at, :], -sin_ref[at, :]
            for b in range(heads // 2):
                x = jnp.where(low, dq[2 * b, at, :], dq[2 * b + 1, at, :]) * score_scale
                out_ref[at, b * 128 : (b + 1) * 128] = turn(x, cosine, sine).astype(BF)
            k0, k1, v0, v1 = dk[0, at, :], dk[1, at, :], dv[0, at, :], dv[1, at, :]
            k0, k1 = k0 + pltpu.roll(k0, 64, 1), k1 + pltpu.roll(k1, 64, 1)
            v0, v1 = v0 + pltpu.roll(v0, 64, 1), v1 + pltpu.roll(v1, 64, 1)
            out_ref[at, qw : qw + 128] = turn(jnp.where(low, k0, k1), cosine, sine).astype(BF)
            out_ref[at, qw + 128 : qw + 256] = jnp.where(low, v0, v1).astype(BF)

    pairs = heads * rows * rows * blocks * (blocks + 1) // 2
    return pl.pallas_call(
        body,
        out_shape=jax.ShapeDtypeStruct((span, width), BF),
        in_specs=[SM] + [VM] * (2 * blocks + 3),
        out_specs=VM,
        scratch_shapes=[
            pltpu.VMEM((heads, span, 128), BF),
            pltpu.VMEM((heads, span, 128), BF),
            pltpu.VMEM((kvs, span, 128), BF),
            pltpu.VMEM((kvs, span, 128), F32),
            pltpu.VMEM((kvs, 128, span), BF),
            pltpu.VMEM((kvs, span, 128), BF),
            pltpu.VMEM((kvs, span, 128), F32),
            pltpu.VMEM((kvs, span, 128), F32),
            pltpu.VMEM((heads, span, 128), F32),
        ],
        compiler_params=params(),
        cost_estimate=cost(pairs * 2560, 8 * span * width, pairs),
        name="attend_back",
    )(scalars, *pieces, *grads, lse, cos, sin)


def join(scalars, mixes, w_out, tok, gain):
    blocks = len(mixes)
    rows, part = mixes[0].shape
    d = tok.shape[1]

    def body(s_ref, *refs):
        ins, (w_ref, tok_ref, gain_ref, mid_ref, hid_ref) = refs[:blocks], refs[blocks:]
        me = s_ref[4]
        branch = jnp.zeros((rows, d), F32)
        for k in range(blocks):
            at = pl.ds(pl.multiple_of(lax.rem(me - k + blocks, blocks) * part, part), part)
            branch = branch + mm(ins[k][...], w_ref[at, :])
        middle = tok_ref[...].astype(F32) + residual_scale * branch
        mid_ref[...] = middle
        hid_ref[...] = (middle * rms(middle) * gain_ref[...]).astype(BF)

    return pl.pallas_call(
        body,
        out_shape=(jax.ShapeDtypeStruct((rows, d), F32), jax.ShapeDtypeStruct((rows, d), BF)),
        in_specs=[SM] + [VM] * (blocks + 3),
        out_specs=(VM, VM),
        compiler_params=params(),
        cost_estimate=cost(2 * rows * d * d, 2 * d * d + 10 * rows * d),
        name="join",
    )(scalars, *mixes, w_out, tok, gain)


def join_back(scalars, addends, middle, cot, gain, w_out):
    blocks = 4
    rows, d = middle.shape
    part = d // blocks
    count = len(addends)

    def body(s_ref, *refs):
        ins, (mid_ref, cot_ref, gain_ref, w_any, gmid_ref, br_ref, gg_ref, *outs) = refs[:count], refs[count:]
        *outs, w_ref, sems = outs
        me = s_ref[4]
        spans = [
            pl.ds(pl.multiple_of(lax.rem(me - k + blocks, blocks) * part, part), part) for k in range(blocks)
        ]
        copies = [
            pltpu.make_async_copy(w_any.at[spans[k], :], w_ref.at[k], sems.at[k]) for k in range(blocks)
        ]
        for copy in copies:
            copy.start()
        grad_hidden = sum(t[...].astype(F32) for t in ins)
        middle = mid_ref[...]
        inv = rms(middle)
        normal = middle * inv
        gg_ref[...] = jnp.sum(grad_hidden * normal, axis=0, keepdims=True)
        u = grad_hidden * gain_ref[...]
        grad_middle = cot_ref[...] + inv * (u - normal * jnp.mean(u * normal, axis=-1, keepdims=True))
        gmid_ref[...] = grad_middle
        br_ref[...] = (residual_scale * grad_middle).astype(BF)
        for k in range(blocks):
            copies[k].wait()
            outs[k][...] = mm(br_ref[...], w_ref[k], NT).astype(BF)

    front = lambda t: pl.BlockSpec((rows, d), lambda i: (0, 0))
    fixed = lambda *shape: pl.BlockSpec(shape, lambda i: (0, 0))
    grad_middle, branch, gain_grad, *mixes = pl.pallas_call(
        body,
        grid=(1,),
        out_shape=[
            jax.ShapeDtypeStruct((rows, d), F32),
            jax.ShapeDtypeStruct((rows, d), BF),
            jax.ShapeDtypeStruct((1, d), F32),
        ]
        + [jax.ShapeDtypeStruct((rows, part), BF)] * blocks,
        in_specs=[SM]
        + [front(t) for t in addends]
        + [fixed(rows, d), fixed(rows, d), fixed(1, d), ANY],
        out_specs=[fixed(rows, d), fixed(rows, d), fixed(1, d)] + [fixed(rows, part)] * blocks,
        scratch_shapes=[pltpu.VMEM((blocks, part, d), BF), pltpu.SemaphoreType.DMA((blocks,))],
        compiler_params=params(),
        cost_estimate=cost(2 * rows * d * d, 2 * d * d + 18 * rows * d),
        name="join_back",
    )(scalars, *addends, middle, cot, gain, w_out)
    return grad_middle, mixes, branch, gain_grad


def join_weights(scalars, here, branch, mixes, nd, ne):
    blocks = len(mixes)
    rows, part = mixes[0].shape
    d = branch.shape[1]
    w_rows = d // (nd * blocks * ne)

    def body(s_ref, here_ref, br_ref, *refs):
        ins, (gwa_ref, gwb_ref) = refs[:blocks], refs[blocks:]
        me = s_ref[4]
        for k in range(blocks):
            gw = mm(ins[k][...], br_ref[...], TN)
            for i in range(part // w_rows):
                q = lax.rem(me - k + blocks, blocks) * (part // w_rows) + i
                e = swapped(jnp.bitwise_xor(lax.rem(q, ne), here_ref[3]))
                b = lax.div(q, ne)
                m = lax.rem(lax.div(b, blocks) - here_ref[0] + nd, nd)
                put = gw[i * w_rows : (i + 1) * w_rows, :].astype(BF)
                split_store(gwa_ref, gwb_ref, e, (m, lax.rem(b, blocks)), put)

    return pl.pallas_call(
        body,
        out_shape=(jax.ShapeDtypeStruct((2, nd, blocks, w_rows, d), BF),) * 2,
        in_specs=[SM, SM] + [VM] * (1 + blocks),
        out_specs=(VM, VM),
        compiler_params=params(),
        cost_estimate=cost(2 * rows * d * d, 2 * d * d + 4 * rows * d),
        name="join_weights",
    )(scalars, here, branch, *mixes)


def halves(w, odd, devices):
    n, r, width = w.shape
    unit = FF // devices
    if 2 * unit != 128:
        parts = w.reshape(n, r, 2, devices // 4, 2, 2, unit)
        parts = jnp.transpose(parts, (5, 0, 1, 2, 3, 4, 6)).reshape(2, n, r, FF)
        return pick(parts, odd), pick(parts, 1 - odd)

    def body(odd_ref, w_ref, mine_ref, their_ref):
        low = lower_half((r, 128))
        even = odd_ref[0] == 0
        for m in range(width // 256):
            a = w_ref[0, :, 2 * m * 128 : (2 * m + 1) * 128].astype(F32)
            b = w_ref[0, :, (2 * m + 1) * 128 : (2 * m + 2) * 128].astype(F32)
            evens = jnp.where(low, a, pltpu.roll(b, 64, 1))
            odds = jnp.where(low, pltpu.roll(a, 64, 1), b)
            at = slice(m * 128, (m + 1) * 128)
            mine_ref[0, :, at] = jnp.where(even, evens, odds).astype(BF)
            their_ref[0, :, at] = jnp.where(even, odds, evens).astype(BF)

    spec = pl.BlockSpec((1, r, FF), lambda e: (e, 0, 0))
    return pl.pallas_call(
        body,
        grid=(n,),
        out_shape=(jax.ShapeDtypeStruct((n, r, FF), BF),) * 2,
        in_specs=[SM, pl.BlockSpec((1, r, width), lambda e: (e, 0, 0))],
        out_specs=(spec, spec),
        compiler_params=params(),
        cost_estimate=cost(0, 4 * n * r * width),
        name="halves",
    )(odd[None].astype(jnp.int32), w)


def whole(parts, odd, devices):
    count = len(parts)
    _, r, width = parts[0][0].shape
    r3 = r // 3
    unit = FF // devices

    def plain(own, other, theirs):
        total = own.astype(F32) + other.astype(F32)
        theirs = theirs.astype(F32)
        pair = jnp.stack([jnp.where(odd == 0, total[0], theirs), jnp.where(odd == 0, theirs, total[0])])
        pair = pair.reshape(2, r, 2, devices // 4, 2, unit)
        down = [total[2, b * r3 : (b + 1) * r3] for b in range(3)]
        return jnp.transpose(pair, (1, 2, 3, 4, 0, 5)).reshape(r, 2 * width), jnp.concatenate(down, axis=1)

    if 2 * unit != 128:
        done = [plain(*p) for p in parts]
        return jnp.stack([p[0] for p in done]), jnp.stack([p[1] for p in done])

    def body(odd_ref, own_ref, other_ref, their_ref, *refs):
        in_ref, down_ref = refs[-2], refs[-1]
        low = lower_half((r, 128))
        even = odd_ref[0] == 0
        for m in range(width // 128):
            at = slice(m * 128, (m + 1) * 128)
            mine = own_ref[0, :, at].astype(F32) + other_ref[0, :, at].astype(F32)
            their = their_ref[:, at].astype(F32)
            evens, odds = jnp.where(even, mine, their), jnp.where(even, their, mine)
            in_ref[0, :, 2 * m * 128 : (2 * m + 1) * 128] = jnp.where(low, evens, pltpu.roll(odds, 64, 1))
            in_ref[0, :, (2 * m + 1) * 128 : (2 * m + 2) * 128] = jnp.where(
                low, pltpu.roll(evens, 64, 1), odds
            )
        for b in range(3):
            at = slice(b * r3, (b + 1) * r3)
            down_ref[0, :, b * width : (b + 1) * width] = (
                own_ref[2, at, :].astype(F32) + other_ref[2, at, :].astype(F32)
            )

    done = ()
    for e, (own, other, theirs) in enumerate(parts):
        fixed = lambda *shape: pl.BlockSpec(shape, lambda i: (0,) * len(shape))
        done = pl.pallas_call(
            body,
            grid=(1,),
            out_shape=(
                jax.ShapeDtypeStruct((count, r, 2 * width), F32),
                jax.ShapeDtypeStruct((count, r3, 3 * width), F32),
            ),
            in_specs=[SM, fixed(3, r, width), fixed(3, r, width), fixed(r, width)] + [ANY] * len(done),
            out_specs=(
                pl.BlockSpec((1, r, 2 * width), lambda i, e=e: (e, 0, 0)),
                pl.BlockSpec((1, r3, 3 * width), lambda i, e=e: (e, 0, 0)),
            ),
            input_output_aliases={4: 0, 5: 1} if done else {},
            compiler_params=params(),
            cost_estimate=cost(0, 20 * r * width),
            name="whole",
        )(odd[None].astype(jnp.int32), own, other, theirs, *done)
    return done


def experts_rows(places, which, rows_in, cots, shards, sums, last):
    piece, d = rows_in[0].shape
    group = 1
    rows = piece * group
    tiles = len(rows_in) // group
    total = rows * tiles
    count, n = len(shards), len(shards[0])
    r, width = shards[0][0][0].shape[-2:]
    arrays = {id(t): t for shard in shards for t, _ in shard}
    slot = {key: k for k, key in enumerate(arrays)}
    arrays = list(arrays.values())
    half = width // 2
    r3 = r // 3
    first = sums is None

    def body(places_ref, *refs):
        n_in = tiles * group
        h_refs, c_refs, refs = refs[:n_in], refs[n_in : 2 * n_in], refs[2 * n_in :]
        w_refs, refs = refs[: len(arrays)], refs[len(arrays) :]
        if not first:
            in_h, in_o, refs = refs[0], refs[1], refs[2:]
        if last:
            out_h, rest_h, out_o, rest_o, gb_ref, gat_ref, *refs = refs
        else:
            out_h, out_o, gb_ref, gat_ref, *refs = refs
        if first:
            ht_ref, *refs = refs
        wiv, wdv, ga_ref, hv, cv, sems, row_sems = refs
        t = pl.program_id(0)
        moves = []
        for i in range(n_in):
            at = pl.ds(i % group * piece, piece)
            moves.append(
                (
                    pltpu.make_async_copy(h_refs[i], hv.at[i // group, at, :], row_sems.at[0, i]),
                    pltpu.make_async_copy(c_refs[i], cv.at[i // group, at, :], row_sems.at[1, i]),
                )
            )

        @pl.when(t == 0)
        def _():
            copies = []
            for i in range(count):
                for e in range(n):
                    array, which_of = shards[i][e]
                    source = w_refs[slot[id(array)]]
                    source = source if which_of is None else source.at[which_of]
                    parts = []
                    for b in range(2):
                        at = pl.multiple_of(places_ref[3 * i + b] * r, r)
                        parts.append((source.at[2 * b], wiv.at[pl.ds(at, r), e * width : (e + 1) * width]))
                    at = pl.multiple_of(places_ref[3 * i + 2] * r3 + e * half, r3)
                    for b in range(3):
                        parts.append(
                            (
                                source.at[1, b * r3 : (b + 1) * r3, :],
                                wdv.at[pl.ds(at, r3), b * width : (b + 1) * width],
                            )
                        )
                    for k, (a, b) in enumerate(parts):
                        copies.append(pltpu.make_async_copy(a, b, sems.at[i, e, k]))
            for copy in copies:
                copy.start()
            for a, b in moves[:group]:
                a.start()
                b.start()
            for copy in copies:
                copy.wait()
            for a, b in moves[group:]:
                a.start()
                b.start()

        for i in range(tiles):

            @pl.when(t == i)
            def _():
                for a, b in moves[i * group : (i + 1) * group]:
                    a.wait()
                    b.wait()

        h = hv[t]
        c = cv[t, :, :d]
        gates = cv[t, :, d:].astype(F32)
        lane = lax.broadcasted_iota(jnp.int32, gates.shape, 1) - places_ref[3 * count]
        for e in range(n):
            g = jnp.sum(jnp.where(lane == which + e, gates, 0.0), axis=1, keepdims=True)
            gu = mm(h, wiv[:, e * width : (e + 1) * width])
            gate, up = gu[:, :half], gu[:, half:]
            sg = jax.nn.sigmoid(gate)
            silu = gate * sg
            ga = mm(c, wdv[e * half : (e + 1) * half, :], NT) * g
            ga_ref[:, e * half : (e + 1) * half] = (silu * up * g).astype(BF)
            gb_ref[:, e * width : e * width + half] = (ga * up * (sg + silu * (1.0 - sg))).astype(BF)
            gb_ref[:, e * width + half : (e + 1) * width] = (ga * silu).astype(BF)
        o = mm(ga_ref[...], wdv[...])
        gh = mm(gb_ref[...], wiv[...], NT)
        gat_ref[...] = ga_ref[...].T
        if first:
            ht_ref[...] = h.T
        if not first:
            o = o + in_o[...].astype(F32)
            gh = gh + in_h[...].astype(F32)
        if last:

            @pl.when(t < tiles // 2)
            def _():
                out_o[...] = o.astype(BF)
                out_h[...] = gh.astype(BF)

            @pl.when(t >= tiles // 2)
            def _():
                rest_o[...] = o.astype(BF)
                rest_h[...] = gh.astype(BF)

        else:
            out_o[...] = o.astype(BF)
            out_h[...] = gh.astype(BF)

    tile = lambda c: pl.BlockSpec((rows, c), lambda t: (t, 0))
    flat = lambda c: pl.BlockSpec((c, rows), lambda t: (0, t))
    if last:
        sum_shapes = (jax.ShapeDtypeStruct((total // 2, d), BF),) * 4
        front = pl.BlockSpec((rows, d), lambda t: (jnp.minimum(t, tiles // 2 - 1), 0))
        back = pl.BlockSpec((rows, d), lambda t: (jnp.maximum(t - tiles // 2, 0), 0))
        sum_specs = (front, back, front, back)
    else:
        sum_shapes = (jax.ShapeDtypeStruct((total, d), BF),) * 2
        sum_specs = (tile(d), tile(d))
    return pl.pallas_call(
        body,
        grid=(tiles,),
        out_shape=sum_shapes
        + (
            jax.ShapeDtypeStruct((total, n * width), BF),
            jax.ShapeDtypeStruct((n * half, total), BF),
        )
        + ((jax.ShapeDtypeStruct((d, total), BF),) if first else ()),
        in_specs=[SM]
        + [ANY] * (2 * len(rows_in) + len(arrays))
        + ([] if first else [tile(d), tile(d)]),
        out_specs=sum_specs + (tile(n * width), flat(n * half)) + ((flat(d),) if first else ()),
        scratch_shapes=[
            pltpu.VMEM((d, n * width), BF),
            pltpu.VMEM((n * half, d), BF),
            pltpu.VMEM((rows, n * half), BF),
            pltpu.VMEM((tiles, rows, d), BF),
            pltpu.VMEM((tiles, rows, cots[0].shape[1]), BF),
            pltpu.SemaphoreType.DMA((count, n, 5)),
            pltpu.SemaphoreType.DMA((2, len(rows_in))),
        ],
        compiler_params=params(),
        cost_estimate=cost(6 * n * total * d * width, 50e6, n * total * half),
        name="experts_rows",
    )(places, *rows_in, *cots, *arrays, *(() if first else sums))


def experts_weights(scalars, rows_t, cots, gb, ga_t, n, devices):
    d, total = rows_t.shape
    width, half = gb.shape[1] // n, ga_t.shape[0] // n
    r = d // devices
    r3 = r // 3
    nd = devices // 4
    tiles = len(cots)
    rows = total // tiles

    def body(s_ref, h_any, gb_any, ga_any, *refs):
        c_refs, refs = refs[:tiles], refs[tiles:]
        outs, (down, h_ref, gb_ref, ga_ref, c_ref, stage, sems, c_sems, out_sems) = refs[: n * nd], refs[n * nd :]
        ahead = [lax.rem(s_ref[0] + k, nd) for k in range(nd)]
        spans = [pl.ds(pl.multiple_of(x * 4 * r, 4 * r), 4 * r) for x in ahead]
        first = [pltpu.make_async_copy(gb_any, gb_ref, sems.at[0])]
        first += [
            pltpu.make_async_copy(h_any.at[spans[k], :], h_ref.at[k], sems.at[1 + k]) for k in range(nd)
        ]
        second = [pltpu.make_async_copy(ga_any, ga_ref, c_sems.at[tiles])]
        second += [
            pltpu.make_async_copy(c_refs[i].at[:, :d], c_ref.at[pl.ds(i * rows, rows), :], c_sems.at[i])
            for i in range(tiles)
        ]
        for copy in first[:2]:
            copy.start()
        first[0].wait()
        for k in range(nd):
            first[1 + k].wait()
            for copy in first[2:] + second if k == 0 else []:
                copy.start()
            part = mm(h_ref[k], gb_ref[...]).astype(BF)
            for z in range(4):
                where = jnp.bitwise_xor(s_ref[2], z // 2)
                slot = jnp.bitwise_xor(s_ref[1], z % 2)
                for e in range(n):
                    stage[e * nd + k, where, slot] = part[z * r : (z + 1) * r, e * width : (e + 1) * width]
        for copy in second:
            copy.wait()
        leaving = []
        for e in range(n):
            down[...] = mm(ga_ref[e * half : (e + 1) * half, :], c_ref[...]).astype(BF)
            for k in range(nd):
                for z in range(2):
                    where = jnp.bitwise_xor(s_ref[2], z)
                    at = pl.ds(pl.multiple_of((2 * ahead[k] + z) * r3, r3), r3)
                    for b in range(3):
                        stage[e * nd + k, where, 2, b * r3 : (b + 1) * r3, :] = down[
                            at, b * width : (b + 1) * width
                        ]
                leaving.append(
                    pltpu.make_async_copy(stage.at[e * nd + k], outs[e * nd + k], out_sems.at[e * nd + k])
                )
                leaving[-1].start()
        for copy in leaving:
            copy.wait()

    outs = pl.pallas_call(
        body,
        out_shape=[jax.ShapeDtypeStruct((2, 3, r, width), BF)] * (n * nd),
        in_specs=[SM] + [ANY] * (3 + tiles),
        out_specs=[ANY] * (n * nd),
        scratch_shapes=[
            pltpu.VMEM((half, d), BF),
            pltpu.VMEM((nd, 4 * r, total), BF),
            pltpu.VMEM((total, n * width), BF),
            pltpu.VMEM((n * half, total), BF),
            pltpu.VMEM((total, d), BF),
            pltpu.VMEM((n * nd, 2, 3, r, width), BF),
            pltpu.SemaphoreType.DMA((1 + nd,)),
            pltpu.SemaphoreType.DMA((tiles + 1,)),
            pltpu.SemaphoreType.DMA((n * nd,)),
        ],
        compiler_params=params(),
        cost_estimate=cost(3 * n * total * d * width, 20e6),
        name="experts_weights",
    )(scalars, rows_t, gb, ga_t, *cots)
    return [outs[e * nd : (e + 1) * nd] for e in range(n)]


def finish(scalars, dqkv, w, blocks):
    total, width = dqkv.shape
    d = w.shape[0]
    rows = total // blocks

    def body(s_ref, dq_ref, w_ref, *outs):
        for k in range(blocks):
            at = lax.rem(s_ref[4] - 1 - k + 2 * blocks, blocks)
            at = pl.ds(pl.multiple_of(at * rows, rows), rows)
            outs[k][...] = mm(dq_ref[at, :], w_ref[...], NT).astype(BF)

    return pl.pallas_call(
        body,
        out_shape=[jax.ShapeDtypeStruct((rows, d), BF)] * blocks,
        in_specs=[SM, VM, VM],
        out_specs=[VM] * blocks,
        compiler_params=params(),
        cost_estimate=cost(2 * total * d * width, 4 * total * d),
        name="finish",
    )(scalars, dqkv, w)


def finish_weights(scalars, here, dqkv, gn, toks, gain, gain_grad, nd, ne):
    blocks = len(toks)
    rows, d = toks[0].shape
    width = dqkv.shape[1]
    w_rows = d // (nd * blocks * ne)

    def body(s_ref, here_ref, dq_ref, gain_ref, gg_ref, *refs):
        ins, gns, (gwa_ref, gwb_ref, acc) = refs[:blocks], refs[blocks : 2 * blocks], refs[2 * blocks :]
        gg = jnp.zeros((1, d), F32)
        for k in range(blocks):
            to = s_ref[k]
            at = pl.ds(pl.multiple_of(to * rows, rows), rows)
            t = ins[k][...].astype(F32)
            normal = t * rms(t)
            normed = (normal * gain_ref[...]).astype(BF)
            gn = gns[(k - 1) % blocks][...].astype(F32)
            gg = gg + jnp.sum(gn * normal, axis=0, keepdims=True)
            part = mm(normed, dq_ref[at, :], TN)
            acc[...] = part if k == 0 else acc[...] + part
        row = lax.broadcasted_iota(jnp.int32, (128, d), 0)
        both = jnp.where(row == 0, gg, jnp.where(row == 1, gg_ref[...], 0.0)).T
        for q in range(d // w_rows):
            e = swapped(jnp.bitwise_xor(q % ne, here_ref[3]))
            m = lax.rem(q // ne // blocks - here_ref[0] + nd, nd)
            at = slice(q * w_rows, (q + 1) * w_rows)
            put = jnp.concatenate([acc[at, :], both[at, :]], axis=1).astype(BF)
            split_store(gwa_ref, gwb_ref, e, (m, q // ne % blocks), put)

    return pl.pallas_call(
        body,
        out_shape=(jax.ShapeDtypeStruct((2, nd, blocks, w_rows, width + 128), BF),) * 2,
        in_specs=[SM, SM] + [VM] * (3 + 2 * blocks),
        out_specs=(VM, VM),
        scratch_shapes=[pltpu.VMEM((d, width), F32)],
        compiler_params=params(),
        cost_estimate=cost(2 * blocks * rows * d * width, 6 * blocks * rows * d),
        name="finish_weights",
    )(scalars, here, dqkv, gain, gain_grad, *toks, *gn)


def per_device(
    tokens,
    gain_attn,
    w_query,
    w_key,
    w_value,
    w_out,
    gain_moe,
    w_in,
    w_down,
    routes,
    gates,
    lengths,
    cotangent,
):
    nd, nz, ne = lax.axis_size("dp"), lax.axis_size("ctx"), lax.axis_size("exp")
    x, z, j = lax.axis_index("dp"), lax.axis_index("ctx"), lax.axis_index("exp")
    rows, d = tokens.shape[1:]
    span = rows * nz
    w_rows = w_query.shape[0]
    heads, kvs = HEADS // nz, KV_HEADS // nz
    qw, kw = heads * HEAD_DIM, kvs * HEAD_DIM
    local_experts = w_in.shape[0]
    experts = local_experts * ne
    i32 = jnp.int32
    mod = lambda v, n: lax.rem(v + 8 * n, n)

    ends = jnp.cumsum(lengths[0]).astype(i32)
    places = [mod(z - k, nz) for k in range(nz)]
    scalars = jnp.concatenate([jnp.stack(places + [z]).astype(i32), ends])
    place = jnp.arange(span, dtype=i32)
    place = place - jnp.max(jnp.where(place[:, None] >= ends[None, :-1], ends[None, :-1], 0), axis=1)
    lane = jnp.arange(128, dtype=i32)
    half = HEAD_DIM // 2
    frequency = rope_base ** (-2.0 * jnp.arange(half, dtype=F32) / HEAD_DIM)
    angles = place.astype(F32)[:, None] * frequency[None, :]
    cos = jnp.tile(jnp.cos(angles), (1, 128 // half))
    sin = jnp.tile(jnp.sin(angles), (1, 128 // half)) * jnp.where((lane & 63) < 32, -1.0, 1.0)[None, :]

    run = Stages(gain_attn)
    gain_a, gain_m = gain_attn[None, :], gain_moe[None, :]
    devices = nd * nz
    odd, zh = jnp.bitwise_and(z, 1), z // 2
    batch = local_experts // 2
    tok, cot = tokens[0], cotangent[0]
    flip_e = lambda v, e: flip(v, "exp", e)

    def row_blocks(found, owners, order):
        at = [
            (mod(x - m, nd) * nz + p) * ne + jnp.bitwise_xor(j, e + 2 * b)
            for e in (0, 1) for b, m in order for p in owners
        ]
        return assemble(found, jnp.stack(at).astype(i32))

    by_m = [(b, m) for m in range(nd) for b in (0, 1)]
    by_b = [(b, m) for b in (0, 1) for m in range(nd)]

    here = jnp.stack([x, odd, zh, j]).astype(i32)

    parts = [
        jnp.concatenate(
            [
                w_query[:, p * qw : (p + 1) * qw],
                w_key[:, p * kw : (p + 1) * kw],
                w_value[:, p * kw : (p + 1) * kw],
            ],
            axis=1,
        )
        for p in range(nz)
    ]
    cut = rows // 2
    toks = [tok, shift(tok, "ctx", 1)]
    w_parts = jnp.stack(parts)
    w_mine = [pick(w_parts, z)] + [shift(pick(w_parts, mod(z + k, nz)), "ctx", k) for k in range(1, nz)]
    run.end(toks, w_mine)

    half_2 = [shift(run.hold(toks[1])[:cut], "ctx", 1)]
    mine_in, their_in = halves(run.hold(w_in), odd, devices)
    down = run.hold(w_down)
    down = jnp.concatenate([down[:, :, b * FF : (b + 1) * FF] for b in range(d // FF)], axis=1)
    w_mine = jnp.stack(w_mine)
    w_mine = jnp.stack([w_mine, flip_e(run.hold(w_mine), 2)])
    line = [hop(run.hold(w_out), pairs) for pairs in (ACROSS, UP, DOWN)]
    run.end(half_2, w_mine, line, mine_in)

    half_2.append(shift(run.hold(toks[1])[cut:], "ctx", 1))
    hits = run.hold(routes)[0][:, :, None] == jnp.arange(128, dtype=i32)[None, None, :]
    dense = jnp.sum(jnp.where(hits, gates[0].astype(F32)[:, :, None], 0.0), axis=1).astype(BF)
    cot_b = jnp.concatenate([(residual_scale * run.hold(cot)).astype(BF), dense], axis=1)
    w_found = ring(run.hold(w_mine), "dp")
    line_end = hop(run.hold(line[0]), OUTER)
    run.end(half_2, w_found, line_end, cot_b)

    toks.append(jnp.concatenate(half_2))
    toks.append(shift(run.hold(toks[2]), "ctx", 1))
    got_1 = flip(run.hold(their_in[:batch]), "ctx", 1)
    w_found = w_found + [flip_e(t, 1) for t in run.hold(w_found)]
    w_line = ring(run.hold(jnp.stack(line_gather(*line, line_end, w_out))), "dp")
    cot_2 = flip_e(run.hold(cot_b), 2)
    w_qkv = row_blocks(w_found, places, by_m)
    at = jnp.stack(places).astype(i32)
    pieces = project(toks[: nz - 1], gain_a, w_qkv, cos, sin, at[: nz - 1])
    run.end(toks, pieces, got_1, w_line, cot_2)

    packet = lambda e, got: jnp.stack([mine_in[e], down[e], got[e % batch]])
    near = [packet(e, got_1) for e in range(batch)]
    far = [flip(run.hold(near[0]), "ctx", 2)]
    own = [ring(run.hold(jnp.stack(near)), "dp")]
    w_line = jnp.stack(w_line)
    w_line = jnp.stack([w_line, flip_e(run.hold(w_line), 2)])
    cot_n = flip(run.hold(cot_b), "ctx", 1)
    pieces = pieces + project([run.hold(toks[3])], gain_a, w_qkv, cos, sin, at[nz - 1 :])
    mix_out, lse = attend(scalars, pieces, heads, kvs)
    run.end(far, own, w_line, cot_n, mix_out)

    mixes = run.hold(mix_out)
    mixes = [mixes[0]] + [shift(mixes[k], "ctx", k) for k in range(1, nz)]
    w_line = [w_line, flip_e(run.hold(w_line), 1)]
    cot_n2 = flip_e(run.hold(cot_n), 2)
    w_out_all = row_blocks(w_line, line_places(z), by_b)
    run.end(mixes, w_out_all, cot_n2)

    cot_1 = flip_e(run.hold(cot_b), 1)
    cot_n1, cot_n3 = flip_e(run.hold(cot_n), 1), flip_e(run.hold(cot_n2), 1)
    got_2 = flip(run.hold(their_in[batch:]), "ctx", 1)
    over = [ring(run.hold(far[0]), "dp")]
    middle, hidden = join(scalars, run.hold(mixes), w_out_all, tok, gain_m)
    run.end(hidden, got_2, over, cot_1, cot_n1, cot_n3)

    hidden_2, hidden_n = flip_e(run.hold(hidden), 2), flip(run.hold(hidden), "ctx", 1)
    far += [flip(run.hold(near[e]), "ctx", 2) for e in range(1, batch)]
    near.append(packet(batch, got_2))
    own.append(ring(run.hold(near[batch]), "dp"))
    hidden_1 = flip_e(run.hold(hidden), 1)
    run.end(hidden_1, hidden_2, hidden_n, far, own)

    hidden_n2 = flip_e(run.hold(hidden_n), 2)
    hidden_n1, hidden_3 = flip_e(run.hold(hidden_n), 1), flip_e(run.hold(hidden_2), 1)
    over += [ring(run.hold(far[e]), "dp") for e in range(1, batch)]
    far.append(flip(run.hold(near[batch]), "ctx", 2))
    near += [packet(e, run.hold(got_2)) for e in range(batch + 1, local_experts)]
    run.end(hidden_n1, hidden_3, hidden_n2, over, far, near)

    rows_in = [hidden, hidden_n, hidden_2, hidden_n2, hidden_1, hidden_n1, hidden_3, None]
    cots = [cot_b, cot_n, cot_2, cot_n2, cot_1, cot_n1, None, cot_n3]
    w_at = []
    for zc in (z, jnp.bitwise_xor(z, 2)):
        for m in range(nd):
            xc = mod(x - m, nd)
            w_at += [xc * nz + zc, xc * nz + jnp.bitwise_xor(zc, 1), xc * 2 + zc // 2]
    w_at = jnp.stack(w_at + [j * local_experts]).astype(i32)
    rows_in = run.hold(rows_in[:-1]) + [flip_e(run.hold(hidden_n2), 1)]
    cots[6] = flip_e(run.hold(cot_2), 1)
    own += [ring(run.hold(near[e]), "dp") for e in range(batch + 1, local_experts)]
    far += [flip(run.hold(near[e]), "ctx", 2) for e in range(batch + 1, local_experts)]
    over.append(ring(run.hold(far[batch]), "dp"))
    shards = [[(t, e) for e in range(batch)] for t in own[0]]
    shards += [[(t, None) for t in some] for some in zip(*over[:batch])]
    sum_h, sum_o, gb, ga_t, rows_t = experts_rows(w_at, 0, rows_in, cots, shards, None, False)
    run.end(far, own, over, sum_h)

    over += [ring(run.hold(far[e]), "dp") for e in range(batch + 1, local_experts)]
    gw_1 = experts_weights(here, rows_t, cots, run.hold(gb), ga_t, batch, devices)
    run.end(over, gw_1)

    x_0 = dp_reduce_pair(run.hold(gw_1[0]))
    shards = [[(t, None) for t in some] for some in zip(*own[1:])]
    shards += [[(t, None) for t in some] for some in zip(*over[batch:])]
    sum_h, rest_h, sum_o, rest_o, gb, ga_t = experts_rows(
        w_at, batch, run.hold(rows_in), cots, shards, (sum_h, sum_o), True
    )
    run.end(x_0, sum_h)

    rest_h = flip_e(run.hold(rest_h), 1)
    run.end(rest_h)

    part = rows // 2
    all_h = sum_h
    sum_h = [
        add(sum_h[a * part : b * part], rest_h[a * part : b * part])
        for a, b in ((2, 3), (3, 4), (4, 5), (5, 6), (6, 7), (7, 8))
    ]
    by_y, by_z = flip_e(run.hold(sum_h[4]), 2), flip(run.hold(sum_h[5]), "ctx", 1)
    z_0 = flip(run.hold(x_0[1]), "ctx", 2)
    x_1 = dp_reduce_pair(run.hold(gw_1[1]))
    rest_o = flip_e(run.hold(rest_o), 1)
    gw_2 = experts_weights(here, rows_t, cots, run.hold(gb), ga_t, batch, devices)
    run.end(by_y, by_z, z_0, x_1, rest_o, gw_2)

    near_h = flip_e(jnp.concatenate([sum_h[2], add(run.hold(sum_h[3]), by_z)]), 2)
    other_h = flip(jnp.concatenate([add(run.hold(sum_h[0]), by_y), sum_h[1]]), "ctx", 1)
    z_1 = flip(run.hold(x_1[1]), "ctx", 2)
    x_2 = dp_reduce_pair(run.hold(gw_2[0]))
    sum_o = [add(sum_o[a * rows : (a + 1) * rows], rest_o[a * rows : (a + 1) * rows]) for a in range(4)]
    run.end(near_h, other_h, z_1, x_2, sum_o)

    grad_middle, grad_mix, branch, grad_gain_m = join_back(
        scalars, [all_h, rest_h, *run.hold([near_h, other_h])], middle, cot, gain_m, w_out_all
    )
    grad_mixes = [grad_mix[0]] + [shift(grad_mix[k], "ctx", -k) for k in range(1, nz)]
    x_3 = dp_reduce_pair(run.hold(gw_2[1]))
    far_o1 = flip_e(run.hold(sum_o[3]), 2)
    wo_a, wo_b = join_weights(scalars, here, branch, mixes, nd, ne)
    ready = lax.optimization_barrier((x_0[0], x_1[0], branch))
    swap = jnp.stack([add(ready[0][1], z_0[1]), add(ready[1][1], z_1[1])])
    other_o = add(sum_o[1], far_o1)
    run.end(grad_mixes, x_3, other_o, wo_b, swap)

    z_2 = flip(run.hold(x_2[1]), "ctx", 2)
    far_o = flip_e(run.hold(sum_o[2]), 2)
    other_o = flip(run.hold(other_o), "ctx", 1)
    wo_b = flip_e(run.hold(wo_b), 1)
    dqkv = attend_back(scalars, pieces, run.hold(grad_mixes), lse, cos, sin, heads, kvs)
    grad_normed = finish(scalars, dqkv, w_qkv, nz)
    wo_far = add(lax.optimization_barrier((wo_a, grad_normed[3]))[0][1], wo_b[1])
    run.end(z_2, far_o, other_o, wo_far, grad_normed)

    z_3 = flip(run.hold(x_3[1]), "ctx", 2)
    gw_a, gw_b = finish_weights(scalars, here, dqkv, run.hold(grad_normed), toks, gain_a, grad_gain_m, nd, ne)
    swap = flip(run.hold(swap), "ctx", 1)
    swap_2 = flip(add(run.hold(x_2[0])[1], z_2[1]), "ctx", 1)
    wo_far = flip_e(run.hold(wo_far), 2)
    run.end(gw_b, swap, swap_2, wo_far, z_3)

    tail = run.hold(grad_normed)
    total = shift(tail[0], "ctx", 1)
    gw_b = flip_e(run.hold(gw_b), 1)
    gw = add(gw_a, gw_b)
    wo_b, wo_far = run.hold([wo_b, wo_far])
    wo = (wo_a[0].astype(F32) + wo_b[0].astype(F32) + wo_far.astype(F32)).astype(BF)
    run.end(total, gw, wo)

    total = shift(add(run.hold(total), tail[1]), "ctx", 1)
    gw_far = flip_e(run.hold(gw[1]), 2)
    wo = dp_reduce(list(run.hold(wo)))
    gw = add(gw[0], gw_far)
    run.end(total, gw, wo)

    total = shift(add(run.hold(total), tail[2]), "ctx", 1)
    gw = dp_reduce(list(run.hold(gw)))
    run.end(total, gw)

    swap_3 = flip(add(run.hold(x_3[0])[1], z_3[1]), "ctx", 1)
    mine = jnp.concatenate(run.hold([gw, wo]), axis=2)
    parts = [pick(mine, z)] + [shift(pick(mine, mod(z + k, nz)), "ctx", k) for k in range(1, nz)]

    gn = tail[3].astype(F32) + total.astype(F32)
    expert_sum = sum_o[0].astype(F32) + far_o.astype(F32) + other_o.astype(F32)
    mixed_out = (middle + residual_scale * expert_sum).astype(BF)
    q_end, k_end, v_end = qw, qw + kw, qw + 2 * kw
    gains = sum(p[:, v_end : v_end + 2].astype(F32) for p in parts)
    grad_out = sum(p[:, v_end + 128 :].astype(F32) for p in parts)
    order = jnp.stack([p[:, :v_end] for p in parts])
    order = [pick(order, mod(z - p, nz)).astype(F32) for p in range(nz)]
    grad_query = jnp.concatenate([g[:, :q_end] for g in order], axis=1)
    grad_key = jnp.concatenate([g[:, q_end:k_end] for g in order], axis=1)
    grad_value = jnp.concatenate([g[:, k_end:] for g in order], axis=1)

    grads_in, grads_down = whole(
        [
            (x_0[0], z_0, swap[0]), (x_1[0], z_1, swap[1]), (x_2[0], z_2, swap_2), (x_3[0], z_3, swap_3)
        ],
        odd,
        devices,
    )

    t = tok.astype(F32)
    inv = rms(t)
    normal = t * inv
    u = gn * gain_a
    grad_tokens = grad_middle + inv * (u - normal * jnp.mean(u * normal, axis=-1, keepdims=True))
    return (
        mixed_out[None],
        grad_tokens[None],
        gains[:, 0],
        grad_query,
        grad_key,
        grad_value,
        grad_out.astype(F32),
        gains[:, 1],
        grads_in,
        grads_down,
    )


def solution(mesh):
    every = ("dp", "ctx", "exp")
    return jax.shard_map(
        per_device,
        mesh=mesh,
        in_specs=(
            P(("dp", "exp"), "ctx", None),
            P(),
            P(every, None),
            P(every, None),
            P(every, None),
            P(every, None),
            P(),
            P("exp", ("dp", "ctx"), None),
            P("exp", ("dp", "ctx"), None),
            P(("dp", "exp"), "ctx", None),
            P(("dp", "exp"), "ctx", None),
            P(("dp", "exp"), None),
            P(("dp", "exp"), "ctx", None),
        ),
        out_specs=(
            P(("dp", "exp"), "ctx", None),
            P(("dp", "exp"), "ctx", None),
            P(every),
            P(every, None),
            P(every, None),
            P(every, None),
            P(every, None),
            P(every),
            P("exp", ("dp", "ctx"), None),
            P("exp", ("dp", "ctx"), None),
        ),
        check_vma=False,
    )
```
